256 devices in a mesh: queue: 32 (over y, x, core), tok: 8 (over z).
Axes of the slice: x: 4, y: 4, z: 8, core: 2. Of those that a mesh axis runs over, the one named last changes fastest.
Arguments:
- queue_tokens: bfloat16 [64, 512, 1152], P('queue', 'tok'), may hold values from -6 to 6
- fresh_frame: bfloat16 [512, 1152], P('tok'), may hold values from -6 to 6
- levels: int32 [64], P('queue'), may hold values from 0 to 63
- mod_table: float32 [64, 6912], replicated, may hold values from -3 to 3
- w_qkv_spatial: bfloat16 [3, 1152, 1152], P(None, None, 'tok'), may hold values from -1 to 1
- w_out_spatial: bfloat16 [1152, 1152], P('tok'), may hold values from -0.1875 to 0.1875
- w_qkv_temporal: bfloat16 [3, 1152, 1152], P(None, None, 'tok'), may hold values from -1 to 1
- w_out_temporal: bfloat16 [1152, 1152], P('tok'), may hold values from -0.1875 to 0.1875
Outputs:
- next_queue: bfloat16 [64, 512, 1152], P('queue', 'tok')
The draws below stay inside these ranges and needn't reach their ends.
All inputs are finite; a program needn't handle non-finite values.
Results may differ from the reference program's by a relative error of at most 0.013.
Values may be sent and summed in bfloat16 or wider, within the bound.
No kernel may reach another device: no remote copies, remote signals or barrier semaphores. Data moves between devices by JAX's collectives and lax.ppermute only.
A program may use at most 128 MiB of HBM per device.

```python
import math
import jax
import jax.numpy as jnp
from jax import lax

D = 1152
HEADS = 16
HDIM = 72
LEVELS = 64
FRAMES = 64
FRAME_TOKENS = 512


def projection_weights(key, spread_top):
    keys = jax.random.split(key, 2)
    base = jax.random.truncated_normal(keys[0], -4.0, 4.0, (3, D, D), jnp.float32) * D ** (-0.5)
    head_scale = jnp.exp(jax.random.uniform(keys[1], (HEADS,), jnp.float32, 0.0, math.log(spread_top)))
    column = jnp.repeat(head_scale, HDIM)[None, :]
    query = base[0] * column
    keyed = base[1] * column
    return jnp.clip(jnp.stack([query, keyed, base[2]]), -1.0, 1.0)


def draw_w_qkv_spatial(key, part):
    key = jax.random.fold_in(key, 11)
    return projection_weights(key, 1.0).astype(jnp.bfloat16)


def draw_w_qkv_temporal(key, part):
    key = jax.random.fold_in(key, 23)
    return projection_weights(key, 1.0).astype(jnp.bfloat16)


def touch_ends(drawn, stream_key, low, top_value):
    longest = drawn.shape.index(max(drawn.shape))
    spots = []
    for shift in (0, 1):
        where = [jax.random.randint(jax.random.fold_in(stream_key, axis), (), 0, length) for axis, length in enumerate(drawn.shape)]
        where[longest] = (where[longest] + shift) % drawn.shape[longest]
        spots.append(tuple(where))
    return drawn.at[spots[0]].set(low).at[spots[1]].set(top_value)


def block_scale(own_key, dims, pieces, low, top_value):
    def one(position, blocks):
        draws = jax.random.uniform(jax.random.fold_in(jax.random.fold_in(own_key, 6), position), (blocks,), jnp.float32, low / len(pieces), top_value / len(pieces))
        return jnp.repeat(jnp.exp(draws), dims[position] // blocks).reshape((-1,) + (1,) * (len(dims) - position - 1))

    loudness = one(*pieces[0])
    for cut in pieces[1:]:
        loudness = loudness * one(*cut)
    return loudness


def bell_draw(own_key, shape, spread, reach, shards=(), held_as=jnp.bfloat16):
    gain = block_scale(own_key, shape, shards, -0.22, 0.18) if shards else 1.0
    result = jax.random.normal(own_key, shape, jnp.float32) * spread * gain
    return jnp.minimum(jnp.maximum(result, -reach), reach).astype(held_as)


def setup_inputs(seed: int = 0) -> dict:
    arg_keys = jax.random.split(jax.random.key(seed), 9)
    queue_tokens = bell_draw(arg_keys[0], (FRAMES, FRAME_TOKENS, D), 1.0, 6.0, ((0, 32), (1, 8)))
    fresh_frame = bell_draw(arg_keys[1], (FRAME_TOKENS, D), 1.0, 6.0, ((0, 8),))
    levels = touch_ends(jax.random.randint(arg_keys[2], (FRAMES,), 0, LEVELS), jax.random.fold_in(arg_keys[2], 1), 0, LEVELS - 1).astype(jnp.int32)
    mod_table = bell_draw(arg_keys[3], (LEVELS, 6 * D), 0.5, 3.0, (), jnp.float32)
    w_qkv_spatial = draw_w_qkv_spatial(jax.random.fold_in(arg_keys[8], 71), 0)
    w_out_spatial = bell_draw(arg_keys[5], (D, D), D ** -0.5, 0.1875, ((0, 8),))
    w_qkv_temporal = draw_w_qkv_temporal(jax.random.fold_in(arg_keys[8], 71), 0)
    w_out_temporal = bell_draw(arg_keys[7], (D, D), D ** -0.5, 0.1875, ((0, 8),))
    return {"queue_tokens": queue_tokens, "fresh_frame": fresh_frame, "levels": levels, "mod_table": mod_table, "w_qkv_spatial": w_qkv_spatial, "w_out_spatial": w_out_spatial, "w_qkv_temporal": w_qkv_temporal, "w_out_temporal": w_out_temporal}


EPS = 1e-06

def normalize(values):
    mean = lax.optimization_barrier(jnp.mean(values, axis=-1, keepdims=True))
    centered = values - mean
    variance = lax.optimization_barrier(jnp.mean(centered * centered, axis=-1, keepdims=True))
    return centered * lax.rsqrt(variance + EPS)

def project_three(hidden, weights):
    flat = hidden.reshape(FRAMES * FRAME_TOKENS, D)
    parts = [jnp.dot(flat, weights[index], preferred_element_type=jnp.float32).astype(jnp.bfloat16) for index in range(3)]
    return [part.reshape(FRAMES, FRAME_TOKENS, HEADS, HDIM) for part in parts]

def spatial_frame(operands):
    query, keyed, valued = operands
    scores = jnp.einsum('shd,thd->hst', query.astype(jnp.float32), keyed.astype(jnp.float32)) * HDIM ** (-0.5)
    weights = jax.nn.softmax(scores, axis=-1).astype(jnp.bfloat16)
    return jnp.einsum('hst,thd->shd', weights.astype(jnp.float32), valued.astype(jnp.float32)).astype(jnp.bfloat16)

def temporal_head(operands):
    query, keyed, valued = operands
    scores = jnp.einsum('fsd,gsd->sfg', query.astype(jnp.float32), keyed.astype(jnp.float32)) * HDIM ** (-0.5)
    weights = jax.nn.softmax(scores, axis=-1)
    mixed = jnp.einsum('sfg,gsd->fsd', weights, valued.astype(jnp.float32), precision=lax.Precision.HIGHEST)
    return mixed.astype(jnp.bfloat16)

def reference(queue_tokens, fresh_frame, levels, mod_table, w_qkv_spatial, w_out_spatial, w_qkv_temporal, w_out_temporal):
    mods = mod_table[levels].reshape(FRAMES, 6, D)
    resid = queue_tokens.astype(jnp.float32)
    hidden = (normalize(resid) * (1.0 + mods[:, 1, None, :]) + mods[:, 0, None, :]).astype(jnp.bfloat16)
    query, keyed, valued = project_three(hidden, w_qkv_spatial)
    attended = lax.map(spatial_frame, (query, keyed, valued))
    branch = jnp.dot(attended.reshape(FRAMES * FRAME_TOKENS, D), w_out_spatial, preferred_element_type=jnp.float32)
    resid = resid + mods[:, 2, None, :] * branch.reshape(FRAMES, FRAME_TOKENS, D)
    hidden = (normalize(resid) * (1.0 + mods[:, 4, None, :]) + mods[:, 3, None, :]).astype(jnp.bfloat16)
    query, keyed, valued = project_three(hidden, w_qkv_temporal)
    by_head = [jnp.transpose(item, (2, 0, 1, 3)) for item in (query, keyed, valued)]
    mixed = lax.map(temporal_head, tuple(by_head))
    mixed = jnp.transpose(mixed, (1, 2, 0, 3)).reshape(FRAMES * FRAME_TOKENS, D)
    branch = jnp.dot(mixed, w_out_temporal, preferred_element_type=jnp.float32)
    output = (resid + mods[:, 5, None, :] * branch.reshape(FRAMES, FRAME_TOKENS, D)).astype(jnp.bfloat16)
    return jnp.concatenate([output[1:], fresh_frame[None]], axis=0)
```

```python
import jax
import jax.numpy as jnp
from jax import lax
from jax.experimental import pallas as pl
from jax.experimental.pallas import tpu as pltpu
from jax.sharding import PartitionSpec as P

HEADS = 16
HDIM = 72
EPS = 1e-06
FACTOR = HDIM ** (-0.5)
BF16 = jnp.bfloat16
F32 = jnp.float32
VMEM = pltpu.VMEM


def params(mib):
    return pltpu.CompilerParams(vmem_limit_bytes=mib * 1024 * 1024)


def vspec():
    return pl.BlockSpec(memory_space=VMEM)


def normalize(values):
    mean = jnp.mean(values, axis=-1, keepdims=True)
    centered = values - mean
    variance = jnp.mean(centered * centered, axis=-1, keepdims=True)
    return centered * lax.rsqrt(variance + EPS)


def first_kernel(levels_ref, table_ref, tokens_ref, mods_ref, h0_ref, h1_ref):
    width = tokens_ref.shape[2]
    for j, out in enumerate((h0_ref, h1_ref)):
        row = table_ref[pl.ds(levels_ref[j], 1), :]
        mods_ref[j : j + 1, :] = row
        values = normalize(tokens_ref[j].astype(F32))
        out[...] = (values * (1.0 + row[:, width : 2 * width]) + row[:, :width]).astype(BF16)


def first(levels, table, tokens):
    _, rows, width = tokens.shape
    block = jax.ShapeDtypeStruct((rows, width), BF16)
    return pl.pallas_call(
        first_kernel,
        out_shape=(jax.ShapeDtypeStruct((2, table.shape[1]), F32), block, block),
        in_specs=[pl.BlockSpec(memory_space=pltpu.SMEM), vspec(), vspec()],
        out_specs=(vspec(), vspec(), vspec()),
        compiler_params=params(32),
        cost_estimate=pl.CostEstimate(flops=4000000, bytes_accessed=3000000, transcendentals=0),
        name="first",
    )(levels, table, tokens)


def columns_kernel(place_ref, *refs):
    blocks, out_ref = refs[:-1], refs[-1]
    count = len(blocks)
    side = blocks[0].shape[1]
    mine = place_ref[0]
    for turn in range(count):

        @pl.when(mine == turn)
        def _():
            for offset in range(count):
                z = (turn + offset) % count
                out_ref[:, z * side : (z + 1) * side] = blocks[offset][...]


def columns(place, blocks):
    rows, side = blocks[0].shape
    return pl.pallas_call(
        columns_kernel,
        out_shape=jax.ShapeDtypeStruct((rows, side * len(blocks)), BF16),
        in_specs=[pl.BlockSpec(memory_space=pltpu.SMEM)] + [vspec()] * len(blocks),
        out_specs=vspec(),
        compiler_params=params(16),
        cost_estimate=pl.CostEstimate(flops=0, bytes_accessed=700000, transcendentals=0),
        name="columns",
    )(place, *blocks)


def spatial_kernel(wq_ref, wo_ref, *refs):
    blocks, outs = refs[: len(refs) // 2], refs[len(refs) // 2 :]
    hidden = jnp.concatenate([ref[...] for ref in blocks], axis=0)
    query, keyed, valued = [
        jnp.dot(hidden, wq_ref[m], preferred_element_type=F32).astype(BF16) for m in range(3)
    ]
    heads = []
    for h in range(query.shape[1] // HDIM):
        cut = slice(h * HDIM, (h + 1) * HDIM)
        scores = FACTOR * lax.dot_general(
            query[:, cut], keyed[:, cut], (((1,), (1,)), ((), ())), preferred_element_type=F32
        )
        weights = jnp.exp(scores - jnp.max(scores, axis=-1, keepdims=True))
        total = jnp.sum(weights, axis=-1, keepdims=True)
        mixed = jnp.dot(weights.astype(BF16), valued[:, cut], preferred_element_type=F32)
        heads.append((mixed / total).astype(BF16))
    attended = jnp.concatenate(heads, axis=1)
    start = 0
    for ref, out in zip(blocks, outs):
        rows = ref.shape[0]
        piece = attended[start : start + rows]
        out[...] = jnp.dot(piece, wo_ref[...], preferred_element_type=F32).astype(BF16)
        start += rows


def spatial(w_qkv, w_out, blocks):
    rows = sum(b.shape[0] for b in blocks)
    width = blocks[0].shape[1]
    return pl.pallas_call(
        spatial_kernel,
        out_shape=[jax.ShapeDtypeStruct(b.shape, BF16) for b in blocks],
        in_specs=[vspec()] * (2 + len(blocks)),
        out_specs=[vspec()] * len(blocks),
        compiler_params=params(48),
        cost_estimate=pl.CostEstimate(
            flops=2 * rows * width * 144 * 4 + 4 * rows * rows * 256,
            bytes_accessed=5000000,
            transcendentals=2 * rows * rows,
        ),
        name="spatial",
    )(w_qkv, w_out, *blocks)


def middle_kernel(tokens_ref, mods_ref, *refs):
    parts, (x1_ref, h2_ref, pack_ref) = refs[:-3], refs[-3:]
    rows, width = x1_ref.shape[1:]
    for j in range(2):
        own, one, two = [parts[3 * j + k][...].astype(F32) for k in range(3)]
        branch = own + one + two

        def row(n):
            return mods_ref[j : j + 1, n * width : (n + 1) * width]

        x1 = tokens_ref[j].astype(F32) + row(2) * branch
        x1_ref[j] = x1
        h2_ref[j] = (normalize(x1) * (1.0 + row(4)) + row(3)).astype(BF16)
        if j == 0:
            pack_ref[:rows] = x1
            pack_ref[rows:] = jnp.broadcast_to(row(5), (8, width))


def middle(tokens, mods, parts):
    _, rows, width = tokens.shape
    return pl.pallas_call(
        middle_kernel,
        out_shape=(
            jax.ShapeDtypeStruct(tokens.shape, F32),
            jax.ShapeDtypeStruct(tokens.shape, BF16),
            jax.ShapeDtypeStruct((rows + 8, width), F32),
        ),
        in_specs=[vspec()] * (2 + len(parts)),
        out_specs=(vspec(), vspec(), vspec()),
        compiler_params=params(32),
        cost_estimate=pl.CostEstimate(flops=4000000, bytes_accessed=3000000, transcendentals=0),
        name="middle",
    )(tokens, mods, *parts)


def temporal_kernel(hidden_ref, weights_ref, out_ref, held, sems):
    pieces, _, depth, width = weights_ref.shape

    def copy(m, r):
        return pltpu.make_async_copy(weights_ref.at[r, m], held.at[m, r], sems.at[m, r])

    for m in range(4):
        for r in range(pieces):
            copy(m, r).start()
    hidden = hidden_ref[...]
    rows = hidden.shape[0]

    def matrix(m):
        for r in range(pieces):
            copy(m, r).wait()
        return held[m].reshape(pieces * depth, width)

    query, keyed, valued = [
        jnp.dot(hidden, matrix(m), preferred_element_type=F32).astype(BF16) for m in range(3)
    ]
    along = lax.broadcasted_iota(jnp.int32, (rows, rows), 0) % 2
    across = lax.broadcasted_iota(jnp.int32, (rows, rows), 1) % 2
    same = along == across
    heads = []
    for h in range(width // HDIM):
        cut = slice(h * HDIM, (h + 1) * HDIM)
        scores = FACTOR * lax.dot_general(
            query[:, cut], keyed[:, cut], (((1,), (1,)), ((), ())), preferred_element_type=F32
        )
        scores = jnp.where(same, scores, -jnp.inf)
        weights = jnp.exp(scores - jnp.max(scores, axis=-1, keepdims=True))
        total = jnp.sum(weights, axis=-1, keepdims=True)
        mixed = jnp.dot(weights.astype(BF16), valued[:, cut], preferred_element_type=F32)
        heads.append((mixed / total).astype(BF16))
    attended = jnp.concatenate(heads, axis=1)
    out_ref[...] = lax.dot_general(
        attended, matrix(3), (((1,), (1,)), ((), ())), preferred_element_type=F32
    ).astype(BF16)


def temporal(hidden, weights):
    pieces, _, depth, width = weights.shape
    rows = hidden.shape[0]
    return pl.pallas_call(
        temporal_kernel,
        out_shape=jax.ShapeDtypeStruct((rows, width), BF16),
        in_specs=[vspec(), pl.BlockSpec(memory_space=pl.ANY)],
        out_specs=vspec(),
        scratch_shapes=[
            VMEM((4, pieces, depth, width), BF16),
            pltpu.SemaphoreType.DMA((4, pieces)),
        ],
        compiler_params=params(48),
        cost_estimate=pl.CostEstimate(
            flops=2 * rows * width * width * 4, bytes_accessed=12000000, transcendentals=16 * rows * rows
        ),
        name="temporal",
    )(hidden, weights)


def last_kernel(tail_ref, x1_ref, mods_ref, pack_ref, branch_ref, fresh_ref, out_ref):
    rows, width = x1_ref.shape[1:]
    gate = mods_ref[1:2, 5 * width :]
    out_ref[0] = (x1_ref[1] + gate * branch_ref[0].astype(F32)).astype(BF16)
    moved = (pack_ref[:rows] + pack_ref[rows : rows + 1] * branch_ref[1].astype(F32)).astype(BF16)

    @pl.when(tail_ref[0] == 0)
    def _():
        out_ref[1] = moved

    @pl.when(tail_ref[0] != 0)
    def _():
        out_ref[1] = fresh_ref[...]


def last(at_tail, x1, mods, pack, branch, fresh):
    return pl.pallas_call(
        last_kernel,
        out_shape=jax.ShapeDtypeStruct(x1.shape, BF16),
        in_specs=[pl.BlockSpec(memory_space=pltpu.SMEM)] + [vspec()] * 5,
        out_specs=vspec(),
        compiler_params=params(32),
        cost_estimate=pl.CostEstimate(flops=1000000, bytes_accessed=2000000, transcendentals=0),
        name="last",
    )(at_tail, x1, mods, pack, branch, fresh)


def per_device(
    queue_tokens,
    fresh_frame,
    levels,
    mod_table,
    w_qkv_spatial,
    w_out_spatial,
    w_qkv_temporal,
    w_out_temporal,
):
    _, rows, width = queue_tokens.shape
    ring = lax.axis_size("tok")
    line = lax.axis_size("queue")
    here = lax.axis_index("tok")
    spot = lax.axis_index("queue")
    up = [(i, (i + 1) % ring) for i in range(ring)]
    down = [(i, (i - 1) % ring) for i in range(ring)]
    half = rows // 2

    def send_up(v):
        return lax.ppermute(v, "tok", up)

    def send_down(v):
        return lax.ppermute(v, "tok", down)

    side = w_qkv_temporal.shape[2]
    strip, which = spot // 4, spot % 4
    from_qkv = lax.dynamic_slice(
        w_qkv_temporal, (jnp.minimum(which, 2), strip * side, 0), (1, side, side)
    )[0]
    from_out = lax.dynamic_slice(w_out_temporal, (0, strip * side), (side, side)).T
    chunk = jnp.where(which == 3, from_out, from_qkv)
    held = {0: chunk}
    below = above = chunk
    for step in range(1, 4):
        below, above = send_up(below), send_down(above)
        held[-step], held[step] = below, above
    held[4] = send_up(below)
    chunk = columns(here.astype(jnp.int32)[None], [held[(o + 3) % 8 - 3] for o in range(8)])
    weights = lax.all_gather(chunk, "queue", axis=0, tiled=False)
    weights = weights.reshape(line // 4, 4, side, width)

    mods, *hidden = first(levels, mod_table, queue_tokens)
    frames = [{0: h} for h in hidden]
    low = list(hidden)
    high = list(hidden)
    for step in range(1, 4):
        for j in range(2):
            low[j], high[j] = send_up(low[j]), send_down(high[j])
            frames[j][-step], frames[j][step] = low[j], high[j]
    for j in range(2):
        frames[j]["a"] = send_up(low[j][:half])
        frames[j]["b"] = send_down(high[j][half:])

    order = [0, 1, -1, 2, -2, 3, -3, "a", "b"]
    parts = []
    for j in range(2):
        done = dict(zip(order, spatial(w_qkv_spatial, w_out_spatial, [frames[j][k] for k in order])))

        def add(value, other):
            return (value.astype(F32) + other.astype(F32)).astype(BF16)

        rise, fall = send_up(done["a"]), send_down(done["b"])
        rise = jnp.concatenate([add(done[3][:half], rise), done[3][half:]])
        fall = jnp.concatenate([done[-3][:half], add(done[-3][half:], fall)])
        for o in (2, 1):
            rise, fall = add(done[o], send_up(rise)), add(done[-o], send_down(fall))
        parts += [done[0], send_up(rise), send_down(fall)]

    x1, h2, pack = middle(queue_tokens, mods, parts)
    pack = lax.ppermute(pack, "queue", [(i, i - 1) for i in range(1, line)])
    per = rows // line
    sent = jnp.transpose(h2.reshape(2, line, per, width), (1, 0, 2, 3)).reshape(line, 2 * per, width)
    got = lax.all_to_all(sent, "queue", 0, 0, tiled=True)
    branch = temporal(got.reshape(line * 2 * per, width), weights)
    branch = jnp.concatenate([branch[per:], branch[:per]])
    got = lax.all_to_all(branch.reshape(line, 2 * per, width), "queue", 0, 0, tiled=True)
    branch = jnp.transpose(got.reshape(line, 2, per, width), (1, 0, 2, 3)).reshape(2, rows, width)
    at_tail = (spot == line - 1).astype(jnp.int32)[None]
    return last(at_tail, x1, mods, pack, branch, fresh_frame)


def solution(mesh):
    return jax.shard_map(
        per_device,
        mesh=mesh,
        in_specs=(
            P("queue", "tok", None),
            P("tok", None),
            P("queue"),
            P(),
            P(None, None, "tok"),
            P("tok", None),
            P(None, None, "tok"),
            P("tok", None),
        ),
        out_specs=P("queue", "tok", None),
        check_vma=False,
    )
```

```python
import jax
import jax.numpy as jnp
from jax import lax
from jax.experimental import pallas as pl
from jax.experimental.pallas import tpu as pltpu
from jax.sharding import PartitionSpec as P

HEADS = 16
HDIM = 72
EPS = 1e-06
FACTOR = HDIM ** (-0.5)
BF16 = jnp.bfloat16
F32 = jnp.float32
VMEM = pltpu.VMEM


def params(mib):
    return pltpu.CompilerParams(vmem_limit_bytes=mib * 1024 * 1024)


def vspec():
    return pl.BlockSpec(memory_space=VMEM)


def normalize(values):
    mean = jnp.mean(values, axis=-1, keepdims=True)
    centered = values - mean
    variance = jnp.mean(centered * centered, axis=-1, keepdims=True)
    return centered * lax.rsqrt(variance + EPS)


def turned(values, matrix):
    return lax.dot_general(values, matrix, (((1,), (1,)), ((), ())), preferred_element_type=F32)


def first_kernel(levels_ref, table_ref, tokens_ref, chunk_ref, mods_ref, h0_ref, h1_ref):
    rows, width = tokens_ref.shape[1:]
    for j, out in enumerate((h0_ref, h1_ref)):
        row = table_ref[pl.ds(levels_ref[j], 1), :]
        mods_ref[j : j + 1, :] = row
        values = normalize(tokens_ref[j].astype(F32))
        out[:rows] = (values * (1.0 + row[:, width : 2 * width]) + row[:, :width]).astype(BF16)
    h0_ref[rows:] = chunk_ref[...]


def first(levels, table, tokens, chunk):
    _, rows, width = tokens.shape
    return pl.pallas_call(
        first_kernel,
        out_shape=(
            jax.ShapeDtypeStruct((2, table.shape[1]), F32),
            jax.ShapeDtypeStruct((rows + chunk.shape[0], width), BF16),
            jax.ShapeDtypeStruct((rows, width), BF16),
        ),
        in_specs=[pl.BlockSpec(memory_space=pltpu.SMEM), vspec(), vspec(), vspec()],
        out_specs=(vspec(), vspec(), vspec()),
        compiler_params=params(8),
        cost_estimate=pl.CostEstimate(flops=4000000, bytes_accessed=3000000, transcendentals=0),
        name="first",
    )(levels, table, tokens, chunk)


def stack_kernel(size, *refs):
    pieces = [ref[ref.shape[0] - size :].astype(F32) for ref in refs[:-1]]
    refs[-1][...] = jnp.concatenate(pieces, axis=0).astype(BF16)


def stack(size, blocks):
    return pl.pallas_call(
        lambda *refs: stack_kernel(size, *refs),
        out_shape=jax.ShapeDtypeStruct((size * len(blocks), blocks[0].shape[1]), BF16),
        in_specs=[vspec()] * len(blocks),
        out_specs=vspec(),
        compiler_params=params(8),
        cost_estimate=pl.CostEstimate(flops=0, bytes_accessed=700000, transcendentals=0),
        name="stack",
    )(*blocks)


def spatial_kernel(sizes, wq_ref, wo_ref, *refs):
    blocks, outs = refs[: len(sizes)], refs[len(sizes) :]
    hidden = jnp.concatenate([ref[:size] for ref, size in zip(blocks, sizes)], axis=0)
    query, keyed, valued = [turned(hidden, wq_ref[m]).astype(BF16) for m in range(3)]
    heads = []
    for h in range(query.shape[1] // HDIM):
        cut = slice(h * HDIM, (h + 1) * HDIM)
        scores = FACTOR * turned(query[:, cut], keyed[:, cut])
        weights = jnp.exp(scores - jnp.max(scores, axis=-1, keepdims=True))
        total = jnp.sum(weights, axis=-1, keepdims=True)
        mixed = jnp.dot(weights.astype(BF16), valued[:, cut], preferred_element_type=F32)
        heads.append((mixed / total).astype(BF16))
    attended = jnp.concatenate(heads, axis=1)
    start = 0
    for size, out in zip(sizes, outs):
        piece = attended[start : start + size]
        out[...] = jnp.dot(piece, wo_ref[...], preferred_element_type=F32).astype(BF16)
        start += size


def spatial(sizes, w_qkv, w_out, blocks):
    rows = sum(sizes)
    width = blocks[0].shape[1]
    return pl.pallas_call(
        lambda *refs: spatial_kernel(sizes, *refs),
        out_shape=[jax.ShapeDtypeStruct((size, width), BF16) for size in sizes],
        in_specs=[vspec()] * (2 + len(blocks)),
        out_specs=[vspec()] * len(blocks),
        compiler_params=params(16),
        cost_estimate=pl.CostEstimate(
            flops=2 * rows * width * 144 * 4 + 4 * rows * rows * 256,
            bytes_accessed=5000000,
            transcendentals=2 * rows * rows,
        ),
        name="spatial",
    )(w_qkv, w_out, *blocks)


def middle_kernel(tokens_ref, mods_ref, *refs):
    parts, (x1_ref, h2_ref, pack_ref) = refs[:-3], refs[-3:]
    rows, width = x1_ref.shape[1:]
    for j in range(2):
        own, one, two = [parts[3 * j + k][...].astype(F32) for k in range(3)]
        branch = own + one + two

        def row(n):
            return mods_ref[j : j + 1, n * width : (n + 1) * width]

        x1 = tokens_ref[j].astype(F32) + row(2) * branch
        x1_ref[j] = x1
        h2_ref[j] = (normalize(x1) * (1.0 + row(4)) + row(3)).astype(BF16)
        if j == 0:
            pack_ref[:rows] = x1
            pack_ref[rows:] = jnp.broadcast_to(row(5), (8, width))


def middle(tokens, mods, parts):
    _, rows, width = tokens.shape
    return pl.pallas_call(
        middle_kernel,
        out_shape=(
            jax.ShapeDtypeStruct(tokens.shape, F32),
            jax.ShapeDtypeStruct(tokens.shape, BF16),
            jax.ShapeDtypeStruct((rows + 8, width), F32),
        ),
        in_specs=[vspec()] * (2 + len(parts)),
        out_specs=(vspec(), vspec(), vspec()),
        compiler_params=params(8),
        cost_estimate=pl.CostEstimate(flops=4000000, bytes_accessed=3000000, transcendentals=0),
        name="middle",
    )(tokens, mods, *parts)


def temporal_kernel(ring, size, per, hidden_ref, weights_ref, out_ref, held, sems):
    pieces, depth, width = weights_ref.shape
    some = pieces // 8

    def copy(n):
        part = pl.ds(n * some, some)
        return pltpu.make_async_copy(weights_ref.at[part], held.at[part], sems.at[n])

    for n in range(8):
        copy(n).start()
    hidden = hidden_ref[...]
    rows = hidden.shape[0]
    half = width // 2

    def matrix(m, s):
        n = 2 * m + s
        copy(n).wait()
        return held[n * some : (n + 1) * some].reshape(half, width)

    lane = lax.broadcasted_iota(jnp.int32, (1, half), 1)
    owned = []
    for z in range(ring):
        mask = jnp.zeros((1, half), jnp.bool_)
        for a in range(some):
            low = a * depth + z * size
            mask = mask | ((lane >= low) & (lane < low + size))
        owned.append(mask)
    along = lax.broadcasted_iota(jnp.int32, (ring * rows, rows), 0) % per
    across = lax.broadcasted_iota(jnp.int32, (ring * rows, rows), 1) % per
    same = along == across

    query = [turned(hidden, matrix(0, s)) for s in range(2)]
    keyed = [turned(hidden, matrix(1, s)).astype(BF16) for s in range(2)]
    valued = [turned(hidden, matrix(2, s)).astype(BF16) for s in range(2)]
    branch = jnp.zeros((rows, width), F32)
    for s in range(2):
        spread = jnp.concatenate([jnp.where(m, query[s], 0.0) for m in owned], axis=0).astype(BF16)
        scores = jnp.where(same, FACTOR * turned(spread, keyed[s]), -jnp.inf)
        weights = jnp.exp(scores - jnp.max(scores, axis=-1, keepdims=True))
        total = jnp.sum(weights, axis=-1, keepdims=True)
        mixed = jnp.dot(weights.astype(BF16), valued[s], preferred_element_type=F32) / total
        attended = jnp.zeros((rows, half), F32)
        for z, m in enumerate(owned):
            attended = jnp.where(m, mixed[z * rows : (z + 1) * rows], attended)
        branch += jnp.dot(attended.astype(BF16), matrix(3, s), preferred_element_type=F32)
    out_ref[...] = jnp.concatenate([branch[per:], branch[:per]], axis=0).astype(BF16)


def temporal(ring, per, hidden, weights):
    pieces, depth, width = weights.shape
    rows = hidden.shape[0]
    return pl.pallas_call(
        lambda *refs: temporal_kernel(ring, depth // ring, per, *refs),
        out_shape=jax.ShapeDtypeStruct((rows, width), BF16),
        in_specs=[vspec(), pl.BlockSpec(memory_space=pl.ANY)],
        out_specs=vspec(),
        scratch_shapes=[
            VMEM((pieces, depth, width), BF16),
            pltpu.SemaphoreType.DMA((8,)),
        ],
        compiler_params=params(36),
        cost_estimate=pl.CostEstimate(
            flops=2 * rows * width * width * 4, bytes_accessed=12000000, transcendentals=16 * rows * rows
        ),
        name="temporal",
    )(hidden, weights)


def last_kernel(tail_ref, x1_ref, mods_ref, pack_ref, branch_ref, fresh_ref, out_ref):
    rows, width = x1_ref.shape[1:]
    gate = mods_ref[1:2, 5 * width :]
    out_ref[0] = (x1_ref[1] + gate * branch_ref[0].astype(F32)).astype(BF16)
    moved = (pack_ref[:rows] + pack_ref[rows : rows + 1] * branch_ref[1].astype(F32)).astype(BF16)

    @pl.when(tail_ref[0] == 0)
    def _():
        out_ref[1] = moved

    @pl.when(tail_ref[0] != 0)
    def _():
        out_ref[1] = fresh_ref[...]


def last(at_tail, x1, mods, pack, branch, fresh):
    return pl.pallas_call(
        last_kernel,
        out_shape=jax.ShapeDtypeStruct(x1.shape, BF16),
        in_specs=[pl.BlockSpec(memory_space=pltpu.SMEM)] + [vspec()] * 5,
        out_specs=vspec(),
        compiler_params=params(8),
        cost_estimate=pl.CostEstimate(flops=1000000, bytes_accessed=2000000, transcendentals=0),
        name="last",
    )(at_tail, x1, mods, pack, branch, fresh)


def per_device(
    queue_tokens,
    fresh_frame,
    levels,
    mod_table,
    w_qkv_spatial,
    w_out_spatial,
    w_qkv_temporal,
    w_out_temporal,
):
    _, rows, width = queue_tokens.shape
    ring = lax.axis_size("tok")
    line = lax.axis_size("queue")
    spot = lax.axis_index("queue")
    up = [(i, (i + 1) % ring) for i in range(ring)]
    down = [(i, (i - 1) % ring) for i in range(ring)]
    half = rows // 2

    def send_up(v):
        return lax.ppermute(v, "tok", up)

    def send_down(v):
        return lax.ppermute(v, "tok", down)

    turned_qkv = jnp.swapaxes(w_qkv_temporal, 1, 2)
    side = w_out_temporal.shape[0]
    size = 4 * side // line
    start = spot * size
    chunk = jnp.where(
        start >= 3 * side,
        lax.dynamic_slice(w_out_temporal, (jnp.maximum(start - 3 * side, 0), 0), (size, width)),
        lax.dynamic_slice(
            turned_qkv.reshape(3 * side, width), (jnp.minimum(start, 3 * side - size), 0), (size, width)
        ),
    )

    mods, *hidden = first(levels, mod_table, queue_tokens, chunk)
    frames = [{0: h} for h in hidden]
    low = list(hidden)
    high = list(hidden)
    for step in range(1, 4):
        for j in range(2):
            low[j], high[j] = send_up(low[j]), send_down(high[j])
            frames[j][-step], frames[j][step] = low[j], high[j]
    for j in range(2):
        frames[j]["a"] = send_up(low[j][:half])
        frames[j]["b"] = send_down(high[j][half:])
    pieces = stack(size, [frames[0][o] for o in (0, 1, 2, 3, "b", -3, -2, -1)])
    weights = lax.all_gather(pieces, "queue", axis=0, tiled=False)

    order = [0, 1, -1, 2, -2, 3, -3, "a", "b"]
    sizes = [rows] * 7 + [half] * 2
    w_spatial = jnp.swapaxes(w_qkv_spatial, 1, 2)
    parts = []
    for j in range(2):
        done = dict(zip(order, spatial(sizes, w_spatial, w_out_spatial, [frames[j][k] for k in order])))

        def add(value, other):
            return (value.astype(F32) + other.astype(F32)).astype(BF16)

        rise, fall = send_up(done["a"]), send_down(done["b"])
        rise = jnp.concatenate([add(done[3][:half], rise), done[3][half:]])
        fall = jnp.concatenate([done[-3][:half], add(done[-3][half:], fall)])
        for o in (2, 1):
            rise, fall = add(done[o], send_up(rise)), add(done[-o], send_down(fall))
        parts += [done[0], send_up(rise), send_down(fall)]

    x1, h2, pack = middle(queue_tokens, mods, parts)
    pack = lax.ppermute(pack, "queue", [(i, i - 1) for i in range(1, line)])
    per = rows // line
    sent = jnp.transpose(h2.reshape(2, line, per, width), (1, 0, 2, 3)).reshape(line, 2 * per, width)
    got = lax.all_to_all(sent, "queue", 0, 0, tiled=True)
    branch = temporal(ring, per, got.reshape(line * 2 * per, width), weights)
    got = lax.all_to_all(branch.reshape(line, 2 * per, width), "queue", 0, 0, tiled=True)
    branch = jnp.transpose(got.reshape(line, 2, per, width), (1, 0, 2, 3)).reshape(2, rows, width)
    at_tail = (spot == line - 1).astype(jnp.int32)[None]
    return last(at_tail, x1, mods, pack, branch, fresh_frame)


def solution(mesh):
    return jax.shard_map(
        per_device,
        mesh=mesh,
        in_specs=(
            P("queue", "tok", None),
            P("tok", None),
            P("queue"),
            P(),
            P(None, None, "tok"),
            P("tok", None),
            P(None, None, "tok"),
            P("tok", None),
        ),
        out_specs=P("queue", "tok", None),
        check_vma=False,
    )
```

```python
import jax
import jax.numpy as jnp
from jax import lax
from jax.experimental import pallas as pl
from jax.experimental.pallas import tpu as pltpu
from jax.sharding import PartitionSpec as P

HEADS = 16
HDIM = 72
EPS = 1e-06
FACTOR = HDIM ** (-0.5)
BF16 = jnp.bfloat16
F32 = jnp.float32
VMEM = pltpu.VMEM


def params(mib):
    return pltpu.CompilerParams(vmem_limit_bytes=mib * 1024 * 1024)


def vspec():
    return pl.BlockSpec(memory_space=VMEM)


def normalize(values):
    mean = jnp.mean(values, axis=-1, keepdims=True)
    centered = values - mean
    variance = jnp.mean(centered * centered, axis=-1, keepdims=True)
    return centered * lax.rsqrt(variance + EPS)


def turned(values, matrix):
    return lax.dot_general(values, matrix, (((1,), (1,)), ((), ())), preferred_element_type=F32)


def first_kernel(levels_ref, table_ref, tokens_ref, chunk_ref, mods_ref, h0_ref, h1_ref):
    rows, width = tokens_ref.shape[1:]
    for j, out in enumerate((h0_ref, h1_ref)):
        row = table_ref[pl.ds(levels_ref[j], 1), :]
        mods_ref[j : j + 1, :] = row
        values = normalize(tokens_ref[j].astype(F32))
        out[:rows] = (values * (1.0 + row[:, width : 2 * width]) + row[:, :width]).astype(BF16)
    h0_ref[rows:] = chunk_ref[...]


def first(levels, table, tokens, chunk):
    _, rows, width = tokens.shape
    return pl.pallas_call(
        first_kernel,
        out_shape=(
            jax.ShapeDtypeStruct((2, table.shape[1]), F32),
            jax.ShapeDtypeStruct((rows + chunk.shape[0], width), BF16),
            jax.ShapeDtypeStruct((rows, width), BF16),
        ),
        in_specs=[pl.BlockSpec(memory_space=pltpu.SMEM), vspec(), vspec(), vspec()],
        out_specs=(vspec(), vspec(), vspec()),
        compiler_params=params(8),
        cost_estimate=pl.CostEstimate(flops=4000000, bytes_accessed=3000000, transcendentals=0),
        name="first",
    )(levels, table, tokens, chunk)


def stack_kernel(size, *refs):
    pieces = [ref[ref.shape[0] - size :].astype(F32) for ref in refs[:-1]]
    refs[-1][...] = jnp.concatenate(pieces, axis=0).astype(BF16)


def stack(size, blocks):
    return pl.pallas_call(
        lambda *refs: stack_kernel(size, *refs),
        out_shape=jax.ShapeDtypeStruct((size * len(blocks), blocks[0].shape[1]), BF16),
        in_specs=[vspec()] * len(blocks),
        out_specs=vspec(),
        compiler_params=params(8),
        cost_estimate=pl.CostEstimate(flops=0, bytes_accessed=700000, transcendentals=0),
        name="stack",
    )(*blocks)


def spatial_kernel(rows, wq_ref, wo_ref, *refs):
    blocks, outs = refs[: len(refs) // 2], refs[len(refs) // 2 :]
    hidden = jnp.concatenate([ref[:rows] for ref in blocks], axis=0)
    query, keyed, valued = [turned(hidden, wq_ref[m]).astype(BF16) for m in range(3)]
    heads = []
    for h in range(query.shape[1] // HDIM):
        cut = slice(h * HDIM, (h + 1) * HDIM)
        scores = FACTOR * turned(query[:, cut], keyed[:, cut])
        weights = jnp.exp(scores - jnp.max(scores, axis=-1, keepdims=True))
        total = jnp.sum(weights, axis=-1, keepdims=True)
        mixed = jnp.dot(weights.astype(BF16), valued[:, cut], preferred_element_type=F32)
        heads.append((mixed / total).astype(BF16))
    attended = jnp.concatenate(heads, axis=1)
    for n, out in enumerate(outs):
        piece = attended[n * rows : (n + 1) * rows]
        out[...] = jnp.dot(piece, wo_ref[...], preferred_element_type=F32).astype(BF16)


def spatial(rows, w_qkv, w_out, blocks):
    width = blocks[0].shape[1]
    whole = rows * len(blocks)
    return pl.pallas_call(
        lambda *refs: spatial_kernel(rows, *refs),
        out_shape=[jax.ShapeDtypeStruct((rows, width), BF16) for _ in blocks],
        in_specs=[vspec()] * (2 + len(blocks)),
        out_specs=[vspec()] * len(blocks),
        compiler_params=params(16),
        cost_estimate=pl.CostEstimate(
            flops=2 * whole * width * 144 * 4 + 4 * whole * whole * 256,
            bytes_accessed=5000000,
            transcendentals=2 * whole * whole,
        ),
        name="spatial",
    )(w_qkv, w_out, *blocks)


def middle_kernel(tokens_ref, mods_ref, *refs):
    parts, (x1_ref, h2_ref, pack_ref) = refs[:-3], refs[-3:]
    rows, width = x1_ref.shape[1:]
    for j in range(2):
        own, one, two = [parts[3 * j + k][...].astype(F32) for k in range(3)]
        branch = own + one + two

        def row(n):
            return mods_ref[j : j + 1, n * width : (n + 1) * width]

        x1 = tokens_ref[j].astype(F32) + row(2) * branch
        x1_ref[j] = x1
        h2_ref[j] = (normalize(x1) * (1.0 + row(4)) + row(3)).astype(BF16)
        if j == 0:
            pack_ref[:rows] = x1
            pack_ref[rows:] = jnp.broadcast_to(row(5), (8, width))


def middle(tokens, mods, parts):
    _, rows, width = tokens.shape
    return pl.pallas_call(
        middle_kernel,
        out_shape=(
            jax.ShapeDtypeStruct(tokens.shape, F32),
            jax.ShapeDtypeStruct(tokens.shape, BF16),
            jax.ShapeDtypeStruct((rows + 8, width), F32),
        ),
        in_specs=[vspec()] * (2 + len(parts)),
        out_specs=(vspec(), vspec(), vspec()),
        compiler_params=params(8),
        cost_estimate=pl.CostEstimate(flops=4000000, bytes_accessed=3000000, transcendentals=0),
        name="middle",
    )(tokens, mods, *parts)


def temporal_kernel(ring, size, per, hidden_ref, weights_ref, out_ref, held, sems):
    pieces, depth, width = weights_ref.shape
    some = pieces // 8

    def copy(n):
        part = pl.ds(n * some, some)
        return pltpu.make_async_copy(weights_ref.at[part], held.at[part], sems.at[n])

    for n in range(8):
        copy(n).start()
    hidden = hidden_ref[...]
    rows = hidden.shape[0]
    half = width // 2

    def matrix(m, s):
        n = 2 * m + s
        copy(n).wait()
        return held[n * some : (n + 1) * some].reshape(half, width)

    lane = lax.broadcasted_iota(jnp.int32, (1, half), 1)
    owned = []
    for z in range(ring):
        mask = jnp.zeros((1, half), jnp.bool_)
        for a in range(some):
            low = a * depth + z * size
            mask = mask | ((lane >= low) & (lane < low + size))
        owned.append(mask)
    along = lax.broadcasted_iota(jnp.int32, (ring * rows, rows), 0) % per
    across = lax.broadcasted_iota(jnp.int32, (ring * rows, rows), 1) % per
    same = along == across

    query = [turned(hidden, matrix(0, s)) for s in range(2)]
    keyed = [turned(hidden, matrix(1, s)).astype(BF16) for s in range(2)]
    valued = [turned(hidden, matrix(2, s)).astype(BF16) for s in range(2)]
    branch = jnp.zeros((rows, width), F32)
    for s in range(2):
        spread = jnp.concatenate([jnp.where(m, query[s], 0.0) for m in owned], axis=0).astype(BF16)
        scores = jnp.where(same, FACTOR * turned(spread, keyed[s]), -jnp.inf)
        weights = jnp.exp(scores - jnp.max(scores, axis=-1, keepdims=True))
        total = jnp.sum(weights, axis=-1, keepdims=True)
        mixed = jnp.dot(weights.astype(BF16), valued[s], preferred_element_type=F32) / total
        attended = jnp.zeros((rows, half), F32)
        for z, m in enumerate(owned):
            attended = jnp.where(m, mixed[z * rows : (z + 1) * rows], attended)
        branch += jnp.dot(attended.astype(BF16), matrix(3, s), preferred_element_type=F32)
    out_ref[...] = jnp.concatenate([branch[per:], branch[:per]], axis=0).astype(BF16)


def temporal(ring, per, hidden, weights):
    pieces, depth, width = weights.shape
    rows = hidden.shape[0]
    return pl.pallas_call(
        lambda *refs: temporal_kernel(ring, depth // ring, per, *refs),
        out_shape=jax.ShapeDtypeStruct((rows, width), BF16),
        in_specs=[vspec(), pl.BlockSpec(memory_space=pl.ANY)],
        out_specs=vspec(),
        scratch_shapes=[
            VMEM((pieces, depth, width), BF16),
            pltpu.SemaphoreType.DMA((8,)),
        ],
        compiler_params=params(50),
        cost_estimate=pl.CostEstimate(
            flops=2 * rows * width * width * 4, bytes_accessed=12000000, transcendentals=16 * rows * rows
        ),
        name="temporal",
    )(hidden, weights)


def last_kernel(tail_ref, x1_ref, mods_ref, pack_ref, branch_ref, fresh_ref, out_ref):
    rows, width = x1_ref.shape[1:]
    gate = mods_ref[1:2, 5 * width :]
    out_ref[0] = (x1_ref[1] + gate * branch_ref[0].astype(F32)).astype(BF16)
    moved = (pack_ref[:rows] + pack_ref[rows : rows + 1] * branch_ref[1].astype(F32)).astype(BF16)

    @pl.when(tail_ref[0] == 0)
    def _():
        out_ref[1] = moved

    @pl.when(tail_ref[0] != 0)
    def _():
        out_ref[1] = fresh_ref[...]


def last(at_tail, x1, mods, pack, branch, fresh):
    return pl.pallas_call(
        last_kernel,
        out_shape=jax.ShapeDtypeStruct(x1.shape, BF16),
        in_specs=[pl.BlockSpec(memory_space=pltpu.SMEM)] + [vspec()] * 5,
        out_specs=vspec(),
        compiler_params=params(8),
        cost_estimate=pl.CostEstimate(flops=1000000, bytes_accessed=2000000, transcendentals=0),
        name="last",
    )(at_tail, x1, mods, pack, branch, fresh)


def per_device(
    queue_tokens,
    fresh_frame,
    levels,
    mod_table,
    w_qkv_spatial,
    w_out_spatial,
    w_qkv_temporal,
    w_out_temporal,
):
    _, rows, width = queue_tokens.shape
    ring = lax.axis_size("tok")
    line = lax.axis_size("queue")
    spot = lax.axis_index("queue")
    up = [(i, (i + 1) % ring) for i in range(ring)]
    down = [(i, (i - 1) % ring) for i in range(ring)]

    def send_up(v):
        return lax.ppermute(v, "tok", up)

    def send_down(v):
        return lax.ppermute(v, "tok", down)

    turned_qkv = jnp.swapaxes(w_qkv_temporal, 1, 2)
    side = w_out_temporal.shape[0]
    size = 4 * side // line
    start = spot * size
    chunk = jnp.where(
        start >= 3 * side,
        lax.dynamic_slice(w_out_temporal, (jnp.maximum(start - 3 * side, 0), 0), (size, width)),
        lax.dynamic_slice(
            turned_qkv.reshape(3 * side, width), (jnp.minimum(start, 3 * side - size), 0), (size, width)
        ),
    )

    mods, *hidden = first(levels, mod_table, queue_tokens, chunk)
    frames = [{0: h} for h in hidden]
    reach = ((4, 3), (3, 4))
    for step in range(1, 5):
        for j in range(2):
            if step <= reach[j][0]:
                frames[j][-step] = send_up(frames[j][1 - step])
            if step <= reach[j][1]:
                frames[j][step] = send_down(frames[j][step - 1])
    order = [[0, 1, 2, 3, -4, -3, -2, -1], [0, 1, 2, 3, 4, -3, -2, -1]]
    *tied, _, _ = lax.optimization_barrier(
        tuple(frames[0][o] for o in order[0]) + (frames[1][4], frames[1][-3])
    )
    pieces = stack(size, tied)
    weights = lax.all_gather(pieces, "queue", axis=0, tiled=False)

    w_spatial = jnp.swapaxes(w_qkv_spatial, 1, 2)
    parts = []

    def add(value, other):
        return (value.astype(F32) + other.astype(F32)).astype(BF16)

    done, rise, fall = [None] * 2, [None] * 2, [None] * 2
    for j in range(2):
        blocks = [frames[j][o] for o in order[j]]
        done[j] = dict(zip(order[j], spatial(rows, w_spatial, w_out_spatial, blocks)))
        far_up, far_down = reach[j]
        rise[j] = send_up(done[j][far_up if far_up < 4 else -4])
        fall[j] = send_down(done[j][-far_down if far_down < 4 else 4])
    rise[0], fall[0], *rest = lax.optimization_barrier((rise[0], fall[0], *[done[1][o] for o in order[1]]))
    done[1] = dict(zip(order[1], rest))
    for j in range(2):
        far_up, far_down = reach[j]
        for o in range(far_up - 1, 0, -1):
            rise[j] = send_up(add(done[j][o], rise[j]))
        for o in range(far_down - 1, 0, -1):
            fall[j] = send_down(add(done[j][-o], fall[j]))
        parts += [done[j][0], rise[j], fall[j]]

    x1, h2, pack = middle(queue_tokens, mods, parts)
    pack = lax.ppermute(pack, "queue", [(i, i - 1) for i in range(1, line)])
    per = rows // line
    sent = jnp.transpose(h2.reshape(2, line, per, width), (1, 0, 2, 3)).reshape(line, 2 * per, width)
    got = lax.all_to_all(sent, "queue", 0, 0, tiled=True)
    branch = temporal(ring, per, got.reshape(line * 2 * per, width), weights)
    got = lax.all_to_all(branch.reshape(line, 2 * per, width), "queue", 0, 0, tiled=True)
    branch = jnp.transpose(got.reshape(line, 2, per, width), (1, 0, 2, 3)).reshape(2, rows, width)
    at_tail = (spot == line - 1).astype(jnp.int32)[None]
    return last(at_tail, x1, mods, pack, branch, fresh_frame)


def solution(mesh):
    return jax.shard_map(
        per_device,
        mesh=mesh,
        in_specs=(
            P("queue", "tok", None),
            P("tok", None),
            P("queue"),
            P(),
            P(None, None, "tok"),
            P("tok", None),
            P(None, None, "tok"),
            P("tok", None),
        ),
        out_specs=P("queue", "tok", None),
        check_vma=False,
    )
```

```python
import jax
import jax.numpy as jnp
from jax import lax
from jax.experimental import pallas as pl
from jax.experimental.pallas import tpu as pltpu
from jax.sharding import PartitionSpec as P

HEADS = 16
HDIM = 72
EPS = 1e-06
FACTOR = HDIM ** (-0.5)
BF16 = jnp.bfloat16
F32 = jnp.float32
VMEM = pltpu.VMEM


def params(mib):
    return pltpu.CompilerParams(vmem_limit_bytes=mib * 1024 * 1024)


def vspec():
    return pl.BlockSpec(memory_space=VMEM)


def normalize(values):
    mean = jnp.mean(values, axis=-1, keepdims=True)
    centered = values - mean
    variance = jnp.mean(centered * centered, axis=-1, keepdims=True)
    return centered * lax.rsqrt(variance + EPS)


def turned(values, matrix):
    return lax.dot_general(values, matrix, (((1,), (1,)), ((), ())), preferred_element_type=F32)


def first_kernel(levels_ref, table_ref, tokens_ref, mods_ref, h0_ref, h1_ref, near, held, sems):
    rows, width = tokens_ref.shape[1:]
    copies = [pltpu.make_async_copy(tokens_ref, held, sems.at[2])]
    for j in range(2):
        base = pl.multiple_of(levels_ref[j] // 8 * 8, 8)
        copies.append(pltpu.make_async_copy(table_ref.at[pl.ds(base, 8)], near.at[j], sems.at[j]))
    for copy in copies:
        copy.start()
    for copy in copies:
        copy.wait()
    for j, out in enumerate((h0_ref, h1_ref)):
        row = near[j, pl.ds(levels_ref[j] % 8, 1), :]
        mods_ref[j : j + 1, :] = row
        values = normalize(held[j].astype(F32))
        out[...] = (values * (1.0 + row[:, width : 2 * width]) + row[:, :width]).astype(BF16)


def first(levels, table, tokens):
    _, rows, width = tokens.shape
    block = jax.ShapeDtypeStruct((rows, width), BF16)
    return pl.pallas_call(
        first_kernel,
        out_shape=(jax.ShapeDtypeStruct((2, table.shape[1]), F32), block, block),
        in_specs=[pl.BlockSpec(memory_space=pltpu.SMEM)] + [pl.BlockSpec(memory_space=pl.ANY)] * 2,
        out_specs=(vspec(), vspec(), vspec()),
        scratch_shapes=[
            VMEM((2, 8, table.shape[1]), F32),
            VMEM(tokens.shape, BF16),
            pltpu.SemaphoreType.DMA((3,)),
        ],
        compiler_params=params(50),
        cost_estimate=pl.CostEstimate(flops=4000000, bytes_accessed=3000000, transcendentals=0),
        name="first",
    )(levels, table, tokens)


def stack_kernel(in_ref, out_ref):
    count, size, width = in_ref.shape
    pieces = [in_ref[n].astype(F32) for n in range(count)]
    out_ref[...] = jnp.concatenate(pieces, axis=0).astype(BF16)


def stack(blocks):
    count, size, width = blocks.shape
    return pl.pallas_call(
        stack_kernel,
        out_shape=jax.ShapeDtypeStruct((count * size, width), BF16),
        in_specs=[vspec()],
        out_specs=vspec(),
        compiler_params=params(8),
        cost_estimate=pl.CostEstimate(flops=0, bytes_accessed=700000, transcendentals=0),
        name="stack",
    )(blocks)


def spatial_kernel(wq_hbm, wo_hbm, *refs):
    *refs, wq_ref, wo_ref, sems = refs
    first_copy = pltpu.make_async_copy(wq_hbm, wq_ref, sems.at[0])
    later_copy = pltpu.make_async_copy(wo_hbm, wo_ref, sems.at[1])
    first_copy.start()
    later_copy.start()
    blocks, outs = refs[: len(refs) // 2], refs[len(refs) // 2 :]
    rows = blocks[0].shape[0]
    hidden = jnp.concatenate([ref[...] for ref in blocks], axis=0)
    first_copy.wait()
    query, keyed, valued = [turned(hidden, wq_ref[m]).astype(BF16) for m in range(3)]
    heads = []
    for h in range(query.shape[1] // HDIM):
        cut = slice(h * HDIM, (h + 1) * HDIM)
        scores = FACTOR * turned(query[:, cut], keyed[:, cut])
        weights = jnp.exp(scores - jnp.max(scores, axis=-1, keepdims=True))
        total = jnp.sum(weights, axis=-1, keepdims=True)
        mixed = jnp.dot(weights.astype(BF16), valued[:, cut], preferred_element_type=F32)
        heads.append((mixed / total).astype(BF16))
    attended = jnp.concatenate(heads, axis=1)
    later_copy.wait()
    for n, out in enumerate(outs):
        piece = attended[n * rows : (n + 1) * rows]
        out[...] = jnp.dot(piece, wo_ref[...], preferred_element_type=F32).astype(BF16)


def spatial(w_qkv, w_out, blocks):
    rows, width = blocks[0].shape
    whole = rows * len(blocks)
    return pl.pallas_call(
        spatial_kernel,
        out_shape=[jax.ShapeDtypeStruct((rows, width), BF16) for _ in blocks],
        in_specs=[pl.BlockSpec(memory_space=pl.ANY)] * 2 + [vspec()] * len(blocks),
        out_specs=[vspec()] * len(blocks),
        scratch_shapes=[
            VMEM(w_qkv.shape, BF16),
            VMEM(w_out.shape, BF16),
            pltpu.SemaphoreType.DMA((2,)),
        ],
        compiler_params=params(40),
        cost_estimate=pl.CostEstimate(
            flops=2 * whole * width * 144 * 4 + 4 * whole * whole * 256,
            bytes_accessed=5000000,
            transcendentals=2 * whole * whole,
        ),
        name="spatial",
    )(w_qkv, w_out, *blocks)


def middle_kernel(tokens_ref, mods_ref, *refs):
    parts, (x1_ref, h2_ref, pack_ref) = refs[:-3], refs[-3:]
    rows, width = x1_ref.shape[1:]
    for j in range(2):
        own, one, two = [parts[3 * j + k][...].astype(F32) for k in range(3)]
        branch = own + one + two

        def row(n):
            return mods_ref[j : j + 1, n * width : (n + 1) * width]

        x1 = tokens_ref[j].astype(F32) + row(2) * branch
        x1_ref[j] = x1
        h2_ref[j] = (normalize(x1) * (1.0 + row(4)) + row(3)).astype(BF16)
        if j == 0:
            pack_ref[:rows] = x1
            pack_ref[rows:] = jnp.broadcast_to(row(5), (8, width))


def middle(tokens, mods, parts):
    _, rows, width = tokens.shape
    return pl.pallas_call(
        middle_kernel,
        out_shape=(
            jax.ShapeDtypeStruct(tokens.shape, F32),
            jax.ShapeDtypeStruct(tokens.shape, BF16),
            jax.ShapeDtypeStruct((rows + 8, width), F32),
        ),
        in_specs=[vspec()] * (2 + len(parts)),
        out_specs=(vspec(), vspec(), vspec()),
        compiler_params=params(8),
        cost_estimate=pl.CostEstimate(flops=4000000, bytes_accessed=3000000, transcendentals=0),
        name="middle",
    )(tokens, mods, *parts)


def temporal_kernel(ring, size, per, hidden_ref, weights_ref, out_ref, held, sems):
    pieces, depth, width = weights_ref.shape
    some = pieces // 8

    def copy(n):
        part = pl.ds(n * some, some)
        return pltpu.make_async_copy(weights_ref.at[part], held.at[part], sems.at[n])

    for n in range(8):
        copy(n).start()
    hidden = hidden_ref[...]
    rows = hidden.shape[0]
    half = width // 2

    def matrix(m, s):
        n = 2 * m + s
        copy(n).wait()
        return held[n * some : (n + 1) * some].reshape(half, width)

    lane = lax.broadcasted_iota(jnp.int32, (1, half), 1)
    owned = []
    for z in range(ring):
        mask = jnp.zeros((1, half), jnp.bool_)
        for a in range(some):
            low = a * depth + z * size
            mask = mask | ((lane >= low) & (lane < low + size))
        owned.append(mask)
    along = lax.broadcasted_iota(jnp.int32, (ring * rows, rows), 0) % per
    across = lax.broadcasted_iota(jnp.int32, (ring * rows, rows), 1) % per
    same = along == across

    query = [turned(hidden, matrix(0, s)) for s in range(2)]
    keyed = [turned(hidden, matrix(1, s)).astype(BF16) for s in range(2)]
    valued = [turned(hidden, matrix(2, s)).astype(BF16) for s in range(2)]
    branch = jnp.zeros((rows, width), F32)
    for s in range(2):
        spread = jnp.concatenate([jnp.where(m, query[s], 0.0) for m in owned], axis=0).astype(BF16)
        scores = jnp.where(same, FACTOR * turned(spread, keyed[s]), -jnp.inf)
        weights = jnp.exp(scores - jnp.max(scores, axis=-1, keepdims=True))
        total = jnp.sum(weights, axis=-1, keepdims=True)
        mixed = jnp.dot(weights.astype(BF16), valued[s], preferred_element_type=F32) / total
        attended = jnp.zeros((rows, half), F32)
        for z, m in enumerate(owned):
            attended = jnp.where(m, mixed[z * rows : (z + 1) * rows], attended)
        branch += jnp.dot(attended.astype(BF16), matrix(3, s), preferred_element_type=F32)
    out_ref[...] = jnp.concatenate([branch[per:], branch[:per]], axis=0).astype(BF16)


def temporal(ring, per, hidden, weights):
    pieces, depth, width = weights.shape
    rows = hidden.shape[0]
    return pl.pallas_call(
        lambda *refs: temporal_kernel(ring, depth // ring, per, *refs),
        out_shape=jax.ShapeDtypeStruct((rows, width), BF16),
        in_specs=[vspec(), pl.BlockSpec(memory_space=pl.ANY)],
        out_specs=vspec(),
        scratch_shapes=[
            VMEM((pieces, depth, width), BF16),
            pltpu.SemaphoreType.DMA((8,)),
        ],
        compiler_params=params(50),
        cost_estimate=pl.CostEstimate(
            flops=2 * rows * width * width * 4, bytes_accessed=12000000, transcendentals=16 * rows * rows
        ),
        name="temporal",
    )(hidden, weights)


def last_kernel(tail_ref, x1_ref, mods_ref, pack_ref, branch_ref, fresh_ref, out_ref):
    rows, width = x1_ref.shape[1:]
    gate = mods_ref[1:2, 5 * width :]
    out_ref[0] = (x1_ref[1] + gate * branch_ref[0].astype(F32)).astype(BF16)
    moved = (pack_ref[:rows] + pack_ref[rows : rows + 1] * branch_ref[1].astype(F32)).astype(BF16)

    @pl.when(tail_ref[0] == 0)
    def _():
        out_ref[1] = moved

    @pl.when(tail_ref[0] != 0)
    def _():
        out_ref[1] = fresh_ref[...]


def last(at_tail, x1, mods, pack, branch, fresh):
    return pl.pallas_call(
        last_kernel,
        out_shape=jax.ShapeDtypeStruct(x1.shape, BF16),
        in_specs=[pl.BlockSpec(memory_space=pltpu.SMEM)] + [vspec()] * 5,
        out_specs=vspec(),
        compiler_params=params(8),
        cost_estimate=pl.CostEstimate(flops=1000000, bytes_accessed=2000000, transcendentals=0),
        name="last",
    )(at_tail, x1, mods, pack, branch, fresh)


def per_device(
    queue_tokens,
    fresh_frame,
    levels,
    mod_table,
    w_qkv_spatial,
    w_out_spatial,
    w_qkv_temporal,
    w_out_temporal,
):
    _, rows, width = queue_tokens.shape
    ring = lax.axis_size("tok")
    line = lax.axis_size("queue")
    spot = lax.axis_index("queue")
    up = [(i, (i + 1) % ring) for i in range(ring)]
    down = [(i, (i - 1) % ring) for i in range(ring)]

    def send_up(v):
        return lax.ppermute(v, "tok", up)

    def send_down(v):
        return lax.ppermute(v, "tok", down)

    turned_qkv = jnp.swapaxes(w_qkv_temporal, 1, 2)
    side = w_out_temporal.shape[0]
    size = 4 * side // line
    start = spot * size
    chunk = jnp.where(
        start >= 3 * side,
        lax.dynamic_slice(w_out_temporal, (jnp.maximum(start - 3 * side, 0), 0), (size, width)),
        lax.dynamic_slice(
            turned_qkv.reshape(3 * side, width), (jnp.minimum(start, 3 * side - size), 0), (size, width)
        ),
    )
    chunks = lax.all_to_all(
        jnp.broadcast_to(chunk[None], (ring, size, width)), "tok", 0, 0, tiled=True
    )
    weights = lax.all_gather(stack(chunks), "queue", axis=0, tiled=False)

    mods, *hidden = first(levels, mod_table, queue_tokens)
    frames = [{0: h} for h in hidden]
    reach = ((4, 3), (3, 4))
    for step in range(1, 5):
        for j in range(2):
            if step <= reach[j][0]:
                frames[j][-step] = send_up(frames[j][1 - step])
            if step <= reach[j][1]:
                frames[j][step] = send_down(frames[j][step - 1])
    order = [[0, 1, 2, 3, -4, -3, -2, -1], [0, 1, 2, 3, 4, -3, -2, -1]]

    w_spatial = jnp.swapaxes(w_qkv_spatial, 1, 2)
    parts = []

    def add(value, other):
        return (value.astype(F32) + other.astype(F32)).astype(BF16)

    done, rise, fall = [None] * 2, [None] * 2, [None] * 2
    for j in range(2):
        blocks = [frames[j][o] for o in order[j]]
        done[j] = dict(zip(order[j], spatial(w_spatial, w_out_spatial, blocks)))
        far_up, far_down = reach[j]
        rise[j] = send_up(done[j][far_up if far_up < 4 else -4])
        fall[j] = send_down(done[j][-far_down if far_down < 4 else 4])
    rise[0], fall[0], *rest = lax.optimization_barrier((rise[0], fall[0], *[done[1][o] for o in order[1]]))
    done[1] = dict(zip(order[1], rest))
    for j in range(2):
        far_up, far_down = reach[j]
        for o in range(far_up - 1, 0, -1):
            rise[j] = send_up(add(done[j][o], rise[j]))
        for o in range(far_down - 1, 0, -1):
            fall[j] = send_down(add(done[j][-o], fall[j]))
        parts += [done[j][0], rise[j], fall[j]]

    x1, h2, pack = middle(queue_tokens, mods, parts)
    pack = lax.ppermute(pack, "queue", [(i, i - 1) for i in range(1, line)])
    per = rows // line
    sent = jnp.transpose(h2.reshape(2, line, per, width), (1, 0, 2, 3)).reshape(line, 2 * per, width)
    got = lax.all_to_all(sent, "queue", 0, 0, tiled=True)
    branch = temporal(ring, per, got.reshape(line * 2 * per, width), weights)
    got = lax.all_to_all(branch.reshape(line, 2 * per, width), "queue", 0, 0, tiled=True)
    branch = jnp.transpose(got.reshape(line, 2, per, width), (1, 0, 2, 3)).reshape(2, rows, width)
    at_tail = (spot == line - 1).astype(jnp.int32)[None]
    return last(at_tail, x1, mods, pack, branch, fresh_frame)


def solution(mesh):
    return jax.shard_map(
        per_device,
        mesh=mesh,
        in_specs=(
            P("queue", "tok", None),
            P("tok", None),
            P("queue"),
            P(),
            P(None, None, "tok"),
            P("tok", None),
            P(None, None, "tok"),
            P("tok", None),
        ),
        out_specs=P("queue", "tok", None),
        check_vma=False,
    )
```

```python
import jax
import jax.numpy as jnp
from jax import lax
from jax.experimental import pallas as pl
from jax.experimental.pallas import tpu as pltpu
from jax.sharding import PartitionSpec as P

HEADS = 16
HDIM = 72
EPS = 1e-06
FACTOR = HDIM ** (-0.5)
BF16 = jnp.bfloat16
F32 = jnp.float32
VMEM = pltpu.VMEM


def params(mib):
    return pltpu.CompilerParams(vmem_limit_bytes=mib * 1024 * 1024)


def vspec():
    return pl.BlockSpec(memory_space=VMEM)


def in_hbm(values):
    return pltpu.with_memory_space_constraint(values, pltpu.HBM)


def normalize(values):
    mean = jnp.mean(values, axis=-1, keepdims=True)
    centered = values - mean
    variance = jnp.mean(centered * centered, axis=-1, keepdims=True)
    return centered * lax.rsqrt(variance + EPS)


def turned(values, matrix):
    return lax.dot_general(values, matrix, (((1,), (1,)), ((), ())), preferred_element_type=F32)


def first_kernel(levels_ref, table_ref, tokens_ref, mods_ref, h0_ref, h1_ref, near, held, sems):
    rows, width = tokens_ref.shape[1:]
    copies = [pltpu.make_async_copy(tokens_ref, held, sems.at[2])]
    for j in range(2):
        base = pl.multiple_of(levels_ref[j] // 8 * 8, 8)
        copies.append(pltpu.make_async_copy(table_ref.at[pl.ds(base, 8)], near.at[j], sems.at[j]))
    for copy in copies:
        copy.start()
    for copy in copies:
        copy.wait()
    for j, out in enumerate((h0_ref, h1_ref)):
        row = near[j, pl.ds(levels_ref[j] % 8, 1), :]
        mods_ref[j : j + 1, :] = row
        values = normalize(held[j].astype(F32))
        out[...] = (values * (1.0 + row[:, width : 2 * width]) + row[:, :width]).astype(BF16)


def first(levels, table, tokens):
    _, rows, width = tokens.shape
    block = jax.ShapeDtypeStruct((rows, width), BF16)
    return pl.pallas_call(
        first_kernel,
        out_shape=(jax.ShapeDtypeStruct((2, table.shape[1]), F32), block, block),
        in_specs=[pl.BlockSpec(memory_space=pltpu.SMEM)] + [pl.BlockSpec(memory_space=pl.ANY)] * 2,
        out_specs=(vspec(), vspec(), vspec()),
        scratch_shapes=[
            VMEM((2, 8, table.shape[1]), F32),
            VMEM(tokens.shape, BF16),
            pltpu.SemaphoreType.DMA((3,)),
        ],
        compiler_params=params(24),
        cost_estimate=pl.CostEstimate(flops=4000000, bytes_accessed=3000000, transcendentals=0),
        name="first",
    )(levels, in_hbm(table), in_hbm(tokens))


def spatial_kernel(wq_hbm, wo_hbm, *refs):
    *refs, wq_ref, wo_ref, sems = refs
    first_copy = pltpu.make_async_copy(wq_hbm, wq_ref, sems.at[0])
    later_copy = pltpu.make_async_copy(wo_hbm, wo_ref, sems.at[1])
    first_copy.start()
    later_copy.start()
    blocks, outs = refs[: len(refs) // 2], refs[len(refs) // 2 :]
    rows = blocks[0].shape[0]
    hidden = jnp.concatenate([ref[...] for ref in blocks], axis=0)
    first_copy.wait()
    query, keyed, valued = [turned(hidden, wq_ref[m]).astype(BF16) for m in range(3)]
    heads = []
    for h in range(query.shape[1] // HDIM):
        cut = slice(h * HDIM, (h + 1) * HDIM)
        scores = FACTOR * turned(query[:, cut], keyed[:, cut])
        weights = jnp.exp(scores - jnp.max(scores, axis=-1, keepdims=True))
        total = jnp.sum(weights, axis=-1, keepdims=True)
        mixed = jnp.dot(weights.astype(BF16), valued[:, cut], preferred_element_type=F32)
        heads.append((mixed / total).astype(BF16))
    attended = jnp.concatenate(heads, axis=1)
    later_copy.wait()
    for n, out in enumerate(outs):
        piece = attended[n * rows : (n + 1) * rows]
        out[...] = jnp.dot(piece, wo_ref[...], preferred_element_type=F32).astype(BF16)


def spatial(w_qkv, w_out, blocks):
    rows, width = blocks[0].shape
    whole = rows * len(blocks)
    return pl.pallas_call(
        spatial_kernel,
        out_shape=[jax.ShapeDtypeStruct((rows, width), BF16) for _ in blocks],
        in_specs=[pl.BlockSpec(memory_space=pl.ANY)] * 2 + [vspec()] * len(blocks),
        out_specs=[vspec()] * len(blocks),
        scratch_shapes=[
            VMEM(w_qkv.shape, BF16),
            VMEM(w_out.shape, BF16),
            pltpu.SemaphoreType.DMA((2,)),
        ],
        compiler_params=params(20),
        cost_estimate=pl.CostEstimate(
            flops=2 * whole * width * 144 * 4 + 4 * whole * whole * 256,
            bytes_accessed=5000000,
            transcendentals=2 * whole * whole,
        ),
        name="spatial",
    )(in_hbm(w_qkv), in_hbm(w_out), *blocks)


def middle_kernel(tokens_ref, mods_ref, *refs):
    parts, (x1_ref, h2_ref, pack_ref) = refs[:-3], refs[-3:]
    rows, width = x1_ref.shape[1:]
    for j in range(2):
        own, one, two = [parts[3 * j + k][...].astype(F32) for k in range(3)]
        branch = own + one + two

        def row(n):
            return mods_ref[j : j + 1, n * width : (n + 1) * width]

        x1 = tokens_ref[j].astype(F32) + row(2) * branch
        x1_ref[j] = x1
        h2_ref[j] = (normalize(x1) * (1.0 + row(4)) + row(3)).astype(BF16)
        if j == 0:
            pack_ref[:rows] = x1
            pack_ref[rows:] = jnp.broadcast_to(row(5), (8, width))


def middle(tokens, mods, parts):
    _, rows, width = tokens.shape
    return pl.pallas_call(
        middle_kernel,
        out_shape=(
            jax.ShapeDtypeStruct(tokens.shape, F32),
            jax.ShapeDtypeStruct(tokens.shape, BF16),
            jax.ShapeDtypeStruct((rows + 8, width), F32),
        ),
        in_specs=[vspec()] * (2 + len(parts)),
        out_specs=(vspec(), vspec(), vspec()),
        compiler_params=params(8),
        cost_estimate=pl.CostEstimate(flops=4000000, bytes_accessed=3000000, transcendentals=0),
        name="middle",
    )(tokens, mods, *parts)


def temporal_kernel(per, hidden_ref, weights_ref, out_ref, held, sems):
    pieces, depth, width = weights_ref.shape
    some = pieces // 8

    def copy(n):
        part = pl.ds(n * some, some)
        return pltpu.make_async_copy(weights_ref.at[part], held.at[part], sems.at[n])

    for n in range(8):
        copy(n).start()
    hidden = hidden_ref[...]
    rows = hidden.shape[0]
    half = width // 2
    heads = half // HDIM

    def matrix(m, s):
        n = 2 * m + s
        copy(n).wait()
        return held[n * some : (n + 1) * some].reshape(half, width)

    lane = lax.broadcasted_iota(jnp.int32, (1, half), 1)
    owned = [(lane >= h * HDIM) & (lane < (h + 1) * HDIM) for h in range(heads)]
    along = lax.broadcasted_iota(jnp.int32, (heads * rows, rows), 0) % per
    across = lax.broadcasted_iota(jnp.int32, (heads * rows, rows), 1) % per
    same = along == across

    query = [turned(hidden, matrix(0, s)) for s in range(2)]
    keyed = [turned(hidden, matrix(1, s)).astype(BF16) for s in range(2)]
    valued = [turned(hidden, matrix(2, s)).astype(BF16) for s in range(2)]
    branch = jnp.zeros((rows, width), F32)
    for s in range(2):
        spread = jnp.concatenate([jnp.where(m, query[s], 0.0) for m in owned], axis=0).astype(BF16)
        scores = jnp.where(same, FACTOR * turned(spread, keyed[s]), -jnp.inf)
        weights = jnp.exp(scores - jnp.max(scores, axis=-1, keepdims=True))
        total = jnp.sum(weights, axis=-1, keepdims=True)
        mixed = jnp.dot(weights.astype(BF16), valued[s], preferred_element_type=F32) / total
        attended = jnp.zeros((rows, half), F32)
        for h, m in enumerate(owned):
            attended = jnp.where(m, mixed[h * rows : (h + 1) * rows], attended)
        branch += jnp.dot(attended.astype(BF16), matrix(3, s), preferred_element_type=F32)
    out_ref[...] = jnp.concatenate([branch[per:], branch[:per]], axis=0).astype(BF16)


def temporal(per, hidden, weights):
    pieces, depth, width = weights.shape
    rows = hidden.shape[0]
    return pl.pallas_call(
        lambda *refs: temporal_kernel(per, *refs),
        out_shape=jax.ShapeDtypeStruct((rows, width), BF16),
        in_specs=[vspec(), pl.BlockSpec(memory_space=pl.ANY)],
        out_specs=vspec(),
        scratch_shapes=[
            VMEM((pieces, depth, width), BF16),
            pltpu.SemaphoreType.DMA((8,)),
        ],
        compiler_params=params(24),
        cost_estimate=pl.CostEstimate(
            flops=2 * rows * width * width * 4, bytes_accessed=12000000, transcendentals=16 * rows * rows
        ),
        name="temporal",
    )(hidden, in_hbm(weights))


def last_kernel(tail_ref, x1_ref, mods_ref, pack_ref, branch_ref, fresh_ref, out_ref):
    rows, width = x1_ref.shape[1:]
    gate = mods_ref[1:2, 5 * width :]
    out_ref[0] = (x1_ref[1] + gate * branch_ref[0].astype(F32)).astype(BF16)
    moved = (pack_ref[:rows] + pack_ref[rows : rows + 1] * branch_ref[1].astype(F32)).astype(BF16)

    @pl.when(tail_ref[0] == 0)
    def _():
        out_ref[1] = moved

    @pl.when(tail_ref[0] != 0)
    def _():
        out_ref[1] = fresh_ref[...]


def last(at_tail, x1, mods, pack, branch, fresh):
    return pl.pallas_call(
        last_kernel,
        out_shape=jax.ShapeDtypeStruct(x1.shape, BF16),
        in_specs=[pl.BlockSpec(memory_space=pltpu.SMEM)] + [vspec()] * 5,
        out_specs=vspec(),
        compiler_params=params(8),
        cost_estimate=pl.CostEstimate(flops=1000000, bytes_accessed=2000000, transcendentals=0),
        name="last",
    )(at_tail, x1, mods, pack, branch, fresh)


def per_device(
    queue_tokens,
    fresh_frame,
    levels,
    mod_table,
    w_qkv_spatial,
    w_out_spatial,
    w_qkv_temporal,
    w_out_temporal,
):
    _, rows, width = queue_tokens.shape
    ring = lax.axis_size("tok")
    line = lax.axis_size("queue")
    spot = lax.axis_index("queue")
    up = [(i, (i + 1) % ring) for i in range(ring)]
    down = [(i, (i - 1) % ring) for i in range(ring)]

    def send_up(v):
        return lax.ppermute(v, "tok", up)

    def send_down(v):
        return lax.ppermute(v, "tok", down)

    turned_qkv = jnp.swapaxes(w_qkv_temporal, 1, 2)
    which = spot // ring
    chunk = jnp.where(
        which == 3, w_out_temporal, lax.dynamic_index_in_dim(turned_qkv, jnp.minimum(which, 2), keepdims=False)
    )
    far = [n // 2 + n % 2 * (ring // 2) for n in range(ring)]
    pairs = [(q * ring + z, q * ring + (z - far[q % ring]) % ring) for q in range(line) for z in range(ring)]
    chunk = lax.ppermute(chunk, ("queue", "tok"), pairs)

    mods, *hidden = first(levels, mod_table, queue_tokens)
    frames = [{0: h} for h in hidden]
    reach = ((4, 3), (3, 4))
    for step in range(1, 5):
        for j in range(2):
            if step <= reach[j][0]:
                frames[j][-step] = send_up(frames[j][1 - step])
            if step <= reach[j][1]:
                frames[j][step] = send_down(frames[j][step - 1])
    chunk, *_ = lax.optimization_barrier((chunk, *[frames[j][o] for j in range(2) for o in (-2, 2)]))
    weights = lax.all_gather(chunk, "queue", axis=0, tiled=False)

    order = [[0, 1, 2, 3, -4, -3, -2, -1], [0, 1, 2, 3, 4, -3, -2, -1]]

    w_spatial = jnp.swapaxes(w_qkv_spatial, 1, 2)
    parts = []

    def add(value, other):
        return (value.astype(F32) + other.astype(F32)).astype(BF16)

    done, rise, fall = [None] * 2, [None] * 2, [None] * 2
    for j in range(2):
        blocks = [frames[j][o] for o in order[j]]
        done[j] = dict(zip(order[j], spatial(w_spatial, w_out_spatial, blocks)))
        far_up, far_down = reach[j]
        rise[j] = send_up(done[j][far_up if far_up < 4 else -4])
        fall[j] = send_down(done[j][-far_down if far_down < 4 else 4])
    rise[0], fall[0], *rest = lax.optimization_barrier((rise[0], fall[0], *[done[1][o] for o in order[1]]))
    done[1] = dict(zip(order[1], rest))
    for j in range(2):
        far_up, far_down = reach[j]
        for o in range(far_up - 1, 0, -1):
            rise[j] = send_up(add(done[j][o], rise[j]))
        for o in range(far_down - 1, 0, -1):
            fall[j] = send_down(add(done[j][-o], fall[j]))
        parts += [done[j][0], rise[j], fall[j]]

    x1, h2, pack = middle(queue_tokens, mods, parts)
    pack = lax.ppermute(pack, "queue", [(i, i - 1) for i in range(1, line)])
    per = rows // line
    sent = jnp.transpose(h2.reshape(2, line, per, width), (1, 0, 2, 3)).reshape(line, 2 * per, width)
    got = lax.all_to_all(sent, "queue", 0, 0, tiled=True)
    branch = temporal(per, got.reshape(line * 2 * per, width), weights)
    got = lax.all_to_all(branch.reshape(line, 2 * per, width), "queue", 0, 0, tiled=True)
    branch = jnp.transpose(got.reshape(line, 2, per, width), (1, 0, 2, 3)).reshape(2, rows, width)
    at_tail = (spot == line - 1).astype(jnp.int32)[None]
    return last(at_tail, x1, mods, pack, branch, fresh_frame)


def solution(mesh):
    return jax.shard_map(
        per_device,
        mesh=mesh,
        in_specs=(
            P("queue", "tok", None),
            P("tok", None),
            P("queue"),
            P(),
            P(None, None, "tok"),
            P("tok", None),
            P(None, None, "tok"),
            P("tok", None),
        ),
        out_specs=P("queue", "tok", None),
        check_vma=False,
    )
```

```python
import jax
import jax.numpy as jnp
from jax import lax
from jax.experimental import pallas as pl
from jax.experimental.pallas import tpu as pltpu
from jax.sharding import PartitionSpec as P

HEADS = 16
HDIM = 72
EPS = 1e-06
FACTOR = HDIM ** (-0.5)
BF16 = jnp.bfloat16
F32 = jnp.float32
VMEM = pltpu.VMEM


def params(mib):
    return pltpu.CompilerParams(vmem_limit_bytes=mib * 1024 * 1024)


def vspec():
    return pl.BlockSpec(memory_space=VMEM)


def in_hbm(values):
    return pltpu.with_memory_space_constraint(values, pltpu.HBM)


def normalize(values):
    mean = jnp.mean(values, axis=-1, keepdims=True)
    centered = values - mean
    variance = jnp.mean(centered * centered, axis=-1, keepdims=True)
    return centered * lax.rsqrt(variance + EPS)


def turned(values, matrix):
    return lax.dot_general(values, matrix, (((1,), (1,)), ((), ())), preferred_element_type=F32)


def first_kernel(levels_ref, table_ref, tokens_ref, h0_ref, h1_ref, near, held, sems):
    rows, width = tokens_ref.shape[1:]
    copies = [pltpu.make_async_copy(tokens_ref, held, sems.at[2])]
    for j in range(2):
        base = pl.multiple_of(levels_ref[j] // 8 * 8, 8)
        copies.append(pltpu.make_async_copy(table_ref.at[pl.ds(base, 8), pl.ds(0, 2 * width)], near.at[j], sems.at[j]))
    for copy in copies:
        copy.start()
    for copy in copies:
        copy.wait()
    for j, out in enumerate((h0_ref, h1_ref)):
        row = near[j, pl.ds(levels_ref[j] % 8, 1), :]
        values = normalize(held[j].astype(F32))
        out[...] = (values * (1.0 + row[:, width : 2 * width]) + row[:, :width]).astype(BF16)


def first(levels, table, tokens):
    _, rows, width = tokens.shape
    block = jax.ShapeDtypeStruct((rows, width), BF16)
    return pl.pallas_call(
        first_kernel,
        out_shape=(block, block),
        in_specs=[pl.BlockSpec(memory_space=pltpu.SMEM)] + [pl.BlockSpec(memory_space=pl.ANY)] * 2,
        out_specs=(vspec(), vspec()),
        scratch_shapes=[
            VMEM((2, 8, 2 * width), F32),
            VMEM(tokens.shape, BF16),
            pltpu.SemaphoreType.DMA((3,)),
        ],
        compiler_params=params(24),
        cost_estimate=pl.CostEstimate(flops=4000000, bytes_accessed=3000000, transcendentals=0),
        name="first",
    )(levels, in_hbm(table), in_hbm(tokens))


def spatial_kernel(offsets, place_ref, w_hbm, *refs):
    *refs, out_ref, w_ref, sem = refs
    copy = pltpu.make_async_copy(w_hbm, w_ref, sem)
    copy.start()
    rows = refs[0].shape[0]
    ring = len(offsets[0])
    copy.wait()
    for j in range(2):
        hidden = jnp.concatenate([ref[...] for ref in refs[j * ring : (j + 1) * ring]], axis=0)
        query = turned(w_ref[0], hidden).astype(BF16)
        keyed = turned(hidden, w_ref[1]).astype(BF16)
        valued = turned(w_ref[2], hidden).astype(BF16)
        heads = []
        for h in range(query.shape[0] // HDIM):
            cut = slice(h * HDIM, (h + 1) * HDIM)
            scores = FACTOR * jnp.dot(keyed[:, cut], query[cut], preferred_element_type=F32)
            weights = jnp.exp(scores - jnp.max(scores, axis=0, keepdims=True))
            total = jnp.sum(weights, axis=0, keepdims=True)
            mixed = jnp.dot(valued[cut], weights.astype(BF16), preferred_element_type=F32)
            heads.append((mixed / total).astype(BF16))
        attended = jnp.concatenate(heads, axis=0)
        for n, offset in enumerate(offsets[j]):
            owner = lax.rem(place_ref[0] + offset + ring, ring)
            out_ref[owner, :, j * rows : (j + 1) * rows] = attended[:, n * rows : (n + 1) * rows]


def spatial(offsets, place, w_qkv, blocks):
    rows, width = blocks[0].shape
    ring = len(offsets[0])
    whole = rows * ring
    return pl.pallas_call(
        lambda *refs: spatial_kernel(offsets, *refs),
        out_shape=jax.ShapeDtypeStruct((ring, w_qkv.shape[1], 2 * rows), BF16),
        in_specs=[pl.BlockSpec(memory_space=pltpu.SMEM), pl.BlockSpec(memory_space=pl.ANY)]
        + [vspec()] * len(blocks),
        out_specs=vspec(),
        scratch_shapes=[VMEM(w_qkv.shape, BF16), pltpu.SemaphoreType.DMA],
        compiler_params=params(20),
        cost_estimate=pl.CostEstimate(
            flops=4 * whole * width * 144 * 3 + 8 * whole * whole * 256,
            bytes_accessed=5000000,
            transcendentals=4 * whole * whole,
        ),
        name="spatial",
    )(place, in_hbm(w_qkv), *blocks)


def bundle_kernel(line, size, levels_ref, mixed_ref, tokens_ref, out_ref):
    ring, side, rows = mixed_ref.shape
    width = ring * side
    per = rows // (2 * line)
    mixed = jnp.concatenate(
        [mixed_ref[z, a * size : (a + 1) * size].astype(F32) for a in range(side // size) for z in range(ring)],
        axis=0,
    ).astype(BF16)
    spot = lax.broadcasted_iota(jnp.int32, (rows, rows), 0)
    frame = spot // per % 2
    source = frame * (rows // 2) + spot // (2 * per) * per + spot % per
    moved = (lax.broadcasted_iota(jnp.int32, (rows, rows), 1) == source).astype(BF16)
    out_ref[:, :width] = turned(moved, mixed).astype(BF16)
    tokens = tokens_ref[...].reshape(rows, width)
    out_ref[:, width : 2 * width] = jnp.dot(moved, tokens, preferred_element_type=F32).astype(BF16)
    lanes = out_ref.shape[1] - 2 * width
    one, two = levels_ref[0].astype(F32), levels_ref[1].astype(F32)
    out_ref[:, 2 * width :] = jnp.where(frame[:, :lanes] == 0, one, two).astype(BF16)


def bundle(line, size, levels, mixed, tokens):
    ring, side, rows = mixed.shape
    return pl.pallas_call(
        lambda *refs: bundle_kernel(line, size, *refs),
        out_shape=jax.ShapeDtypeStruct((rows, 2 * ring * side + 128), BF16),
        in_specs=[pl.BlockSpec(memory_space=pltpu.SMEM), vspec(), vspec()],
        out_specs=vspec(),
        compiler_params=params(12),
        cost_estimate=pl.CostEstimate(flops=80000000, bytes_accessed=1500000, transcendentals=0),
        name="bundle",
    )(levels, mixed, tokens)


def temporal_kernel(ring, size, per, got_ref, table_hbm, weights_hbm, out_ref, held, table_ref, sems):
    depth, width = held.shape[1:]
    some = 6 // 2
    half = width // 2

    def copy(n):
        part = pl.ds(n * some, some)
        return pltpu.make_async_copy(weights_hbm.at[part], held.at[part], sems.at[n])

    table_copy = pltpu.make_async_copy(table_hbm.at[:, pl.ds(2 * width, 4 * width)], table_ref, sems.at[10])
    for n in (8, 9):
        copy(n).start()
    table_copy.start()
    for n in range(8):
        copy(n).start()
    rows = got_ref.shape[0]

    def matrix(m, s):
        n = 2 * m + s
        copy(n).wait()
        return held[n * some : (n + 1) * some].reshape(half, width)

    branch = jnp.zeros((rows, width), F32)
    for s in range(2):
        branch += jnp.dot(got_ref[:, s * half : (s + 1) * half], matrix(4, s), preferred_element_type=F32)
    level = got_ref[:, 2 * width :].astype(F32)[:, : table_ref.shape[0]]
    column = lax.broadcasted_iota(jnp.int32, level.shape, 1).astype(F32)
    onehot = (level == column).astype(BF16)
    table_copy.wait()

    def mods(n):
        values = table_ref[:, n * width : (n + 1) * width]
        large = values.astype(BF16)
        small = (values - large.astype(F32)).astype(BF16)
        return jnp.dot(onehot, large, preferred_element_type=F32) + jnp.dot(
            onehot, small, preferred_element_type=F32
        )

    x1 = got_ref[:, width : 2 * width].astype(F32) + mods(0) * branch
    hidden = (normalize(x1) * (1.0 + mods(2)) + mods(1)).astype(BF16)

    lane = lax.broadcasted_iota(jnp.int32, (1, half), 1)
    owned = []
    for z in range(ring):
        mask = jnp.zeros((1, half), jnp.bool_)
        for a in range(some):
            low = a * depth + z * size
            mask = mask | ((lane >= low) & (lane < low + size))
        owned.append(mask)
    along = lax.broadcasted_iota(jnp.int32, (ring * rows, rows), 0) % per
    across = lax.broadcasted_iota(jnp.int32, (ring * rows, rows), 1) % per
    same = along == across

    query = [turned(hidden, matrix(0, s)) for s in range(2)]
    keyed = [turned(hidden, matrix(1, s)).astype(BF16) for s in range(2)]
    valued = [turned(hidden, matrix(2, s)).astype(BF16) for s in range(2)]
    branch = jnp.zeros((rows, width), F32)
    for s in range(2):
        spread = jnp.concatenate([jnp.where(m, query[s], 0.0) for m in owned], axis=0).astype(BF16)
        scores = jnp.where(same, FACTOR * turned(spread, keyed[s]), -jnp.inf)
        weights = jnp.exp(scores - jnp.max(scores, axis=-1, keepdims=True))
        total = jnp.sum(weights, axis=-1, keepdims=True)
        mixed = jnp.dot(weights.astype(BF16), valued[s], preferred_element_type=F32) / total
        attended = jnp.zeros((rows, half), F32)
        for z, m in enumerate(owned):
            attended = jnp.where(m, mixed[z * rows : (z + 1) * rows], attended)
        branch += jnp.dot(attended.astype(BF16), matrix(3, s), preferred_element_type=F32)
    y = x1 + mods(3) * branch
    out_ref[...] = jnp.concatenate([y[per:], y[:per]], axis=0).astype(BF16)


def temporal(ring, size, per, got, table, weights):
    _, depth, width = weights.shape
    rows = got.shape[0]
    return pl.pallas_call(
        lambda *refs: temporal_kernel(ring, size, per, *refs),
        out_shape=jax.ShapeDtypeStruct((rows, width), BF16),
        in_specs=[vspec(), pl.BlockSpec(memory_space=pl.ANY), pl.BlockSpec(memory_space=pl.ANY)],
        out_specs=vspec(),
        scratch_shapes=[
            VMEM((30, depth, width), BF16),
            VMEM((table.shape[0], 4 * width), F32),
            pltpu.SemaphoreType.DMA((11,)),
        ],
        compiler_params=params(40),
        cost_estimate=pl.CostEstimate(
            flops=2 * rows * width * width * 5, bytes_accessed=15000000, transcendentals=16 * rows * rows
        ),
        name="temporal",
    )(got, in_hbm(table), in_hbm(weights))


def per_device(
    queue_tokens,
    fresh_frame,
    levels,
    mod_table,
    w_qkv_spatial,
    w_out_spatial,
    w_qkv_temporal,
    w_out_temporal,
):
    _, rows, width = queue_tokens.shape
    ring = lax.axis_size("tok")
    line = lax.axis_size("queue")
    spot = lax.axis_index("queue")
    up = [(i, (i + 1) % ring) for i in range(ring)]
    down = [(i, (i - 1) % ring) for i in range(ring)]

    def send_up(v):
        return lax.ppermute(v, "tok", up)

    def send_down(v):
        return lax.ppermute(v, "tok", down)

    side = w_out_temporal.shape[0]
    size = side // 6
    start = spot * size
    turned_qkv = jnp.swapaxes(w_qkv_temporal, 1, 2).reshape(3 * side, width)

    def rows_from(matrix, first_row):
        at = jnp.clip(start - first_row, 0, matrix.shape[0] - size)
        return lax.dynamic_slice(matrix, (at, 0), (size, width))

    chunk = jnp.where(
        start < 3 * side,
        rows_from(turned_qkv, 0),
        jnp.where(start < 4 * side, rows_from(w_out_temporal, 3 * side), rows_from(w_out_spatial, 4 * side)),
    )
    chunks = lax.all_to_all(
        jnp.broadcast_to(chunk[None], (ring, size, width)), "tok", 0, 0, tiled=True
    )
    weights = lax.all_gather(chunks.reshape(ring * size, width), "queue", axis=0, tiled=False)

    hidden = first(levels, mod_table, queue_tokens)
    frames = [{0: h} for h in hidden]
    reach = ((4, 3), (3, 4))
    for step in range(1, 5):
        for j in range(2):
            if step <= reach[j][0]:
                frames[j][-step] = send_up(frames[j][1 - step])
            if step <= reach[j][1]:
                frames[j][step] = send_down(frames[j][step - 1])
    offsets = [[0, 1, 2, 3, -4, -3, -2, -1], [0, 1, 2, 3, 4, -3, -2, -1]]
    place = lax.axis_index("tok").astype(jnp.int32)[None]
    mixed = spatial(
        offsets,
        place,
        jnp.swapaxes(w_qkv_spatial, 1, 2),
        [frames[j][o] for j in range(2) for o in offsets[j]],
    )
    mixed = lax.all_to_all(mixed, "tok", 0, 0, tiled=True)

    per = rows // line
    sent = bundle(line, size, levels, mixed, queue_tokens)
    got = lax.all_to_all(sent.reshape(line, 2 * per, sent.shape[1]), "queue", 0, 0, tiled=True)
    moved = temporal(ring, size, per, got.reshape(sent.shape), mod_table, weights)
    got = lax.all_to_all(moved.reshape(line, 2 * per, width), "queue", 0, 0, tiled=True)
    got = jnp.transpose(got.reshape(line, 2, per, width), (1, 0, 2, 3)).reshape(2, rows, width)
    tail = jnp.where(spot == line - 1, fresh_frame, got[1])
    return jnp.stack([got[0], tail])


def solution(mesh):
    return jax.shard_map(
        per_device,
        mesh=mesh,
        in_specs=(
            P("queue", "tok", None),
            P("tok", None),
            P("queue"),
            P(),
            P(None, None, "tok"),
            P("tok", None),
            P(None, None, "tok"),
            P("tok", None),
        ),
        out_specs=P("queue", "tok", None),
        check_vma=False,
    )
```

```python
import jax
import jax.numpy as jnp
from jax import lax
from jax.experimental import pallas as pl
from jax.experimental.pallas import tpu as pltpu
from jax.sharding import PartitionSpec as P

HEADS = 16
HDIM = 72
EPS = 1e-06
FACTOR = HDIM ** (-0.5)
BF16 = jnp.bfloat16
F32 = jnp.float32
VMEM = pltpu.VMEM


def params(mib):
    return pltpu.CompilerParams(vmem_limit_bytes=mib * 1024 * 1024)


def vspec():
    return pl.BlockSpec(memory_space=VMEM)


def in_hbm(values):
    return pltpu.with_memory_space_constraint(values, pltpu.HBM)


def normalize(values):
    mean = jnp.mean(values, axis=-1, keepdims=True)
    centered = values - mean
    variance = jnp.mean(centered * centered, axis=-1, keepdims=True)
    return centered * lax.rsqrt(variance + EPS)


def turned(values, matrix):
    return lax.dot_general(values, matrix, (((1,), (1,)), ((), ())), preferred_element_type=F32)


def first_kernel(line, levels_hbm, table_hbm, tokens_hbm, h0_ref, h1_ref, side_ref, table_ref, held, levels_ref, sems):
    _, rows, width = held.shape
    copies = [
        pltpu.make_async_copy(levels_hbm, levels_ref, sems.at[0]),
        pltpu.make_async_copy(tokens_hbm, held, sems.at[1]),
        pltpu.make_async_copy(table_hbm.at[:, pl.ds(0, 2 * width)], table_ref, sems.at[2]),
    ]
    for copy in copies:
        copy.start()
    for copy in copies:
        copy.wait()
    for j, out in enumerate((h0_ref, h1_ref)):
        row = table_ref[pl.ds(levels_ref[j], 1), :]
        values = normalize(held[j].astype(F32))
        out[...] = (values * (1.0 + row[:, width:]) + row[:, :width]).astype(BF16)
    moved, frame = order_matrix(line, 2 * rows)
    tokens = held[...].reshape(2 * rows, width)
    side_ref[:, :width] = jnp.dot(moved, tokens, preferred_element_type=F32).astype(BF16)
    one, two = levels_ref[0].astype(F32), levels_ref[1].astype(F32)
    side_ref[:, width:] = jnp.where(frame == 0, one, two).astype(BF16)


def order_matrix(line, rows):
    per = rows // (2 * line)
    spot = lax.broadcasted_iota(jnp.int32, (rows, rows), 0)
    frame = spot // per % 2
    source = frame * (rows // 2) + spot // (2 * per) * per + spot % per
    moved = (lax.broadcasted_iota(jnp.int32, (rows, rows), 1) == source).astype(BF16)
    return moved, frame


def first(line, levels, table, tokens):
    _, rows, width = tokens.shape
    block = jax.ShapeDtypeStruct((rows, width), BF16)
    return pl.pallas_call(
        lambda *refs: first_kernel(line, *refs),
        out_shape=(block, block, jax.ShapeDtypeStruct((2 * rows, width + 2 * rows), BF16)),
        in_specs=[pl.BlockSpec(memory_space=pl.ANY)] * 3,
        out_specs=(vspec(), vspec(), vspec()),
        scratch_shapes=[
            VMEM((table.shape[0], 2 * width), F32),
            VMEM(tokens.shape, BF16),
            pltpu.SMEM(levels.shape, jnp.int32),
            pltpu.SemaphoreType.DMA((3,)),
        ],
        compiler_params=params(12),
        cost_estimate=pl.CostEstimate(flops=40000000, bytes_accessed=1500000, transcendentals=0),
        name="first",
    )(in_hbm(levels), in_hbm(table), in_hbm(tokens))


def spatial_kernel(offsets, place_ref, w_hbm, *refs):
    *refs, out_ref, w_ref, sem = refs
    copy = pltpu.make_async_copy(w_hbm, w_ref, sem)
    copy.start()
    rows = refs[0].shape[0]
    ring = len(offsets[0])
    copy.wait()
    for j in range(2):
        hidden = jnp.concatenate([ref[...] for ref in refs[j * ring : (j + 1) * ring]], axis=0)
        query = turned(w_ref[0], hidden).astype(BF16)
        keyed = turned(hidden, w_ref[1]).astype(BF16)
        valued = turned(w_ref[2], hidden).astype(BF16)
        heads = []
        for h in range(query.shape[0] // HDIM):
            cut = slice(h * HDIM, (h + 1) * HDIM)
            scores = FACTOR * jnp.dot(keyed[:, cut], query[cut], preferred_element_type=F32)
            weights = jnp.exp(scores - jnp.max(scores, axis=0, keepdims=True))
            total = jnp.sum(weights, axis=0, keepdims=True)
            mixed = jnp.dot(valued[cut], weights.astype(BF16), preferred_element_type=F32)
            heads.append((mixed / total).astype(BF16))
        attended = jnp.concatenate(heads, axis=0)
        for n, offset in enumerate(offsets[j]):
            owner = lax.rem(place_ref[0] + offset + ring, ring)
            out_ref[owner, :, j * rows : (j + 1) * rows] = attended[:, n * rows : (n + 1) * rows]


def spatial(offsets, place, w_qkv, blocks):
    rows, width = blocks[0].shape
    ring = len(offsets[0])
    whole = rows * ring
    return pl.pallas_call(
        lambda *refs: spatial_kernel(offsets, *refs),
        out_shape=jax.ShapeDtypeStruct((ring, w_qkv.shape[1], 2 * rows), BF16),
        in_specs=[pl.BlockSpec(memory_space=pltpu.SMEM), pl.BlockSpec(memory_space=pl.ANY)]
        + [vspec()] * len(blocks),
        out_specs=vspec(),
        scratch_shapes=[VMEM(w_qkv.shape, BF16), pltpu.SemaphoreType.DMA],
        compiler_params=params(20),
        cost_estimate=pl.CostEstimate(
            flops=4 * whole * width * 144 * 3 + 8 * whole * whole * 256,
            bytes_accessed=5000000,
            transcendentals=4 * whole * whole,
        ),
        name="spatial",
    )(place, in_hbm(w_qkv), *blocks)


def bundle_kernel(line, size, mixed_ref, side_ref, out_ref):
    ring, side, rows = mixed_ref.shape
    width = ring * side
    mixed = jnp.concatenate(
        [mixed_ref[z, a * size : (a + 1) * size].astype(F32) for a in range(side // size) for z in range(ring)],
        axis=0,
    ).astype(BF16)
    moved, _ = order_matrix(line, rows)
    out_ref[:, :width] = turned(moved, mixed).astype(BF16)
    out_ref[:, width:] = side_ref[...]


def bundle(line, size, mixed, tokens):
    ring, side, rows = mixed.shape
    return pl.pallas_call(
        lambda *refs: bundle_kernel(line, size, *refs),
        out_shape=jax.ShapeDtypeStruct((rows, ring * side + tokens.shape[1]), BF16),
        in_specs=[vspec(), vspec()],
        out_specs=vspec(),
        compiler_params=params(12),
        cost_estimate=pl.CostEstimate(flops=40000000, bytes_accessed=1500000, transcendentals=0),
        name="bundle",
    )(mixed, tokens)


def temporal_kernel(ring, size, per, got_ref, table_hbm, weights_hbm, out_ref, held, table_ref, sems):
    depth, width = held.shape[1:]
    some = 6 // 2
    half = width // 2

    def copy(n):
        part = pl.ds(n * some, some)
        return pltpu.make_async_copy(weights_hbm.at[part], held.at[part], sems.at[n])

    table_copy = pltpu.make_async_copy(table_hbm.at[:, pl.ds(2 * width, 4 * width)], table_ref, sems.at[10])
    for n in (8, 9):
        copy(n).start()
    table_copy.start()
    for n in range(8):
        copy(n).start()
    rows = got_ref.shape[0]

    def matrix(m, s):
        n = 2 * m + s
        copy(n).wait()
        return held[n * some : (n + 1) * some].reshape(half, width)

    branch = jnp.zeros((rows, width), F32)
    for s in range(2):
        branch += jnp.dot(got_ref[:, s * half : (s + 1) * half], matrix(4, s), preferred_element_type=F32)
    level = got_ref[:, 2 * width :].astype(F32)[:, : table_ref.shape[0]]
    column = lax.broadcasted_iota(jnp.int32, level.shape, 1).astype(F32)
    onehot = (level == column).astype(BF16)
    table_copy.wait()

    def mods(n):
        values = table_ref[:, n * width : (n + 1) * width]
        large = values.astype(BF16)
        small = (values - large.astype(F32)).astype(BF16)
        return jnp.dot(onehot, large, preferred_element_type=F32) + jnp.dot(
            onehot, small, preferred_element_type=F32
        )

    x1 = got_ref[:, width : 2 * width].astype(F32) + mods(0) * branch
    hidden = (normalize(x1) * (1.0 + mods(2)) + mods(1)).astype(BF16)

    lane = lax.broadcasted_iota(jnp.int32, (1, half), 1)
    owned = []
    for z in range(ring):
        mask = jnp.zeros((1, half), jnp.bool_)
        for a in range(some):
            low = a * depth + z * size
            mask = mask | ((lane >= low) & (lane < low + size))
        owned.append(mask)
    along = lax.broadcasted_iota(jnp.int32, (ring * rows, rows), 0) % per
    across = lax.broadcasted_iota(jnp.int32, (ring * rows, rows), 1) % per
    same = along == across

    query = [turned(hidden, matrix(0, s)) for s in range(2)]
    keyed = [turned(hidden, matrix(1, s)).astype(BF16) for s in range(2)]
    valued = [turned(hidden, matrix(2, s)).astype(BF16) for s in range(2)]
    branch = jnp.zeros((rows, width), F32)
    for s in range(2):
        spread = jnp.concatenate([jnp.where(m, query[s], 0.0) for m in owned], axis=0).astype(BF16)
        scores = jnp.where(same, FACTOR * turned(spread, keyed[s]), -jnp.inf)
        weights = jnp.exp(scores - jnp.max(scores, axis=-1, keepdims=True))
        total = jnp.sum(weights, axis=-1, keepdims=True)
        mixed = jnp.dot(weights.astype(BF16), valued[s], preferred_element_type=F32) / total
        attended = jnp.zeros((rows, half), F32)
        for z, m in enumerate(owned):
            attended = jnp.where(m, mixed[z * rows : (z + 1) * rows], attended)
        branch += jnp.dot(attended.astype(BF16), matrix(3, s), preferred_element_type=F32)
    y = x1 + mods(3) * branch
    out_ref[...] = jnp.concatenate([y[per:], y[:per]], axis=0).astype(BF16)


def temporal(ring, size, per, got, table, weights):
    _, depth, width = weights.shape
    rows = got.shape[0]
    return pl.pallas_call(
        lambda *refs: temporal_kernel(ring, size, per, *refs),
        out_shape=jax.ShapeDtypeStruct((rows, width), BF16),
        in_specs=[vspec(), pl.BlockSpec(memory_space=pl.ANY), pl.BlockSpec(memory_space=pl.ANY)],
        out_specs=vspec(),
        scratch_shapes=[
            VMEM((30, depth, width), BF16),
            VMEM((table.shape[0], 4 * width), F32),
            pltpu.SemaphoreType.DMA((11,)),
        ],
        compiler_params=params(40),
        cost_estimate=pl.CostEstimate(
            flops=2 * rows * width * width * 5, bytes_accessed=15000000, transcendentals=16 * rows * rows
        ),
        name="temporal",
    )(got, in_hbm(table), in_hbm(weights))


def per_device(
    queue_tokens,
    fresh_frame,
    levels,
    mod_table,
    w_qkv_spatial,
    w_out_spatial,
    w_qkv_temporal,
    w_out_temporal,
):
    _, rows, width = queue_tokens.shape
    ring = lax.axis_size("tok")
    line = lax.axis_size("queue")
    spot = lax.axis_index("queue")
    up = [(i, (i + 1) % ring) for i in range(ring)]
    down = [(i, (i - 1) % ring) for i in range(ring)]

    def send_up(v):
        return lax.ppermute(v, "tok", up)

    def send_down(v):
        return lax.ppermute(v, "tok", down)

    side = w_out_temporal.shape[0]
    size = side // 6
    start = spot * size
    turned_qkv = jnp.swapaxes(w_qkv_temporal, 1, 2).reshape(3 * side, width)

    def rows_from(matrix, first_row):
        at = jnp.clip(start - first_row, 0, matrix.shape[0] - size)
        return lax.dynamic_slice(matrix, (at, 0), (size, width))

    chunk = jnp.where(
        start < 3 * side,
        rows_from(turned_qkv, 0),
        jnp.where(start < 4 * side, rows_from(w_out_temporal, 3 * side), rows_from(w_out_spatial, 4 * side)),
    )
    chunks = lax.all_to_all(
        jnp.broadcast_to(chunk[None], (ring, size, width)), "tok", 0, 0, tiled=True
    )

    *hidden, side_rows = first(line, levels, mod_table, queue_tokens)
    frames = [{0: h} for h in hidden]
    reach = ((4, 3), (3, 4))
    for step in range(1, 5):
        for j in range(2):
            if step <= reach[j][0]:
                frames[j][-step] = send_up(frames[j][1 - step])
            if step <= reach[j][1]:
                frames[j][step] = send_down(frames[j][step - 1])
    chunks, *_ = lax.optimization_barrier((chunks, *[frames[j][o] for j in range(2) for o in (-1, 1)]))
    weights = lax.all_gather(chunks.reshape(ring * size, width), "queue", axis=0, tiled=False)

    offsets = [[0, 1, 2, 3, -4, -3, -2, -1], [0, 1, 2, 3, 4, -3, -2, -1]]
    place = lax.axis_index("tok").astype(jnp.int32)[None]
    mixed = spatial(
        offsets,
        place,
        jnp.swapaxes(w_qkv_spatial, 1, 2),
        [frames[j][o] for j in range(2) for o in offsets[j]],
    )
    mixed = lax.all_to_all(mixed, "tok", 0, 0, tiled=True)

    per = rows // line
    sent = bundle(line, size, mixed, side_rows)
    got = lax.all_to_all(sent.reshape(line, 2 * per, sent.shape[1]), "queue", 0, 0, tiled=True)
    moved = temporal(ring, size, per, got.reshape(sent.shape), mod_table, weights)
    got = lax.all_to_all(moved.reshape(line, 2 * per, width), "queue", 0, 0, tiled=True)
    got = jnp.transpose(got.reshape(line, 2, per, width), (1, 0, 2, 3)).reshape(2, rows, width)
    tail = jnp.where(spot == line - 1, fresh_frame, got[1])
    return jnp.stack([got[0], tail])


def solution(mesh):
    return jax.shard_map(
        per_device,
        mesh=mesh,
        in_specs=(
            P("queue", "tok", None),
            P("tok", None),
            P("queue"),
            P(),
            P(None, None, "tok"),
            P("tok", None),
            P(None, None, "tok"),
            P("tok", None),
        ),
        out_specs=P("queue", "tok", None),
        check_vma=False,
    )
```

```python
import jax
import jax.numpy as jnp
from jax import lax
from jax.experimental import pallas as pl
from jax.experimental.pallas import tpu as pltpu
from jax.sharding import PartitionSpec as P

HEADS = 16
HDIM = 72
EPS = 1e-06
FACTOR = HDIM ** (-0.5)
BF16 = jnp.bfloat16
F32 = jnp.float32
VMEM = pltpu.VMEM


def params(mib):
    return pltpu.CompilerParams(vmem_limit_bytes=mib * 1024 * 1024)


def vspec():
    return pl.BlockSpec(memory_space=VMEM)


def in_hbm(values):
    return pltpu.with_memory_space_constraint(values, pltpu.HBM)


def normalize(values):
    mean = jnp.mean(values, axis=-1, keepdims=True)
    centered = values - mean
    variance = jnp.mean(centered * centered, axis=-1, keepdims=True)
    return centered * lax.rsqrt(variance + EPS)


def turned(values, matrix):
    return lax.dot_general(values, matrix, (((1,), (1,)), ((), ())), preferred_element_type=F32)


def first_kernel(line, levels_hbm, table_hbm, tokens_hbm, h0_ref, h1_ref, side_ref, table_ref, held, levels_ref, sems):
    _, rows, width = held.shape
    copies = [
        pltpu.make_async_copy(levels_hbm, levels_ref, sems.at[0]),
        pltpu.make_async_copy(tokens_hbm, held, sems.at[1]),
        pltpu.make_async_copy(table_hbm.at[:, pl.ds(0, 2 * width)], table_ref, sems.at[2]),
    ]
    for copy in copies:
        copy.start()
    for copy in copies:
        copy.wait()
    for j, out in enumerate((h0_ref, h1_ref)):
        row = table_ref[pl.ds(levels_ref[j], 1), :]
        values = normalize(held[j].astype(F32))
        out[...] = (values * (1.0 + row[:, width:]) + row[:, :width]).astype(BF16)
    moved, frame = order_matrix(line, 2 * rows)
    tokens = held[...].reshape(2 * rows, width)
    side_ref[:, :width] = jnp.dot(moved, tokens, preferred_element_type=F32).astype(BF16)
    one, two = levels_ref[0].astype(F32), levels_ref[1].astype(F32)
    side_ref[:, width:] = jnp.where(frame == 0, one, two).astype(BF16)


def order_matrix(line, rows):
    per = rows // (2 * line)
    spot = lax.broadcasted_iota(jnp.int32, (rows, rows), 0)
    frame = spot // per % 2
    source = frame * (rows // 2) + spot // (2 * per) * per + spot % per
    moved = (lax.broadcasted_iota(jnp.int32, (rows, rows), 1) == source).astype(BF16)
    return moved, frame


def first(line, levels, table, tokens):
    _, rows, width = tokens.shape
    block = jax.ShapeDtypeStruct((rows, width), BF16)
    return pl.pallas_call(
        lambda *refs: first_kernel(line, *refs),
        out_shape=(block, block, jax.ShapeDtypeStruct((2 * rows, width + 2 * rows), BF16)),
        in_specs=[pl.BlockSpec(memory_space=pl.ANY)] * 3,
        out_specs=(vspec(), vspec(), vspec()),
        scratch_shapes=[
            VMEM((table.shape[0], 2 * width), F32),
            VMEM(tokens.shape, BF16),
            pltpu.SMEM(levels.shape, jnp.int32),
            pltpu.SemaphoreType.DMA((3,)),
        ],
        compiler_params=params(12),
        cost_estimate=pl.CostEstimate(flops=40000000, bytes_accessed=1500000, transcendentals=0),
        name="first",
    )(in_hbm(levels), in_hbm(table), in_hbm(tokens))


def spatial_kernel(offsets, place_ref, w_hbm, *refs):
    *refs, out_ref, w_ref, sem = refs
    copy = pltpu.make_async_copy(w_hbm, w_ref, sem)
    copy.start()
    rows = refs[0].shape[0]
    ring = len(offsets[0])
    for j in range(2):
        hidden = jnp.concatenate([ref[...] for ref in refs[j * ring : (j + 1) * ring]], axis=0)
        if j == 0:
            copy.wait()
        projected = turned(w_ref[...], hidden).astype(BF16)
        side = projected.shape[0] // 3
        heads = []
        for h in range(side // HDIM):
            query, keyed, valued = [
                projected[m * side + h * HDIM : m * side + (h + 1) * HDIM] for m in range(3)
            ]
            scores = FACTOR * lax.dot_general(
                keyed, query, (((0,), (0,)), ((), ())), preferred_element_type=F32
            )
            weights = jnp.exp(scores - jnp.max(scores, axis=0, keepdims=True))
            total = jnp.sum(weights, axis=0, keepdims=True)
            mixed = jnp.dot(valued, weights.astype(BF16), preferred_element_type=F32)
            heads.append((mixed / total).astype(BF16))
        attended = jnp.concatenate(heads, axis=0)
        for n, offset in enumerate(offsets[j]):
            owner = lax.rem(place_ref[0] + offset + ring, ring)
            out_ref[owner, :, j * rows : (j + 1) * rows] = attended[:, n * rows : (n + 1) * rows]


def spatial(offsets, place, w_qkv, blocks):
    rows, width = blocks[0].shape
    ring = len(offsets[0])
    whole = rows * ring
    return pl.pallas_call(
        lambda *refs: spatial_kernel(offsets, *refs),
        out_shape=jax.ShapeDtypeStruct((ring, w_qkv.shape[0] // 3, 2 * rows), BF16),
        in_specs=[pl.BlockSpec(memory_space=pltpu.SMEM), pl.BlockSpec(memory_space=pl.ANY)]
        + [vspec()] * len(blocks),
        out_specs=vspec(),
        scratch_shapes=[VMEM(w_qkv.shape, BF16), pltpu.SemaphoreType.DMA],
        compiler_params=params(20),
        cost_estimate=pl.CostEstimate(
            flops=4 * whole * width * 144 * 3 + 8 * whole * whole * 256,
            bytes_accessed=5000000,
            transcendentals=4 * whole * whole,
        ),
        name="spatial",
    )(place, in_hbm(w_qkv), *blocks)


def bundle_kernel(line, size, mixed_ref, side_ref, out_ref):
    ring, side, rows = mixed_ref.shape
    width = ring * side
    mixed = jnp.concatenate(
        [mixed_ref[z, a * size : (a + 1) * size].astype(F32) for a in range(side // size) for z in range(ring)],
        axis=0,
    ).astype(BF16)
    moved, _ = order_matrix(line, rows)
    out_ref[:, :width] = turned(moved, mixed).astype(BF16)
    out_ref[:, width:] = side_ref[...]


def bundle(line, size, mixed, tokens):
    ring, side, rows = mixed.shape
    return pl.pallas_call(
        lambda *refs: bundle_kernel(line, size, *refs),
        out_shape=jax.ShapeDtypeStruct((rows, ring * side + tokens.shape[1]), BF16),
        in_specs=[vspec(), vspec()],
        out_specs=vspec(),
        compiler_params=params(12),
        cost_estimate=pl.CostEstimate(flops=40000000, bytes_accessed=1500000, transcendentals=0),
        name="bundle",
    )(mixed, tokens)


def temporal_kernel(ring, size, per, got_ref, table_hbm, weights_hbm, out_ref, held, table_ref, sems):
    depth, width = held.shape[1:]
    some = 6 // 2
    half = width // 2

    def copy(n):
        part = pl.ds(n * some, some)
        return pltpu.make_async_copy(weights_hbm.at[part], held.at[part], sems.at[n])

    table_copy = pltpu.make_async_copy(table_hbm.at[:, pl.ds(2 * width, 4 * width)], table_ref, sems.at[10])
    for n in (8, 9):
        copy(n).start()
    table_copy.start()
    for n in range(8):
        copy(n).start()
    rows = got_ref.shape[0]

    def matrix(m, s):
        n = 2 * m + s
        copy(n).wait()
        return held[n * some : (n + 1) * some].reshape(half, width)

    branch = jnp.zeros((rows, width), F32)
    for s in range(2):
        branch += jnp.dot(got_ref[:, s * half : (s + 1) * half], matrix(4, s), preferred_element_type=F32)
    level = got_ref[:, 2 * width :].astype(F32)[:, : table_ref.shape[0]]
    column = lax.broadcasted_iota(jnp.int32, level.shape, 1).astype(F32)
    onehot = (level == column).astype(BF16)
    table_copy.wait()

    def mods(n):
        values = table_ref[:, n * width : (n + 1) * width]
        large = values.astype(BF16)
        small = (values - large.astype(F32)).astype(BF16)
        return jnp.dot(onehot, large, preferred_element_type=F32) + jnp.dot(
            onehot, small, preferred_element_type=F32
        )

    x1 = got_ref[:, width : 2 * width].astype(F32) + mods(0) * branch
    hidden = (normalize(x1) * (1.0 + mods(2)) + mods(1)).astype(BF16)

    row = lax.broadcasted_iota(jnp.int32, (half, 1), 0)
    owner = row // size % ring
    along = lax.broadcasted_iota(jnp.int32, (rows, ring * rows), 0) % per
    across = lax.broadcasted_iota(jnp.int32, (rows, ring * rows), 1) % per
    same = along == across

    query = [turned(matrix(0, s), hidden) for s in range(2)]
    keyed = [turned(hidden, matrix(1, s)).astype(BF16) for s in range(2)]
    valued = [turned(matrix(2, s), hidden).astype(BF16) for s in range(2)]
    branch = jnp.zeros((rows, width), F32)
    for s in range(2):
        spread = jnp.concatenate(
            [jnp.where(owner == z, query[s], 0.0).astype(BF16) for z in range(ring)], axis=1
        )
        scores = FACTOR * jnp.dot(keyed[s], spread, preferred_element_type=F32)
        scores = jnp.where(same, scores, -jnp.inf)
        weights = jnp.exp(scores - jnp.max(scores, axis=0, keepdims=True))
        inverse = 1.0 / jnp.sum(weights, axis=0, keepdims=True)
        mixed = jnp.dot(valued[s], weights.astype(BF16), preferred_element_type=F32)
        attended = jnp.concatenate(
            [
                mixed[a * depth + z * size : a * depth + (z + 1) * size, z * rows : (z + 1) * rows]
                * inverse[:, z * rows : (z + 1) * rows]
                for a in range(some)
                for z in range(ring)
            ],
            axis=0,
        ).astype(BF16)
        branch += lax.dot_general(
            attended, matrix(3, s), (((0,), (0,)), ((), ())), preferred_element_type=F32
        )
    y = x1 + mods(3) * branch
    y = jnp.concatenate([y[per:], y[:per]], axis=0)
    out_ref[...] = y.astype(BF16)


def temporal(ring, size, per, got, table, weights):
    _, depth, width = weights.shape
    rows = got.shape[0]
    return pl.pallas_call(
        lambda *refs: temporal_kernel(ring, size, per, *refs),
        out_shape=jax.ShapeDtypeStruct((rows, width), BF16),
        in_specs=[vspec(), pl.BlockSpec(memory_space=pl.ANY), pl.BlockSpec(memory_space=pl.ANY)],
        out_specs=vspec(),
        scratch_shapes=[
            VMEM((30, depth, width), BF16),
            VMEM((table.shape[0], 4 * width), F32),
            pltpu.SemaphoreType.DMA((11,)),
        ],
        compiler_params=params(40),
        cost_estimate=pl.CostEstimate(
            flops=2 * rows * width * width * 5, bytes_accessed=15000000, transcendentals=16 * rows * rows
        ),
        name="temporal",
    )(got, in_hbm(table), in_hbm(weights))


def last_kernel(line, tail_ref, got_ref, fresh_ref, out_ref):
    rows = fresh_ref.shape[0]
    per = rows // line
    spot = lax.broadcasted_iota(jnp.int32, (2 * rows, 2 * rows), 1)
    source = spot // per % 2 * rows + spot // (2 * per) * per + spot % per
    back = (lax.broadcasted_iota(jnp.int32, (2 * rows, 2 * rows), 0) == source).astype(BF16)
    values = jnp.dot(back, got_ref[...], preferred_element_type=F32).astype(BF16)
    out_ref[0] = values[:rows]

    @pl.when(tail_ref[0] == 0)
    def _():
        out_ref[1] = values[rows:]

    @pl.when(tail_ref[0] != 0)
    def _():
        out_ref[1] = fresh_ref[...]


def last(tail, line, got, fresh):
    rows, width = fresh.shape
    return pl.pallas_call(
        lambda *refs: last_kernel(line, *refs),
        out_shape=jax.ShapeDtypeStruct((2, rows, width), BF16),
        in_specs=[pl.BlockSpec(memory_space=pltpu.SMEM), vspec(), vspec()],
        out_specs=vspec(),
        compiler_params=params(8),
        cost_estimate=pl.CostEstimate(flops=40000000, bytes_accessed=1000000, transcendentals=0),
        name="last",
    )(tail, got, fresh)


def per_device(
    queue_tokens,
    fresh_frame,
    levels,
    mod_table,
    w_qkv_spatial,
    w_out_spatial,
    w_qkv_temporal,
    w_out_temporal,
):
    _, rows, width = queue_tokens.shape
    ring = lax.axis_size("tok")
    line = lax.axis_size("queue")
    spot = lax.axis_index("queue")
    up = [(i, (i + 1) % ring) for i in range(ring)]
    down = [(i, (i - 1) % ring) for i in range(ring)]

    def send_up(v):
        return lax.ppermute(v, "tok", up)

    def send_down(v):
        return lax.ppermute(v, "tok", down)

    side = w_out_temporal.shape[0]
    size = side // 6
    start = spot * size
    turned_qkv = jnp.swapaxes(w_qkv_temporal, 1, 2).reshape(3 * side, width)

    def rows_from(matrix, first_row):
        at = jnp.clip(start - first_row, 0, matrix.shape[0] - size)
        return lax.dynamic_slice(matrix, (at, 0), (size, width))

    chunk = jnp.where(
        start < 3 * side,
        rows_from(turned_qkv, 0),
        jnp.where(start < 4 * side, rows_from(w_out_temporal, 3 * side), rows_from(w_out_spatial, 4 * side)),
    )
    chunks = lax.all_to_all(
        jnp.broadcast_to(chunk[None], (ring, size, width)), "tok", 0, 0, tiled=True
    )

    *hidden, side_rows = first(line, levels, mod_table, queue_tokens)
    tail = (spot == line - 1).astype(jnp.int32)[None]
    hidden[0], tail = lax.optimization_barrier((hidden[0], tail))
    frames = [{0: h} for h in hidden]
    reach = ((4, 3), (3, 4))
    for step in range(1, 5):
        for j in range(2):
            if step <= reach[j][0]:
                frames[j][-step] = send_up(frames[j][1 - step])
            if step <= reach[j][1]:
                frames[j][step] = send_down(frames[j][step - 1])
    weights = lax.all_gather(chunks.reshape(ring * size, width), "queue", axis=0, tiled=False)

    offsets = [[0, 1, 2, 3, -4, -3, -2, -1], [0, 1, 2, 3, 4, -3, -2, -1]]
    place = lax.axis_index("tok").astype(jnp.int32)[None]
    mixed = spatial(
        offsets,
        place,
        jnp.swapaxes(w_qkv_spatial, 1, 2).reshape(3 * side, width),
        [frames[j][o] for j in range(2) for o in offsets[j]],
    )
    mixed = lax.all_to_all(mixed, "tok", 0, 0, tiled=True)

    per = rows // line
    sent = bundle(line, size, mixed, side_rows)
    got = lax.all_to_all(sent.reshape(line, 2 * per, sent.shape[1]), "queue", 0, 0, tiled=True)
    moved = temporal(ring, size, per, got.reshape(sent.shape), mod_table, weights)
    got = lax.all_to_all(moved.reshape(line, 2 * per, width), "queue", 0, 0, tiled=True)
    return last(tail, line, got.reshape(2 * rows, width), fresh_frame)


def solution(mesh):
    return jax.shard_map(
        per_device,
        mesh=mesh,
        in_specs=(
            P("queue", "tok", None),
            P("tok", None),
            P("queue"),
            P(),
            P(None, None, "tok"),
            P("tok", None),
            P(None, None, "tok"),
            P("tok", None),
        ),
        out_specs=P("queue", "tok", None),
        check_vma=False,
    )
```

```python
import jax
import jax.numpy as jnp
from jax import lax
from jax.experimental import pallas as pl
from jax.experimental.pallas import tpu as pltpu
from jax.sharding import PartitionSpec as P

HEADS = 16
HDIM = 72
EPS = 1e-06
FACTOR = HDIM ** (-0.5)
BF16 = jnp.bfloat16
F32 = jnp.float32
VMEM = pltpu.VMEM


def params(mib):
    return pltpu.CompilerParams(vmem_limit_bytes=mib * 1024 * 1024)


def vspec():
    return pl.BlockSpec(memory_space=VMEM)


def in_hbm(values):
    return pltpu.with_memory_space_constraint(values, pltpu.HBM)


def normalize(values):
    mean = jnp.mean(values, axis=-1, keepdims=True)
    centered = values - mean
    variance = jnp.mean(centered * centered, axis=-1, keepdims=True)
    return centered * lax.rsqrt(variance + EPS)


def turned(values, matrix):
    return lax.dot_general(values, matrix, (((1,), (1,)), ((), ())), preferred_element_type=F32)


def first_kernel(line, levels_hbm, table_hbm, tokens_hbm, h0_ref, h1_ref, side_ref, table_ref, held, levels_ref, sems):
    _, rows, width = held.shape
    copies = [
        pltpu.make_async_copy(levels_hbm, levels_ref, sems.at[0]),
        pltpu.make_async_copy(tokens_hbm, held, sems.at[1]),
        pltpu.make_async_copy(table_hbm.at[:, pl.ds(0, 2 * width)], table_ref, sems.at[2]),
    ]
    for copy in copies:
        copy.start()
    for copy in copies:
        copy.wait()
    for j, out in enumerate((h0_ref, h1_ref)):
        row = table_ref[pl.ds(levels_ref[j], 1), :]
        values = normalize(held[j].astype(F32))
        out[...] = (values * (1.0 + row[:, width:]) + row[:, :width]).astype(BF16)
    moved, frame = order_matrix(line, 2 * rows)
    tokens = held[...].reshape(2 * rows, width)
    side_ref[:, :width] = jnp.dot(moved, tokens, preferred_element_type=F32).astype(BF16)
    one, two = levels_ref[0].astype(F32), levels_ref[1].astype(F32)
    side_ref[:, width:] = jnp.where(frame == 0, one, two).astype(BF16)


def order_matrix(line, rows):
    per = rows // (2 * line)
    spot = lax.broadcasted_iota(jnp.int32, (rows, rows), 0)
    frame = spot // per % 2
    source = frame * (rows // 2) + spot // (2 * per) * per + spot % per
    moved = (lax.broadcasted_iota(jnp.int32, (rows, rows), 1) == source).astype(BF16)
    return moved, frame


def first(line, levels, table, tokens):
    _, rows, width = tokens.shape
    block = jax.ShapeDtypeStruct((rows, width), BF16)
    return pl.pallas_call(
        lambda *refs: first_kernel(line, *refs),
        out_shape=(block, block, jax.ShapeDtypeStruct((2 * rows, width + 2 * rows), BF16)),
        in_specs=[pl.BlockSpec(memory_space=pl.ANY)] * 3,
        out_specs=(vspec(), vspec(), vspec()),
        scratch_shapes=[
            VMEM((table.shape[0], 2 * width), F32),
            VMEM(tokens.shape, BF16),
            pltpu.SMEM(levels.shape, jnp.int32),
            pltpu.SemaphoreType.DMA((3,)),
        ],
        compiler_params=params(12),
        cost_estimate=pl.CostEstimate(flops=40000000, bytes_accessed=1500000, transcendentals=0),
        name="first",
    )(in_hbm(levels), in_hbm(table), in_hbm(tokens))


def others_kernel(place_ref, chunks_ref, out_ref):
    ring, size, width = chunks_ref.shape
    pieces = [chunks_ref[lax.rem(place_ref[0] + offset, ring)].astype(F32) for offset in range(1, ring)]
    spare = out_ref.shape[0] - (ring - 1) * size
    out_ref[...] = jnp.concatenate(pieces + [jnp.zeros((spare, width), F32)], axis=0).astype(BF16)


def others(place, chunks, rows):
    return pl.pallas_call(
        others_kernel,
        out_shape=jax.ShapeDtypeStruct((rows, chunks.shape[2]), BF16),
        in_specs=[pl.BlockSpec(memory_space=pltpu.SMEM), vspec()],
        out_specs=vspec(),
        compiler_params=params(8),
        cost_estimate=pl.CostEstimate(flops=0, bytes_accessed=900000, transcendentals=0),
        name="others",
    )(place, chunks)


def spatial_kernel(offsets, place_ref, w_hbm, *refs):
    *refs, out_ref, w_ref, sem = refs
    copy = pltpu.make_async_copy(w_hbm, w_ref, sem)
    copy.start()
    rows = refs[0].shape[0]
    ring = len(offsets[0])
    for j in range(2):
        hidden = jnp.concatenate([ref[...] for ref in refs[j * ring : (j + 1) * ring]], axis=0)
        if j == 0:
            copy.wait()
        projected = turned(w_ref[...], hidden).astype(BF16)
        side = projected.shape[0] // 3
        heads = []
        for h in range(side // HDIM):
            query, keyed, valued = [
                projected[m * side + h * HDIM : m * side + (h + 1) * HDIM] for m in range(3)
            ]
            scores = FACTOR * lax.dot_general(
                keyed, query, (((0,), (0,)), ((), ())), preferred_element_type=F32
            )
            weights = jnp.exp(scores - jnp.max(scores, axis=0, keepdims=True))
            total = jnp.sum(weights, axis=0, keepdims=True)
            mixed = jnp.dot(valued, weights.astype(BF16), preferred_element_type=F32)
            heads.append((mixed / total).astype(BF16))
        attended = jnp.concatenate(heads, axis=0)
        for n, offset in enumerate(offsets[j]):
            owner = lax.rem(place_ref[0] + offset + ring, ring)
            out_ref[owner, :, j * rows : (j + 1) * rows] = attended[:, n * rows : (n + 1) * rows]


def spatial(offsets, place, w_qkv, blocks):
    rows, width = blocks[0].shape
    ring = len(offsets[0])
    whole = rows * ring
    return pl.pallas_call(
        lambda *refs: spatial_kernel(offsets, *refs),
        out_shape=jax.ShapeDtypeStruct((ring, w_qkv.shape[0] // 3, 2 * rows), BF16),
        in_specs=[pl.BlockSpec(memory_space=pltpu.SMEM), pl.BlockSpec(memory_space=pl.ANY)]
        + [vspec()] * len(blocks),
        out_specs=vspec(),
        scratch_shapes=[VMEM(w_qkv.shape, BF16), pltpu.SemaphoreType.DMA],
        compiler_params=params(20),
        cost_estimate=pl.CostEstimate(
            flops=4 * whole * width * 144 * 3 + 8 * whole * whole * 256,
            bytes_accessed=5000000,
            transcendentals=4 * whole * whole,
        ),
        name="spatial",
    )(place, in_hbm(w_qkv), *blocks)


def bundle_kernel(line, size, group, place_ref, mixed_ref, side_ref, out_ref):
    ring, side, rows = mixed_ref.shape
    width = ring * side
    pieces = []
    for s in range(2):
        for k in range(3 * s, 3 * s + 3):
            for offset in range(1, ring):
                z = lax.rem(place_ref[0] + offset, ring)
                pieces.append(mixed_ref[z, k * size : (k + 1) * size].astype(F32))
            pieces.append(jnp.zeros((group - (ring - 1) * size, rows), F32))
        if s == 0:
            pieces.append(mixed_ref[place_ref[0]].astype(F32))
    mixed = jnp.concatenate(pieces, axis=0).astype(BF16)
    moved, _ = order_matrix(line, rows)
    end = width + mixed.shape[0]
    out_ref[:, :width] = side_ref[:, :width]
    out_ref[:, width:end] = turned(moved, mixed).astype(BF16)
    out_ref[:, end:] = side_ref[:, width : width + out_ref.shape[1] - end]


def bundle(line, size, group, place, mixed, tokens):
    ring, side, rows = mixed.shape
    whole = ring * side + 6 * group + side
    lanes = -(-(whole + 64) // 128) * 128
    return pl.pallas_call(
        lambda *refs: bundle_kernel(line, size, group, *refs),
        out_shape=jax.ShapeDtypeStruct((rows, lanes), BF16),
        in_specs=[pl.BlockSpec(memory_space=pltpu.SMEM), vspec(), vspec()],
        out_specs=vspec(),
        compiler_params=params(12),
        cost_estimate=pl.CostEstimate(flops=40000000, bytes_accessed=1500000, transcendentals=0),
        name="bundle",
    )(place, mixed, tokens)


def temporal_kernel(
    size, per, got_ref, table_hbm, own_qkv, own_temporal, own_spatial, weights_hbm, out_ref, one_ref, two_ref, table_ref, sems
):
    group, width = weights_hbm.shape[1:]
    side = own_temporal.shape[0]
    ring = width // side
    held = (one_ref, two_ref)
    gathered = 3 * group

    def start(m, s):
        for k in range(3):
            pltpu.make_async_copy(
                weights_hbm.at[6 * m + 3 * s + k], held[s].at[m, pl.ds(k * group, group)], sems.at[2 * m + s]
            ).start()
        if s == 0:
            own = own_qkv.at[m] if m < 3 else (own_temporal, own_spatial)[m - 3]
            pltpu.make_async_copy(own, one_ref.at[m, pl.ds(gathered, side)], sems.at[2 * m]).start()

    table_copy = pltpu.make_async_copy(table_hbm.at[:, pl.ds(2 * width, 4 * width)], table_ref, sems.at[10])
    table_copy.start()
    for m, s in ((4, 0), (4, 1), (0, 0), (1, 0), (2, 0), (3, 0), (0, 1), (1, 1), (2, 1), (3, 1)):
        start(m, s)
    rows = got_ref.shape[0]

    def matrix(m, s):
        pltpu.make_async_copy(held[s].at[m], held[s].at[m], sems.at[2 * m + s]).wait()
        return held[s][m]

    split = width + gathered + side
    end = split + gathered
    level = got_ref[:, end : end + table_ref.shape[0]].astype(F32)
    column = lax.broadcasted_iota(jnp.int32, level.shape, 1).astype(F32)
    onehot = (level == column).astype(BF16)
    table_copy.wait()

    def mods(n):
        values = table_ref[:, n * width : (n + 1) * width]
        large = values.astype(BF16)
        small = (values - large.astype(F32)).astype(BF16)
        return jnp.dot(onehot, large, preferred_element_type=F32) + jnp.dot(
            onehot, small, preferred_element_type=F32
        )

    gate1, shift2, scale2, gate2 = [mods(n) for n in range(4)]
    branch = jnp.dot(got_ref[:, width:split], matrix(4, 0), preferred_element_type=F32)
    branch += jnp.dot(got_ref[:, split:end], matrix(4, 1), preferred_element_type=F32)
    x1 = got_ref[:, :width].astype(F32) + gate1 * branch
    hidden = (normalize(x1) * (1.0 + scale2) + shift2).astype(BF16)

    branch = jnp.zeros((rows, width), F32)
    for s in range(2):
        heads = ring + 1 if s == 0 else ring - 1
        query = turned(matrix(0, s), hidden)
        keyed = turned(hidden, matrix(1, s)).astype(BF16)
        valued = turned(matrix(2, s), hidden).astype(BF16)
        row = lax.broadcasted_iota(jnp.int32, (query.shape[0], 1), 0)
        inside = row % group
        owner = jnp.where(inside < (ring - 1) * size, inside // size, -1)
        owner = jnp.where(row >= gathered, ring - 1 + (row - gathered) // HDIM, owner)
        along = lax.broadcasted_iota(jnp.int32, (rows, heads * rows), 0) % per
        across = lax.broadcasted_iota(jnp.int32, (rows, heads * rows), 1) % per
        spread = jnp.concatenate(
            [jnp.where(owner == h, query, 0.0).astype(BF16) for h in range(heads)], axis=1
        )
        scores = FACTOR * jnp.dot(keyed, spread, preferred_element_type=F32)
        scores = jnp.where(along == across, scores, -jnp.inf)
        weights = jnp.exp(scores - jnp.max(scores, axis=0, keepdims=True))
        inverse = 1.0 / jnp.sum(weights, axis=0, keepdims=True)
        mixed = jnp.dot(valued, weights.astype(BF16), preferred_element_type=F32)

        def piece(first_row, count, h):
            columns = slice(h * rows, (h + 1) * rows)
            return mixed[first_row : first_row + count, columns] * inverse[:, columns]

        pieces = []
        for k in range(3):
            pieces += [piece(k * group + h * size, size, h) for h in range(ring - 1)]
            pieces.append(jnp.zeros((group - (ring - 1) * size, rows), F32))
        pieces += [piece(gathered + (h - ring + 1) * HDIM, HDIM, h) for h in range(ring - 1, heads)]
        attended = jnp.concatenate(pieces, axis=0).astype(BF16)
        branch += lax.dot_general(
            attended, matrix(3, s), (((0,), (0,)), ((), ())), preferred_element_type=F32
        )
    y = x1 + gate2 * branch
    y = jnp.concatenate([y[per:], y[:per]], axis=0)
    out_ref[...] = y.astype(BF16)


def temporal(size, per, got, table, own, weights):
    group, width = weights.shape[1:]
    side = own[1].shape[0]
    rows = got.shape[0]
    return pl.pallas_call(
        lambda *refs: temporal_kernel(size, per, *refs),
        out_shape=jax.ShapeDtypeStruct((rows, width), BF16),
        in_specs=[vspec()] + [pl.BlockSpec(memory_space=pl.ANY)] * 5,
        out_specs=vspec(),
        scratch_shapes=[
            VMEM((5, 3 * group + side, width), BF16),
            VMEM((5, 3 * group, width), BF16),
            VMEM((table.shape[0], 4 * width), F32),
            pltpu.SemaphoreType.DMA((11,)),
        ],
        compiler_params=params(40),
        cost_estimate=pl.CostEstimate(
            flops=2 * rows * width * width * 5, bytes_accessed=15000000, transcendentals=16 * rows * rows
        ),
        name="temporal",
    )(got, in_hbm(table), *[in_hbm(v) for v in own], in_hbm(weights))


def last_kernel(line, tail_ref, got_ref, fresh_ref, out_ref):
    rows = fresh_ref.shape[0]
    per = rows // line
    spot = lax.broadcasted_iota(jnp.int32, (2 * rows, 2 * rows), 1)
    source = spot // per % 2 * rows + spot // (2 * per) * per + spot % per
    back = (lax.broadcasted_iota(jnp.int32, (2 * rows, 2 * rows), 0) == source).astype(BF16)
    values = jnp.dot(back, got_ref[...], preferred_element_type=F32).astype(BF16)
    out_ref[0] = values[:rows]

    @pl.when(tail_ref[0] == 0)
    def _():
        out_ref[1] = values[rows:]

    @pl.when(tail_ref[0] != 0)
    def _():
        out_ref[1] = fresh_ref[...]


def last(tail, line, got, fresh):
    rows, width = fresh.shape
    return pl.pallas_call(
        lambda *refs: last_kernel(line, *refs),
        out_shape=jax.ShapeDtypeStruct((2, rows, width), BF16),
        in_specs=[pl.BlockSpec(memory_space=pltpu.SMEM), vspec(), vspec()],
        out_specs=vspec(),
        compiler_params=params(8),
        cost_estimate=pl.CostEstimate(flops=40000000, bytes_accessed=1000000, transcendentals=0),
        name="last",
    )(tail, got, fresh)


def per_device(
    queue_tokens,
    fresh_frame,
    levels,
    mod_table,
    w_qkv_spatial,
    w_out_spatial,
    w_qkv_temporal,
    w_out_temporal,
):
    _, rows, width = queue_tokens.shape
    ring = lax.axis_size("tok")
    line = lax.axis_size("queue")
    spot = lax.axis_index("queue")
    up = [(i, (i + 1) % ring) for i in range(ring)]
    down = [(i, (i - 1) % ring) for i in range(ring)]

    def send_up(v):
        return lax.ppermute(v, "tok", up)

    def send_down(v):
        return lax.ppermute(v, "tok", down)

    side = w_out_temporal.shape[0]
    size = side // 6
    start = spot * size
    turned_qkv = jnp.swapaxes(w_qkv_temporal, 1, 2).reshape(3 * side, width)

    def rows_from(matrix, first_row):
        at = jnp.clip(start - first_row, 0, matrix.shape[0] - size)
        return lax.dynamic_slice(matrix, (at, 0), (size, width))

    chunk = jnp.where(
        start < 3 * side,
        rows_from(turned_qkv, 0),
        jnp.where(start < 4 * side, rows_from(w_out_temporal, 3 * side), rows_from(w_out_spatial, 4 * side)),
    )
    place = lax.axis_index("tok").astype(jnp.int32)[None]
    tail = (spot == line - 1).astype(jnp.int32)[None]
    chunk, place, tail = lax.optimization_barrier((chunk, place, tail))
    chunks = lax.all_to_all(
        jnp.broadcast_to(chunk[None], (ring, size, width)), "tok", 0, 0, tiled=True
    )

    *hidden, side_rows = first(line, levels, mod_table, queue_tokens)
    frames = [{0: h} for h in hidden]
    reach = ((4, 3), (3, 4))
    for step in range(1, 5):
        for j in range(2):
            if step <= reach[j][0]:
                frames[j][-step] = send_up(frames[j][1 - step])
            if step <= reach[j][1]:
                frames[j][step] = send_down(frames[j][step - 1])
    group = -(-(ring - 1) * size // 16) * 16
    weights = lax.all_gather(others(place, chunks, group), "queue", axis=0, tiled=False)

    offsets = [[0, 1, 2, 3, -4, -3, -2, -1], [0, 1, 2, 3, 4, -3, -2, -1]]
    mixed = spatial(
        offsets,
        place,
        jnp.swapaxes(w_qkv_spatial, 1, 2).reshape(3 * side, width),
        [frames[j][o] for j in range(2) for o in offsets[j]],
    )
    mixed = lax.all_to_all(mixed, "tok", 0, 0, tiled=True)

    per = rows // line
    sent = bundle(line, size, group, place, mixed, side_rows)
    got = lax.all_to_all(sent.reshape(line, 2 * per, sent.shape[1]), "queue", 0, 0, tiled=True)
    own = (turned_qkv.reshape(3, side, width), w_out_temporal, w_out_spatial)
    moved = temporal(size, per, got.reshape(sent.shape), mod_table, own, weights)
    got = lax.all_to_all(moved.reshape(line, 2 * per, width), "queue", 0, 0, tiled=True)
    return last(tail, line, got.reshape(2 * rows, width), fresh_frame)


def solution(mesh):
    return jax.shard_map(
        per_device,
        mesh=mesh,
        in_specs=(
            P("queue", "tok", None),
            P("tok", None),
            P("queue"),
            P(),
            P(None, None, "tok"),
            P("tok", None),
            P(None, None, "tok"),
            P("tok", None),
        ),
        out_specs=P("queue", "tok", None),
        check_vma=False,
    )
```

```python
import jax
import jax.numpy as jnp
from jax import lax
from jax.experimental import pallas as pl
from jax.experimental.pallas import tpu as pltpu
from jax.sharding import PartitionSpec as P

HEADS = 16
HDIM = 72
EPS = 1e-06
FACTOR = HDIM ** (-0.5) * 1.4426950408889634
BF16 = jnp.bfloat16
F32 = jnp.float32
VMEM = pltpu.VMEM


def params(mib):
    return pltpu.CompilerParams(vmem_limit_bytes=mib * 1024 * 1024)


def vspec():
    return pl.BlockSpec(memory_space=VMEM)


def in_hbm(values):
    return pltpu.with_memory_space_constraint(values, pltpu.HBM)


def normalize(values):
    mean = jnp.mean(values, axis=-1, keepdims=True)
    centered = values - mean
    variance = jnp.mean(centered * centered, axis=-1, keepdims=True)
    return centered * lax.rsqrt(variance + EPS)


def turned(values, matrix):
    return lax.dot_general(values, matrix, (((1,), (1,)), ((), ())), preferred_element_type=F32)


def first_kernel(line, levels_hbm, table_hbm, tokens_hbm, h0_ref, h1_ref, side_ref, table_ref, held, levels_ref, sems):
    _, rows, width = held.shape
    copies = [
        pltpu.make_async_copy(levels_hbm, levels_ref, sems.at[0]),
        pltpu.make_async_copy(tokens_hbm, held, sems.at[1]),
        pltpu.make_async_copy(table_hbm.at[:, pl.ds(0, 2 * width)], table_ref, sems.at[2]),
    ]
    for copy in copies:
        copy.start()
    for copy in copies:
        copy.wait()
    for j, out in enumerate((h0_ref, h1_ref)):
        row = table_ref[pl.ds(levels_ref[j], 1), :]
        values = normalize(held[j].astype(F32))
        out[...] = (values * (1.0 + row[:, width:]) + row[:, :width]).astype(BF16)
    moved, frame = order_matrix(line, 2 * rows)
    tokens = held[...].reshape(2 * rows, width)
    side_ref[:, :width] = jnp.dot(moved, tokens, preferred_element_type=F32).astype(BF16)
    one, two = levels_ref[0].astype(F32), levels_ref[1].astype(F32)
    side_ref[:, width:] = jnp.where(frame == 0, one, two).astype(BF16)


def order_matrix(line, rows):
    per = rows // (2 * line)
    spot = lax.broadcasted_iota(jnp.int32, (rows, rows), 0)
    frame = spot // per % 2
    source = frame * (rows // 2) + spot // (2 * per) * per + spot % per
    moved = (lax.broadcasted_iota(jnp.int32, (rows, rows), 1) == source).astype(BF16)
    return moved, frame


def first(line, levels, table, tokens):
    _, rows, width = tokens.shape
    block = jax.ShapeDtypeStruct((rows, width), BF16)
    return pl.pallas_call(
        lambda *refs: first_kernel(line, *refs),
        out_shape=(block, block, jax.ShapeDtypeStruct((2 * rows, width + 2 * rows), BF16)),
        in_specs=[pl.BlockSpec(memory_space=pl.ANY)] * 3,
        out_specs=(vspec(), vspec(), vspec()),
        scratch_shapes=[
            VMEM((table.shape[0], 2 * width), F32),
            VMEM(tokens.shape, BF16),
            pltpu.SMEM(levels.shape, jnp.int32),
            pltpu.SemaphoreType.DMA((3,)),
        ],
        compiler_params=params(12),
        cost_estimate=pl.CostEstimate(flops=40000000, bytes_accessed=1500000, transcendentals=0),
        name="first",
    )(in_hbm(levels), in_hbm(table), in_hbm(tokens))


def others_kernel(place_ref, chunks_ref, out_ref):
    ring, size, width = chunks_ref.shape
    pieces = [chunks_ref[lax.rem(place_ref[0] + offset, ring)].astype(F32) for offset in range(1, ring)]
    spare = out_ref.shape[0] - (ring - 1) * size
    out_ref[...] = jnp.concatenate(pieces + [jnp.zeros((spare, width), F32)], axis=0).astype(BF16)


def others(place, chunks, rows):
    return pl.pallas_call(
        others_kernel,
        out_shape=jax.ShapeDtypeStruct((rows, chunks.shape[2]), BF16),
        in_specs=[pl.BlockSpec(memory_space=pltpu.SMEM), vspec()],
        out_specs=vspec(),
        compiler_params=params(8),
        cost_estimate=pl.CostEstimate(flops=0, bytes_accessed=900000, transcendentals=0),
        name="others",
    )(place, chunks)


def spatial_kernel(offsets, place_ref, w_hbm, *refs):
    *refs, out_ref, w_ref, sem = refs
    copy = pltpu.make_async_copy(w_hbm, w_ref, sem)
    copy.start()
    rows = refs[0].shape[0]
    ring = len(offsets[0])
    for j in range(2):
        hidden = jnp.concatenate([ref[...] for ref in refs[j * ring : (j + 1) * ring]], axis=0)
        if j == 0:
            copy.wait()
        projected = turned(w_ref[...], hidden)
        side = projected.shape[0] // 3
        projected = jnp.concatenate([FACTOR * projected[:side], projected[side:]], axis=0).astype(BF16)
        heads = []
        for h in range(side // HDIM):
            query, keyed, valued = [
                projected[m * side + h * HDIM : m * side + (h + 1) * HDIM] for m in range(3)
            ]
            scores = lax.dot_general(
                keyed, query, (((0,), (0,)), ((), ())), preferred_element_type=F32
            )
            weights = jnp.exp2(scores - jnp.max(scores, axis=0, keepdims=True))
            total = jnp.sum(weights, axis=0, keepdims=True)
            mixed = jnp.dot(valued, weights.astype(BF16), preferred_element_type=F32)
            heads.append((mixed / total).astype(BF16))
        attended = jnp.concatenate(heads, axis=0)
        for n, offset in enumerate(offsets[j]):
            owner = lax.rem(place_ref[0] + offset + ring, ring)
            out_ref[owner, :, j * rows : (j + 1) * rows] = attended[:, n * rows : (n + 1) * rows]


def spatial(offsets, place, w_qkv, blocks):
    rows, width = blocks[0].shape
    ring = len(offsets[0])
    whole = rows * ring
    return pl.pallas_call(
        lambda *refs: spatial_kernel(offsets, *refs),
        out_shape=jax.ShapeDtypeStruct((ring, w_qkv.shape[0] // 3, 2 * rows), BF16),
        in_specs=[pl.BlockSpec(memory_space=pltpu.SMEM), pl.BlockSpec(memory_space=pl.ANY)]
        + [vspec()] * len(blocks),
        out_specs=vspec(),
        scratch_shapes=[VMEM(w_qkv.shape, BF16), pltpu.SemaphoreType.DMA],
        compiler_params=params(20),
        cost_estimate=pl.CostEstimate(
            flops=4 * whole * width * 144 * 3 + 8 * whole * whole * 256,
            bytes_accessed=5000000,
            transcendentals=4 * whole * whole,
        ),
        name="spatial",
    )(place, in_hbm(w_qkv), *blocks)


def bundle_kernel(line, size, group, place_ref, mixed_ref, side_ref, out_ref):
    ring, side, rows = mixed_ref.shape
    width = ring * side
    parts = [mixed_ref[lax.rem(place_ref[0] + offset, ring)].astype(F32) for offset in range(ring)]
    pieces = []
    for s in range(2):
        for k in range(3 * s, 3 * s + 3):
            pieces += [parts[offset][k * size : (k + 1) * size] for offset in range(1, ring)]
            pieces.append(jnp.zeros((group - (ring - 1) * size, rows), F32))
        if s == 0:
            pieces.append(parts[0])
    mixed = jnp.concatenate(pieces, axis=0).astype(BF16)
    moved, _ = order_matrix(line, rows)
    end = width + mixed.shape[0]
    out_ref[:, :width] = side_ref[:, :width]
    out_ref[:, width:end] = turned(moved, mixed).astype(BF16)
    out_ref[:, end:] = side_ref[:, width : width + out_ref.shape[1] - end]


def bundle(line, size, group, place, mixed, tokens):
    ring, side, rows = mixed.shape
    whole = ring * side + 6 * group + side
    lanes = -(-(whole + 64) // 128) * 128
    return pl.pallas_call(
        lambda *refs: bundle_kernel(line, size, group, *refs),
        out_shape=jax.ShapeDtypeStruct((rows, lanes), BF16),
        in_specs=[pl.BlockSpec(memory_space=pltpu.SMEM), vspec(), vspec()],
        out_specs=vspec(),
        compiler_params=params(12),
        cost_estimate=pl.CostEstimate(flops=40000000, bytes_accessed=1500000, transcendentals=0),
        name="bundle",
    )(place, mixed, tokens)


def temporal_kernel(
    size, per, got_ref, table_hbm, own_qkv, own_temporal, own_spatial, weights_hbm, out_ref, one_ref, two_ref, table_ref, sems
):
    group, width = weights_hbm.shape[1:]
    side = own_temporal.shape[0]
    ring = width // side
    held = (one_ref, two_ref)
    gathered = 3 * group

    def start(m, s):
        for k in range(3):
            pltpu.make_async_copy(
                weights_hbm.at[6 * m + 3 * s + k], held[s].at[m, pl.ds(k * group, group)], sems.at[2 * m + s]
            ).start()
        if s == 0:
            own = own_qkv.at[m] if m < 3 else (own_temporal, own_spatial)[m - 3]
            pltpu.make_async_copy(own, one_ref.at[m, pl.ds(gathered, side)], sems.at[2 * m]).start()

    table_copy = pltpu.make_async_copy(table_hbm.at[:, pl.ds(2 * width, 4 * width)], table_ref, sems.at[10])
    table_copy.start()
    for m, s in ((4, 0), (4, 1), (0, 0), (1, 0), (2, 0), (3, 0), (0, 1), (1, 1), (2, 1), (3, 1)):
        start(m, s)
    rows = got_ref.shape[0]

    def matrix(m, s):
        pltpu.make_async_copy(held[s].at[m], held[s].at[m], sems.at[2 * m + s]).wait()
        return held[s][m]

    split = width + gathered + side
    end = split + gathered
    level = got_ref[:, end : end + table_ref.shape[0]].astype(F32)
    column = lax.broadcasted_iota(jnp.int32, level.shape, 1).astype(F32)
    onehot = (level == column).astype(BF16)
    table_copy.wait()

    def mods(n):
        values = table_ref[:, n * width : (n + 1) * width]
        large = values.astype(BF16)
        small = (values - large.astype(F32)).astype(BF16)
        return jnp.dot(onehot, large, preferred_element_type=F32) + jnp.dot(
            onehot, small, preferred_element_type=F32
        )

    gate1, shift2, scale2, gate2 = [mods(n) for n in range(4)]
    branch = jnp.dot(got_ref[:, width:split], matrix(4, 0), preferred_element_type=F32)
    branch += jnp.dot(got_ref[:, split:end], matrix(4, 1), preferred_element_type=F32)
    x1 = got_ref[:, :width].astype(F32) + gate1 * branch
    hidden = (normalize(x1) * (1.0 + scale2) + shift2).astype(BF16)

    branch = jnp.zeros((rows, width), F32)
    for s in range(2):
        heads = ring + 1 if s == 0 else ring - 1
        query = FACTOR * turned(matrix(0, s), hidden)
        keyed = turned(hidden, matrix(1, s)).astype(BF16)
        valued = turned(matrix(2, s), hidden).astype(BF16)
        row = lax.broadcasted_iota(jnp.int32, (query.shape[0], 1), 0)
        inside = row % group
        owner = jnp.where(inside < (ring - 1) * size, inside // size, -1)
        owner = jnp.where(row >= gathered, ring - 1 + (row - gathered) // HDIM, owner)
        along = lax.broadcasted_iota(jnp.int32, (rows, heads * rows), 0) % per
        across = lax.broadcasted_iota(jnp.int32, (rows, heads * rows), 1) % per
        spread = jnp.concatenate(
            [jnp.where(owner == h, query, 0.0).astype(BF16) for h in range(heads)], axis=1
        )
        scores = jnp.dot(keyed, spread, preferred_element_type=F32)
        scores = jnp.where(along == across, scores, -jnp.inf)
        weights = jnp.exp2(scores - jnp.max(scores, axis=0, keepdims=True))
        inverse = 1.0 / jnp.sum(weights, axis=0, keepdims=True)
        mixed = jnp.dot(valued, weights.astype(BF16), preferred_element_type=F32)

        def piece(first_row, count, h):
            columns = slice(h * rows, (h + 1) * rows)
            return mixed[first_row : first_row + count, columns] * inverse[:, columns]

        pieces = []
        for k in range(3):
            pieces += [piece(k * group + h * size, size, h) for h in range(ring - 1)]
            pieces.append(jnp.zeros((group - (ring - 1) * size, rows), F32))
        pieces += [piece(gathered + (h - ring + 1) * HDIM, HDIM, h) for h in range(ring - 1, heads)]
        attended = jnp.concatenate(pieces, axis=0).astype(BF16)
        branch += lax.dot_general(
            attended, matrix(3, s), (((0,), (0,)), ((), ())), preferred_element_type=F32
        )
    y = x1 + gate2 * branch
    y = jnp.concatenate([y[per:], y[:per]], axis=0)
    out_ref[...] = y.astype(BF16)


def temporal(size, per, got, table, own, weights):
    group, width = weights.shape[1:]
    side = own[1].shape[0]
    rows = got.shape[0]
    return pl.pallas_call(
        lambda *refs: temporal_kernel(size, per, *refs),
        out_shape=jax.ShapeDtypeStruct((rows, width), BF16),
        in_specs=[vspec()] + [pl.BlockSpec(memory_space=pl.ANY)] * 5,
        out_specs=vspec(),
        scratch_shapes=[
            VMEM((5, 3 * group + side, width), BF16),
            VMEM((5, 3 * group, width), BF16),
            VMEM((table.shape[0], 4 * width), F32),
            pltpu.SemaphoreType.DMA((11,)),
        ],
        compiler_params=params(40),
        cost_estimate=pl.CostEstimate(
            flops=2 * rows * width * width * 5, bytes_accessed=15000000, transcendentals=16 * rows * rows
        ),
        name="temporal",
    )(got, in_hbm(table), *[in_hbm(v) for v in own], in_hbm(weights))


def last_kernel(line, tail_ref, got_ref, fresh_ref, out_ref):
    rows = fresh_ref.shape[0]
    per = rows // line
    spot = lax.broadcasted_iota(jnp.int32, (2 * rows, 2 * rows), 1)
    source = spot // per % 2 * rows + spot // (2 * per) * per + spot % per
    back = (lax.broadcasted_iota(jnp.int32, (2 * rows, 2 * rows), 0) == source).astype(BF16)
    values = jnp.dot(back, got_ref[...], preferred_element_type=F32).astype(BF16)
    out_ref[0] = values[:rows]

    @pl.when(tail_ref[0] == 0)
    def _():
        out_ref[1] = values[rows:]

    @pl.when(tail_ref[0] != 0)
    def _():
        out_ref[1] = fresh_ref[...]


def last(tail, line, got, fresh):
    rows, width = fresh.shape
    return pl.pallas_call(
        lambda *refs: last_kernel(line, *refs),
        out_shape=jax.ShapeDtypeStruct((2, rows, width), BF16),
        in_specs=[pl.BlockSpec(memory_space=pltpu.SMEM), vspec(), vspec()],
        out_specs=vspec(),
        compiler_params=params(8),
        cost_estimate=pl.CostEstimate(flops=40000000, bytes_accessed=1000000, transcendentals=0),
        name="last",
    )(tail, got, fresh)


def per_device(
    queue_tokens,
    fresh_frame,
    levels,
    mod_table,
    w_qkv_spatial,
    w_out_spatial,
    w_qkv_temporal,
    w_out_temporal,
):
    _, rows, width = queue_tokens.shape
    ring = lax.axis_size("tok")
    line = lax.axis_size("queue")
    spot = lax.axis_index("queue")
    up = [(i, (i + 1) % ring) for i in range(ring)]
    down = [(i, (i - 1) % ring) for i in range(ring)]

    def send_up(v):
        return lax.ppermute(v, "tok", up)

    def send_down(v):
        return lax.ppermute(v, "tok", down)

    side = w_out_temporal.shape[0]
    size = side // 6
    start = spot * size
    turned_qkv = jnp.swapaxes(w_qkv_temporal, 1, 2).reshape(3 * side, width)

    def rows_from(matrix, first_row):
        at = jnp.clip(start - first_row, 0, matrix.shape[0] - size)
        return lax.dynamic_slice(matrix, (at, 0), (size, width))

    chunk = jnp.where(
        start < 3 * side,
        rows_from(turned_qkv, 0),
        jnp.where(start < 4 * side, rows_from(w_out_temporal, 3 * side), rows_from(w_out_spatial, 4 * side)),
    )
    place = lax.axis_index("tok").astype(jnp.int32)[None]
    tail = (spot == line - 1).astype(jnp.int32)[None]
    chunk, place, tail = lax.optimization_barrier((chunk, place, tail))
    chunks = lax.all_to_all(
        jnp.broadcast_to(chunk[None], (ring, size, width)), "tok", 0, 0, tiled=True
    )

    *hidden, side_rows = first(line, levels, mod_table, queue_tokens)
    frames = [{0: h} for h in hidden]
    reach = ((4, 3), (3, 4))
    for step in range(1, 5):
        for j in range(2):
            if step <= reach[j][0]:
                frames[j][-step] = send_up(frames[j][1 - step])
            if step <= reach[j][1]:
                frames[j][step] = send_down(frames[j][step - 1])
    group = -(-(ring - 1) * size // 16) * 16
    weights = lax.all_gather(others(place, chunks, group), "queue", axis=0, tiled=False)

    offsets = [[0, 1, 2, 3, -4, -3, -2, -1], [0, 1, 2, 3, 4, -3, -2, -1]]
    mixed = spatial(
        offsets,
        place,
        jnp.swapaxes(w_qkv_spatial, 1, 2).reshape(3 * side, width),
        [frames[j][o] for j in range(2) for o in offsets[j]],
    )
    mixed = lax.all_to_all(mixed, "tok", 0, 0, tiled=True)

    per = rows // line
    sent = bundle(line, size, group, place, mixed, side_rows)
    got = lax.all_to_all(sent.reshape(line, 2 * per, sent.shape[1]), "queue", 0, 0, tiled=True)
    own = (turned_qkv.reshape(3, side, width), w_out_temporal, w_out_spatial)
    moved = temporal(size, per, got.reshape(sent.shape), mod_table, own, weights)
    got = lax.all_to_all(moved.reshape(line, 2 * per, width), "queue", 0, 0, tiled=True)
    return last(tail, line, got.reshape(2 * rows, width), fresh_frame)


def solution(mesh):
    return jax.shard_map(
        per_device,
        mesh=mesh,
        in_specs=(
            P("queue", "tok", None),
            P("tok", None),
            P("queue"),
            P(),
            P(None, None, "tok"),
            P("tok", None),
            P(None, None, "tok"),
            P("tok", None),
        ),
        out_specs=P("queue", "tok", None),
        check_vma=False,
    )
```

```python
import jax
import jax.numpy as jnp
from jax import lax
from jax.experimental import pallas as pl
from jax.experimental.pallas import tpu as pltpu
from jax.sharding import PartitionSpec as P

HEADS = 16
HDIM = 72
EPS = 1e-06
FACTOR = HDIM ** (-0.5) * 1.4426950408889634
BF16 = jnp.bfloat16
F32 = jnp.float32
VMEM = pltpu.VMEM


def params(mib):
    return pltpu.CompilerParams(vmem_limit_bytes=mib * 1024 * 1024)


def vspec():
    return pl.BlockSpec(memory_space=VMEM)


def in_hbm(values):
    return pltpu.with_memory_space_constraint(values, pltpu.HBM)


def normalize(values):
    mean = jnp.mean(values, axis=-1, keepdims=True)
    centered = values - mean
    variance = jnp.mean(centered * centered, axis=-1, keepdims=True)
    return centered * lax.rsqrt(variance + EPS)


def turned(values, matrix):
    return lax.dot_general(values, matrix, (((1,), (1,)), ((), ())), preferred_element_type=F32)


def first_kernel(line, levels_hbm, table_hbm, tokens_hbm, h0_ref, h1_ref, side_ref, table_ref, held, levels_ref, sems):
    _, rows, width = held.shape
    copies = [
        pltpu.make_async_copy(levels_hbm, levels_ref, sems.at[0]),
        pltpu.make_async_copy(tokens_hbm, held, sems.at[1]),
        pltpu.make_async_copy(table_hbm.at[:, pl.ds(0, 2 * width)], table_ref, sems.at[2]),
    ]
    for copy in copies:
        copy.start()
    for copy in copies:
        copy.wait()
    for j, out in enumerate((h0_ref, h1_ref)):
        row = table_ref[pl.ds(levels_ref[j], 1), :]
        values = normalize(held[j].astype(F32))
        out[...] = (values * (1.0 + row[:, width:]) + row[:, :width]).astype(BF16)
    moved, frame = order_matrix(line, 2 * rows)
    tokens = held[...].reshape(2 * rows, width)
    side_ref[:, :width] = jnp.dot(moved, tokens, preferred_element_type=F32).astype(BF16)
    one, two = levels_ref[0].astype(F32), levels_ref[1].astype(F32)
    side_ref[:, width:] = jnp.where(frame == 0, one, two).astype(BF16)


def order_matrix(line, rows):
    per = rows // (2 * line)
    spot = lax.broadcasted_iota(jnp.int32, (rows, rows), 0)
    frame = spot // per % 2
    source = frame * (rows // 2) + spot // (2 * per) * per + spot % per
    moved = (lax.broadcasted_iota(jnp.int32, (rows, rows), 1) == source).astype(BF16)
    return moved, frame


def first(line, levels, table, tokens):
    _, rows, width = tokens.shape
    block = jax.ShapeDtypeStruct((rows, width), BF16)
    return pl.pallas_call(
        lambda *refs: first_kernel(line, *refs),
        out_shape=(block, block, jax.ShapeDtypeStruct((2 * rows, width + 2 * rows), BF16)),
        in_specs=[pl.BlockSpec(memory_space=pl.ANY)] * 3,
        out_specs=(vspec(), vspec(), vspec()),
        scratch_shapes=[
            VMEM((table.shape[0], 2 * width), F32),
            VMEM(tokens.shape, BF16),
            pltpu.SMEM(levels.shape, jnp.int32),
            pltpu.SemaphoreType.DMA((3,)),
        ],
        compiler_params=params(12),
        cost_estimate=pl.CostEstimate(flops=40000000, bytes_accessed=1500000, transcendentals=0),
        name="first",
    )(in_hbm(levels), in_hbm(table), in_hbm(tokens))


def others_kernel(place_ref, chunks_ref, out_ref):
    ring, size, width = chunks_ref.shape
    pieces = [chunks_ref[lax.rem(place_ref[0] + offset, ring)].astype(F32) for offset in range(1, ring)]
    spare = out_ref.shape[0] - (ring - 1) * size
    out_ref[...] = jnp.concatenate(pieces + [jnp.zeros((spare, width), F32)], axis=0).astype(BF16)


def others(place, chunks, rows):
    return pl.pallas_call(
        others_kernel,
        out_shape=jax.ShapeDtypeStruct((rows, chunks.shape[2]), BF16),
        in_specs=[pl.BlockSpec(memory_space=pltpu.SMEM), vspec()],
        out_specs=vspec(),
        compiler_params=params(8),
        cost_estimate=pl.CostEstimate(flops=0, bytes_accessed=900000, transcendentals=0),
        name="others",
    )(place, chunks)


def spatial_kernel(offsets, place_ref, w_hbm, table_hbm, *refs):
    *refs, out_ref, large_ref, small_ref, w_ref, table_ref, sems = refs
    copy = pltpu.make_async_copy(w_hbm, w_ref, sems.at[0])
    copy.start()
    count = table_ref.shape[1]
    table_copy = pltpu.make_async_copy(
        table_hbm.at[:, pl.ds(table_hbm.shape[1] - count, count)], table_ref, sems.at[1]
    )
    table_copy.start()
    rows = refs[0].shape[0]
    ring = len(offsets[0])
    for j in range(2):
        hidden = jnp.concatenate([ref[...] for ref in refs[j * ring : (j + 1) * ring]], axis=0)
        if j == 0:
            copy.wait()
        projected = turned(w_ref[...], hidden)
        side = projected.shape[0] // 3
        projected = jnp.concatenate([FACTOR * projected[:side], projected[side:]], axis=0).astype(BF16)
        heads = []
        for h in range(side // HDIM):
            query, keyed, valued = [
                projected[m * side + h * HDIM : m * side + (h + 1) * HDIM] for m in range(3)
            ]
            scores = lax.dot_general(
                keyed, query, (((0,), (0,)), ((), ())), preferred_element_type=F32
            )
            weights = jnp.exp2(scores - jnp.max(scores, axis=0, keepdims=True))
            total = jnp.sum(weights, axis=0, keepdims=True)
            mixed = jnp.dot(valued, weights.astype(BF16), preferred_element_type=F32)
            heads.append((mixed / total).astype(BF16))
        attended = jnp.concatenate(heads, axis=0)
        for n, offset in enumerate(offsets[j]):
            owner = lax.rem(place_ref[0] + offset + ring, ring)
            out_ref[owner, :, j * rows : (j + 1) * rows] = attended[:, n * rows : (n + 1) * rows]
    table_copy.wait()
    values = table_ref[...]
    large = values.astype(BF16)
    large_ref[...] = large
    small_ref[...] = (values - large.astype(F32)).astype(BF16)


def spatial(offsets, place, w_qkv, table, blocks):
    rows, width = blocks[0].shape
    ring = len(offsets[0])
    whole = rows * ring
    return pl.pallas_call(
        lambda *refs: spatial_kernel(offsets, *refs),
        out_shape=(
            jax.ShapeDtypeStruct((ring, w_qkv.shape[0] // 3, 2 * rows), BF16),
            jax.ShapeDtypeStruct((table.shape[0], 4 * width), BF16),
            jax.ShapeDtypeStruct((table.shape[0], 4 * width), BF16),
        ),
        in_specs=[pl.BlockSpec(memory_space=pltpu.SMEM)]
        + [pl.BlockSpec(memory_space=pl.ANY)] * 2
        + [vspec()] * len(blocks),
        out_specs=(vspec(), vspec(), vspec()),
        scratch_shapes=[
            VMEM(w_qkv.shape, BF16),
            VMEM((table.shape[0], 4 * width), F32),
            pltpu.SemaphoreType.DMA((2,)),
        ],
        compiler_params=params(20),
        cost_estimate=pl.CostEstimate(
            flops=4 * whole * width * 144 * 3 + 8 * whole * whole * 256,
            bytes_accessed=8000000,
            transcendentals=4 * whole * whole,
        ),
        name="spatial",
    )(place, in_hbm(w_qkv), in_hbm(table), *blocks)


def bundle_kernel(line, size, group, place_ref, mixed_ref, side_ref, out_ref):
    ring, side, rows = mixed_ref.shape
    width = ring * side
    parts = [mixed_ref[lax.rem(place_ref[0] + offset, ring)].astype(F32) for offset in range(ring)]
    pieces = []
    for s in range(2):
        for k in range(3 * s, 3 * s + 3):
            pieces += [parts[offset][k * size : (k + 1) * size] for offset in range(1, ring)]
            pieces.append(jnp.zeros((group - (ring - 1) * size, rows), F32))
        if s == 0:
            pieces.append(parts[0])
    mixed = jnp.concatenate(pieces, axis=0).astype(BF16)
    moved, _ = order_matrix(line, rows)
    end = width + mixed.shape[0]
    out_ref[:, :width] = side_ref[:, :width]
    out_ref[:, width:end] = turned(moved, mixed).astype(BF16)
    out_ref[:, end:] = side_ref[:, width : width + out_ref.shape[1] - end]


def bundle(line, size, group, place, mixed, tokens):
    ring, side, rows = mixed.shape
    whole = ring * side + 6 * group + side
    lanes = -(-(whole + 64) // 128) * 128
    return pl.pallas_call(
        lambda *refs: bundle_kernel(line, size, group, *refs),
        out_shape=jax.ShapeDtypeStruct((rows, lanes), BF16),
        in_specs=[pl.BlockSpec(memory_space=pltpu.SMEM), vspec(), vspec()],
        out_specs=vspec(),
        compiler_params=params(12),
        cost_estimate=pl.CostEstimate(flops=40000000, bytes_accessed=1500000, transcendentals=0),
        name="bundle",
    )(place, mixed, tokens)


def temporal_kernel(
    size, per, got_ref, large_ref, small_ref, own_qkv, own_temporal, own_spatial, weights_hbm, out_ref, one_ref, two_ref, sems
):
    group, width = weights_hbm.shape[1:]
    side = own_temporal.shape[0]
    ring = width // side
    held = (one_ref, two_ref)
    gathered = 3 * group

    def start(m, s):
        for k in range(3):
            pltpu.make_async_copy(
                weights_hbm.at[6 * m + 3 * s + k], held[s].at[m, pl.ds(k * group, group)], sems.at[2 * m + s]
            ).start()
        if s == 0:
            own = own_qkv.at[m] if m < 3 else (own_temporal, own_spatial)[m - 3]
            pltpu.make_async_copy(own, one_ref.at[m, pl.ds(gathered, side)], sems.at[2 * m]).start()

    for m, s in ((4, 0), (4, 1), (0, 0), (1, 0), (2, 0), (3, 0), (0, 1), (1, 1), (2, 1), (3, 1)):
        start(m, s)
    rows = got_ref.shape[0]

    def matrix(m, s):
        pltpu.make_async_copy(held[s].at[m], held[s].at[m], sems.at[2 * m + s]).wait()
        return held[s][m]

    split = width + gathered + side
    end = split + gathered
    level = got_ref[:, end : end + large_ref.shape[0]].astype(F32)
    column = lax.broadcasted_iota(jnp.int32, level.shape, 1).astype(F32)
    onehot = (level == column).astype(BF16)

    def mods(n):
        part = slice(n * width, (n + 1) * width)
        return jnp.dot(onehot, large_ref[:, part], preferred_element_type=F32) + jnp.dot(
            onehot, small_ref[:, part], preferred_element_type=F32
        )

    gate1, shift2, scale2, gate2 = [mods(n) for n in range(4)]
    branch = jnp.dot(got_ref[:, width:split], matrix(4, 0), preferred_element_type=F32)
    branch += jnp.dot(got_ref[:, split:end], matrix(4, 1), preferred_element_type=F32)
    x1 = got_ref[:, :width].astype(F32) + gate1 * branch
    hidden = (normalize(x1) * (1.0 + scale2) + shift2).astype(BF16)

    branch = jnp.zeros((rows, width), F32)
    for s in range(2):
        heads = ring + 1 if s == 0 else ring - 1
        query = FACTOR * turned(matrix(0, s), hidden)
        keyed = turned(hidden, matrix(1, s)).astype(BF16)
        valued = turned(matrix(2, s), hidden).astype(BF16)
        row = lax.broadcasted_iota(jnp.int32, (query.shape[0], 1), 0)
        inside = row % group
        owner = jnp.where(inside < (ring - 1) * size, inside // size, -1)
        owner = jnp.where(row >= gathered, ring - 1 + (row - gathered) // HDIM, owner)
        along = lax.broadcasted_iota(jnp.int32, (rows, heads * rows), 0) % per
        across = lax.broadcasted_iota(jnp.int32, (rows, heads * rows), 1) % per
        spread = jnp.concatenate(
            [jnp.where(owner == h, query, 0.0).astype(BF16) for h in range(heads)], axis=1
        )
        scores = jnp.dot(keyed, spread, preferred_element_type=F32)
        scores = jnp.where(along == across, scores, -jnp.inf)
        weights = jnp.exp2(scores - jnp.max(scores, axis=0, keepdims=True))
        inverse = 1.0 / jnp.sum(weights, axis=0, keepdims=True)
        mixed = jnp.dot(valued, weights.astype(BF16), preferred_element_type=F32)

        def piece(first_row, count, h):
            columns = slice(h * rows, (h + 1) * rows)
            return mixed[first_row : first_row + count, columns] * inverse[:, columns]

        pieces = []
        for k in range(3):
            pieces += [piece(k * group + h * size, size, h) for h in range(ring - 1)]
            pieces.append(jnp.zeros((group - (ring - 1) * size, rows), F32))
        pieces += [piece(gathered + (h - ring + 1) * HDIM, HDIM, h) for h in range(ring - 1, heads)]
        attended = jnp.concatenate(pieces, axis=0).astype(BF16)
        branch += lax.dot_general(
            attended, matrix(3, s), (((0,), (0,)), ((), ())), preferred_element_type=F32
        )
    y = x1 + gate2 * branch
    y = jnp.concatenate([y[per:], y[:per]], axis=0)
    out_ref[...] = y.astype(BF16)


def temporal(size, per, got, staged, own, weights):
    group, width = weights.shape[1:]
    side = own[1].shape[0]
    rows = got.shape[0]
    return pl.pallas_call(
        lambda *refs: temporal_kernel(size, per, *refs),
        out_shape=jax.ShapeDtypeStruct((rows, width), BF16),
        in_specs=[vspec()] * 3 + [pl.BlockSpec(memory_space=pl.ANY)] * 4,
        out_specs=vspec(),
        scratch_shapes=[
            VMEM((5, 3 * group + side, width), BF16),
            VMEM((5, 3 * group, width), BF16),
            pltpu.SemaphoreType.DMA((10,)),
        ],
        compiler_params=params(40),
        cost_estimate=pl.CostEstimate(
            flops=2 * rows * width * width * 5, bytes_accessed=15000000, transcendentals=16 * rows * rows
        ),
        name="temporal",
    )(got, *staged, *[in_hbm(v) for v in own], in_hbm(weights))


def last_kernel(line, tail_ref, got_ref, fresh_ref, out_ref):
    rows = fresh_ref.shape[0]
    per = rows // line
    spot = lax.broadcasted_iota(jnp.int32, (2 * rows, 2 * rows), 1)
    source = spot // per % 2 * rows + spot // (2 * per) * per + spot % per
    back = (lax.broadcasted_iota(jnp.int32, (2 * rows, 2 * rows), 0) == source).astype(BF16)
    values = jnp.dot(back, got_ref[...], preferred_element_type=F32).astype(BF16)
    out_ref[0] = values[:rows]

    @pl.when(tail_ref[0] == 0)
    def _():
        out_ref[1] = values[rows:]

    @pl.when(tail_ref[0] != 0)
    def _():
        out_ref[1] = fresh_ref[...]


def last(tail, line, got, fresh):
    rows, width = fresh.shape
    return pl.pallas_call(
        lambda *refs: last_kernel(line, *refs),
        out_shape=jax.ShapeDtypeStruct((2, rows, width), BF16),
        in_specs=[pl.BlockSpec(memory_space=pltpu.SMEM), vspec(), vspec()],
        out_specs=vspec(),
        compiler_params=params(8),
        cost_estimate=pl.CostEstimate(flops=40000000, bytes_accessed=1000000, transcendentals=0),
        name="last",
    )(tail, got, fresh)


def per_device(
    queue_tokens,
    fresh_frame,
    levels,
    mod_table,
    w_qkv_spatial,
    w_out_spatial,
    w_qkv_temporal,
    w_out_temporal,
):
    _, rows, width = queue_tokens.shape
    ring = lax.axis_size("tok")
    line = lax.axis_size("queue")
    spot = lax.axis_index("queue")
    up = [(i, (i + 1) % ring) for i in range(ring)]
    down = [(i, (i - 1) % ring) for i in range(ring)]

    def send_up(v):
        return lax.ppermute(v, "tok", up)

    def send_down(v):
        return lax.ppermute(v, "tok", down)

    side = w_out_temporal.shape[0]
    size = side // 6
    start = spot * size
    turned_qkv = jnp.swapaxes(w_qkv_temporal, 1, 2).reshape(3 * side, width)

    def rows_from(matrix, first_row):
        at = jnp.clip(start - first_row, 0, matrix.shape[0] - size)
        return lax.dynamic_slice(matrix, (at, 0), (size, width))

    chunk = jnp.where(
        start < 3 * side,
        rows_from(turned_qkv, 0),
        jnp.where(start < 4 * side, rows_from(w_out_temporal, 3 * side), rows_from(w_out_spatial, 4 * side)),
    )
    place = lax.axis_index("tok").astype(jnp.int32)[None]
    tail = (spot == line - 1).astype(jnp.int32)[None]
    chunk, place, tail = lax.optimization_barrier((chunk, place, tail))
    chunks = lax.all_to_all(
        jnp.broadcast_to(chunk[None], (ring, size, width)), "tok", 0, 0, tiled=True
    )

    *hidden, side_rows = first(line, levels, mod_table, queue_tokens)
    frames = [{0: h} for h in hidden]
    reach = ((4, 3), (3, 4))
    for step in range(1, 5):
        for j in range(2):
            if step <= reach[j][0]:
                frames[j][-step] = send_up(frames[j][1 - step])
            if step <= reach[j][1]:
                frames[j][step] = send_down(frames[j][step - 1])
    group = -(-(ring - 1) * size // 16) * 16
    weights = lax.all_gather(others(place, chunks, group), "queue", axis=0, tiled=False)

    offsets = [[0, 1, 2, 3, -4, -3, -2, -1], [0, 1, 2, 3, 4, -3, -2, -1]]
    own = (turned_qkv.reshape(3, side, width), w_out_temporal, w_out_spatial)
    mixed, *staged = spatial(
        offsets,
        place,
        jnp.swapaxes(w_qkv_spatial, 1, 2).reshape(3 * side, width),
        mod_table,
        [frames[j][o] for j in range(2) for o in offsets[j]],
    )
    mixed = lax.all_to_all(mixed, "tok", 0, 0, tiled=True)

    per = rows // line
    sent = bundle(line, size, group, place, mixed, side_rows)
    got = lax.all_to_all(sent.reshape(line, 2 * per, sent.shape[1]), "queue", 0, 0, tiled=True)
    moved = temporal(size, per, got.reshape(sent.shape), staged, own, weights)
    got = lax.all_to_all(moved.reshape(line, 2 * per, width), "queue", 0, 0, tiled=True)
    return last(tail, line, got.reshape(2 * rows, width), fresh_frame)


def solution(mesh):
    return jax.shard_map(
        per_device,
        mesh=mesh,
        in_specs=(
            P("queue", "tok", None),
            P("tok", None),
            P("queue"),
            P(),
            P(None, None, "tok"),
            P("tok", None),
            P(None, None, "tok"),
            P("tok", None),
        ),
        out_specs=P("queue", "tok", None),
        check_vma=False,
    )
```

```python
import jax
import jax.numpy as jnp
from jax import lax
from jax.experimental import pallas as pl
from jax.experimental.pallas import tpu as pltpu
from jax.sharding import PartitionSpec as P

HEADS = 16
HDIM = 72
EPS = 1e-06
FACTOR = HDIM ** (-0.5) * 1.4426950408889634
BF16 = jnp.bfloat16
F32 = jnp.float32
VMEM = pltpu.VMEM


def params(mib):
    return pltpu.CompilerParams(vmem_limit_bytes=mib * 1024 * 1024)


def vspec():
    return pl.BlockSpec(memory_space=VMEM)


def in_hbm(values):
    return pltpu.with_memory_space_constraint(values, pltpu.HBM)


def normalize(values):
    mean = jnp.mean(values, axis=-1, keepdims=True)
    centered = values - mean
    variance = jnp.mean(centered * centered, axis=-1, keepdims=True)
    return centered * lax.rsqrt(variance + EPS)


def turned(values, matrix):
    return lax.dot_general(values, matrix, (((1,), (1,)), ((), ())), preferred_element_type=F32)


def first_kernel(line, levels_hbm, table_hbm, tokens_hbm, h0_ref, h1_ref, side_ref, table_ref, held, levels_ref, sems):
    _, rows, width = held.shape
    copies = [
        pltpu.make_async_copy(levels_hbm, levels_ref, sems.at[0]),
        pltpu.make_async_copy(tokens_hbm, held, sems.at[1]),
        pltpu.make_async_copy(table_hbm.at[:, pl.ds(0, 2 * width)], table_ref, sems.at[2]),
    ]
    for copy in copies:
        copy.start()
    for copy in copies:
        copy.wait()
    for j, out in enumerate((h0_ref, h1_ref)):
        row = table_ref[pl.ds(levels_ref[j], 1), :]
        values = normalize(held[j].astype(F32))
        out[...] = (values * (1.0 + row[:, width:]) + row[:, :width]).astype(BF16)
    moved, frame = order_matrix(line, 2 * rows)
    tokens = held[...].reshape(2 * rows, width)
    side_ref[:, :width] = jnp.dot(moved, tokens, preferred_element_type=F32).astype(BF16)
    one, two = levels_ref[0].astype(F32), levels_ref[1].astype(F32)
    side_ref[:, width:] = jnp.where(frame == 0, one, two).astype(BF16)


def order_matrix(line, rows):
    per = rows // (2 * line)
    spot = lax.broadcasted_iota(jnp.int32, (rows, rows), 0)
    frame = spot // per % 2
    source = frame * (rows // 2) + spot // (2 * per) * per + spot % per
    moved = (lax.broadcasted_iota(jnp.int32, (rows, rows), 1) == source).astype(BF16)
    return moved, frame


def first(line, levels, table, tokens):
    _, rows, width = tokens.shape
    block = jax.ShapeDtypeStruct((rows, width), BF16)
    return pl.pallas_call(
        lambda *refs: first_kernel(line, *refs),
        out_shape=(block, block, jax.ShapeDtypeStruct((2 * rows, width + 2 * rows), BF16)),
        in_specs=[pl.BlockSpec(memory_space=pl.ANY)] * 3,
        out_specs=(vspec(), vspec(), vspec()),
        scratch_shapes=[
            VMEM((table.shape[0], 2 * width), F32),
            VMEM(tokens.shape, BF16),
            pltpu.SMEM(levels.shape, jnp.int32),
            pltpu.SemaphoreType.DMA((3,)),
        ],
        compiler_params=params(12),
        cost_estimate=pl.CostEstimate(flops=40000000, bytes_accessed=1500000, transcendentals=0),
        name="first",
    )(in_hbm(levels), in_hbm(table), in_hbm(tokens))


def others_kernel(place_ref, chunks_ref, out_ref):
    ring, size, width = chunks_ref.shape
    pieces = [chunks_ref[lax.rem(place_ref[0] + offset, ring)].astype(F32) for offset in range(1, ring)]
    spare = out_ref.shape[0] - (ring - 1) * size
    out_ref[...] = jnp.concatenate(pieces + [jnp.zeros((spare, width), F32)], axis=0).astype(BF16)


def others(place, chunks, rows):
    return pl.pallas_call(
        others_kernel,
        out_shape=jax.ShapeDtypeStruct((rows, chunks.shape[2]), BF16),
        in_specs=[pl.BlockSpec(memory_space=pltpu.SMEM), vspec()],
        out_specs=vspec(),
        compiler_params=params(8),
        cost_estimate=pl.CostEstimate(flops=0, bytes_accessed=900000, transcendentals=0),
        name="others",
    )(place, chunks)


def spatial_kernel(offsets, place_ref, w_hbm, table_hbm, *refs):
    *refs, out_ref, large_ref, small_ref, w_ref, table_ref, sems = refs
    copy = pltpu.make_async_copy(w_hbm, w_ref, sems.at[0])
    copy.start()
    count = table_ref.shape[1]
    table_copy = pltpu.make_async_copy(
        table_hbm.at[:, pl.ds(table_hbm.shape[1] - count, count)], table_ref, sems.at[1]
    )
    table_copy.start()
    rows = refs[0].shape[0]
    ring = len(offsets[0])
    for j in range(2):
        hidden = jnp.concatenate([ref[...] for ref in refs[j * ring : (j + 1) * ring]], axis=0)
        if j == 0:
            copy.wait()
        projected = turned(w_ref[...], hidden)
        side = projected.shape[0] // 3
        projected = jnp.concatenate([FACTOR * projected[:side], projected[side:]], axis=0).astype(BF16)
        heads = []
        for h in range(side // HDIM):
            query, keyed, valued = [
                projected[m * side + h * HDIM : m * side + (h + 1) * HDIM] for m in range(3)
            ]
            scores = lax.dot_general(
                keyed, query, (((0,), (0,)), ((), ())), preferred_element_type=F32
            )
            weights = jnp.exp2(scores - jnp.max(scores, axis=0, keepdims=True))
            total = jnp.sum(weights, axis=0, keepdims=True)
            mixed = jnp.dot(valued, weights.astype(BF16), preferred_element_type=F32)
            heads.append((mixed / total).astype(BF16))
        attended = jnp.concatenate(heads, axis=0)
        for n, offset in enumerate(offsets[j]):
            owner = lax.rem(place_ref[0] + offset + ring, ring)
            out_ref[owner, :, j * rows : (j + 1) * rows] = attended[:, n * rows : (n + 1) * rows]
    table_copy.wait()
    values = table_ref[...]
    large = values.astype(BF16)
    large_ref[...] = large
    small_ref[...] = (values - large.astype(F32)).astype(BF16)


def spatial(offsets, place, w_qkv, table, blocks):
    rows, width = blocks[0].shape
    ring = len(offsets[0])
    whole = rows * ring
    return pl.pallas_call(
        lambda *refs: spatial_kernel(offsets, *refs),
        out_shape=(
            jax.ShapeDtypeStruct((ring, w_qkv.shape[0] // 3, 2 * rows), BF16),
            jax.ShapeDtypeStruct((table.shape[0], 4 * width), BF16),
            jax.ShapeDtypeStruct((table.shape[0], 4 * width), BF16),
        ),
        in_specs=[pl.BlockSpec(memory_space=pltpu.SMEM)]
        + [pl.BlockSpec(memory_space=pl.ANY)] * 2
        + [vspec()] * len(blocks),
        out_specs=(vspec(), vspec(), vspec()),
        scratch_shapes=[
            VMEM(w_qkv.shape, BF16),
            VMEM((table.shape[0], 4 * width), F32),
            pltpu.SemaphoreType.DMA((2,)),
        ],
        compiler_params=params(20),
        cost_estimate=pl.CostEstimate(
            flops=4 * whole * width * 144 * 3 + 8 * whole * whole * 256,
            bytes_accessed=8000000,
            transcendentals=4 * whole * whole,
        ),
        name="spatial",
    )(place, in_hbm(w_qkv), in_hbm(table), *blocks)


def bundle_kernel(line, size, group, place_ref, mixed_ref, side_ref, out_ref):
    ring, side, rows = mixed_ref.shape
    width = ring * side
    parts = [mixed_ref[lax.rem(place_ref[0] + offset, ring)].astype(F32) for offset in range(ring)]
    pieces = []
    for s in range(2):
        for k in range(3 * s, 3 * s + 3):
            pieces += [parts[offset][k * size : (k + 1) * size] for offset in range(1, ring)]
            pieces.append(jnp.zeros((group - (ring - 1) * size, rows), F32))
        if s == 0:
            pieces.append(parts[0])
    mixed = jnp.concatenate(pieces, axis=0).astype(BF16)
    moved, _ = order_matrix(line, rows)
    end = width + mixed.shape[0]
    out_ref[:, :width] = side_ref[:, :width]
    out_ref[:, width:end] = turned(moved, mixed).astype(BF16)
    out_ref[:, end:] = side_ref[:, width : width + out_ref.shape[1] - end]


def bundle(line, size, group, place, mixed, tokens):
    ring, side, rows = mixed.shape
    whole = ring * side + 6 * group + side
    lanes = -(-(whole + 64) // 128) * 128
    return pl.pallas_call(
        lambda *refs: bundle_kernel(line, size, group, *refs),
        out_shape=jax.ShapeDtypeStruct((rows, lanes), BF16),
        in_specs=[pl.BlockSpec(memory_space=pltpu.SMEM), vspec(), vspec()],
        out_specs=vspec(),
        compiler_params=params(12),
        cost_estimate=pl.CostEstimate(flops=40000000, bytes_accessed=1500000, transcendentals=0),
        name="bundle",
    )(place, mixed, tokens)


def temporal_kernel(
    size, per, got_ref, large_ref, small_ref, own_qkv, own_temporal, own_spatial, weights_hbm, out_ref, one_ref, two_ref, sems
):
    group, width = weights_hbm.shape[1:]
    side = own_temporal.shape[0]
    ring = width // side
    held = (one_ref, two_ref)
    gathered = 3 * group

    def start(m, s):
        for k in range(3):
            pltpu.make_async_copy(
                weights_hbm.at[6 * m + 3 * s + k], held[s].at[m, pl.ds(k * group, group)], sems.at[2 * m + s]
            ).start()
        if s == 0:
            own = own_qkv.at[m] if m < 3 else (own_temporal, own_spatial)[m - 3]
            pltpu.make_async_copy(own, one_ref.at[m, pl.ds(gathered, side)], sems.at[2 * m]).start()

    for m, s in ((4, 0), (4, 1), (0, 0), (1, 0), (2, 0), (3, 0), (0, 1), (1, 1), (2, 1), (3, 1)):
        start(m, s)
    rows = got_ref.shape[0]

    def matrix(m, s):
        pltpu.make_async_copy(held[s].at[m], held[s].at[m], sems.at[2 * m + s]).wait()
        return held[s][m]

    split = width + gathered + side
    end = split + gathered
    level = got_ref[:, end : end + large_ref.shape[0]].astype(F32)
    column = lax.broadcasted_iota(jnp.int32, level.shape, 1).astype(F32)
    onehot = (level == column).astype(BF16)

    def mods(n):
        part = slice(n * width, (n + 1) * width)
        return jnp.dot(onehot, large_ref[:, part], preferred_element_type=F32) + jnp.dot(
            onehot, small_ref[:, part], preferred_element_type=F32
        )

    gate1, shift2, scale2, gate2 = [mods(n) for n in range(4)]
    branch = jnp.dot(got_ref[:, width:split], matrix(4, 0), preferred_element_type=F32)
    branch += jnp.dot(got_ref[:, split:end], matrix(4, 1), preferred_element_type=F32)
    x1 = got_ref[:, :width].astype(F32) + gate1 * branch
    hidden = (normalize(x1) * (1.0 + scale2) + shift2).astype(BF16)

    branch = jnp.zeros((rows, width), F32)
    for s in range(2):
        heads = ring + 1 if s == 0 else ring - 1
        query = FACTOR * turned(matrix(0, s), hidden)
        keyed = turned(hidden, matrix(1, s)).astype(BF16)
        valued = turned(matrix(2, s), hidden).astype(BF16)
        row = lax.broadcasted_iota(jnp.int32, (query.shape[0], 1), 0)
        inside = row % group
        owner = jnp.where(inside < (ring - 1) * size, inside // size, -1)
        owner = jnp.where(row >= gathered, ring - 1 + (row - gathered) // HDIM, owner)
        along = lax.broadcasted_iota(jnp.int32, (rows, 1), 0) % per
        across = lax.broadcasted_iota(jnp.int32, (1, heads * rows), 1) % per
        spread = jnp.concatenate(
            [jnp.where(owner == h, query, 0.0).astype(BF16) for h in range(heads)], axis=1
        )
        scores = jnp.dot(keyed, spread, preferred_element_type=F32)
        scores = jnp.where(along == across, scores, -jnp.inf)
        weights = jnp.exp2(scores - jnp.max(scores, axis=0, keepdims=True))
        inverse = 1.0 / jnp.sum(weights, axis=0, keepdims=True)
        mixed = jnp.dot(valued, weights.astype(BF16), preferred_element_type=F32)

        def piece(first_row, count, h):
            columns = slice(h * rows, (h + 1) * rows)
            return mixed[first_row : first_row + count, columns] * inverse[:, columns]

        pieces = []
        for k in range(3):
            pieces += [piece(k * group + h * size, size, h) for h in range(ring - 1)]
            pieces.append(jnp.zeros((group - (ring - 1) * size, rows), F32))
        pieces += [piece(gathered + (h - ring + 1) * HDIM, HDIM, h) for h in range(ring - 1, heads)]
        attended = jnp.concatenate(pieces, axis=0).astype(BF16)
        branch += lax.dot_general(
            attended, matrix(3, s), (((0,), (0,)), ((), ())), preferred_element_type=F32
        )
    y = x1 + gate2 * branch
    y = jnp.concatenate([y[per:], y[:per]], axis=0)
    out_ref[...] = y.astype(BF16)


def temporal(size, per, got, staged, own, weights):
    group, width = weights.shape[1:]
    side = own[1].shape[0]
    rows = got.shape[0]
    return pl.pallas_call(
        lambda *refs: temporal_kernel(size, per, *refs),
        out_shape=jax.ShapeDtypeStruct((rows, width), BF16),
        in_specs=[vspec()] * 3 + [pl.BlockSpec(memory_space=pl.ANY)] * 4,
        out_specs=vspec(),
        scratch_shapes=[
            VMEM((5, 3 * group + side, width), BF16),
            VMEM((5, 3 * group, width), BF16),
            pltpu.SemaphoreType.DMA((10,)),
        ],
        compiler_params=params(40),
        cost_estimate=pl.CostEstimate(
            flops=2 * rows * width * width * 5, bytes_accessed=15000000, transcendentals=16 * rows * rows
        ),
        name="temporal",
    )(got, *staged, *[in_hbm(v) for v in own], in_hbm(weights))


def last_kernel(line, tail_ref, got_ref, fresh_ref, out_ref):
    rows = fresh_ref.shape[0]
    per = rows // line
    spot = lax.broadcasted_iota(jnp.int32, (2 * rows, 2 * rows), 1)
    source = spot // per % 2 * rows + spot // (2 * per) * per + spot % per
    back = (lax.broadcasted_iota(jnp.int32, (2 * rows, 2 * rows), 0) == source).astype(BF16)
    values = jnp.dot(back, got_ref[...], preferred_element_type=F32).astype(BF16)
    out_ref[0] = values[:rows]

    @pl.when(tail_ref[0] == 0)
    def _():
        out_ref[1] = values[rows:]

    @pl.when(tail_ref[0] != 0)
    def _():
        out_ref[1] = fresh_ref[...]


def last(tail, line, got, fresh):
    rows, width = fresh.shape
    return pl.pallas_call(
        lambda *refs: last_kernel(line, *refs),
        out_shape=jax.ShapeDtypeStruct((2, rows, width), BF16),
        in_specs=[pl.BlockSpec(memory_space=pltpu.SMEM), vspec(), vspec()],
        out_specs=vspec(),
        compiler_params=params(8),
        cost_estimate=pl.CostEstimate(flops=40000000, bytes_accessed=1000000, transcendentals=0),
        name="last",
    )(tail, got, fresh)


def per_device(
    queue_tokens,
    fresh_frame,
    levels,
    mod_table,
    w_qkv_spatial,
    w_out_spatial,
    w_qkv_temporal,
    w_out_temporal,
):
    _, rows, width = queue_tokens.shape
    ring = lax.axis_size("tok")
    line = lax.axis_size("queue")
    spot = lax.axis_index("queue")
    up = [(i, (i + 1) % ring) for i in range(ring)]
    down = [(i, (i - 1) % ring) for i in range(ring)]

    def send_up(v):
        return lax.ppermute(v, "tok", up)

    def send_down(v):
        return lax.ppermute(v, "tok", down)

    side = w_out_temporal.shape[0]
    size = side // 6
    start = spot * size
    turned_qkv = jnp.swapaxes(w_qkv_temporal, 1, 2).reshape(3 * side, width)

    def rows_from(matrix, first_row):
        at = jnp.clip(start - first_row, 0, matrix.shape[0] - size)
        return lax.dynamic_slice(matrix, (at, 0), (size, width))

    chunk = jnp.where(
        start < 3 * side,
        rows_from(turned_qkv, 0),
        jnp.where(start < 4 * side, rows_from(w_out_temporal, 3 * side), rows_from(w_out_spatial, 4 * side)),
    )
    place = lax.axis_index("tok").astype(jnp.int32)[None]
    tail = (spot == line - 1).astype(jnp.int32)[None]
    chunk, place, tail = lax.optimization_barrier((chunk, place, tail))
    chunks = lax.all_to_all(
        jnp.broadcast_to(chunk[None], (ring, size, width)), "tok", 0, 0, tiled=True
    )

    *hidden, side_rows = first(line, levels, mod_table, queue_tokens)
    frames = [{0: h} for h in hidden]
    reach = ((4, 3), (3, 4))
    for step in range(1, 5):
        for j in range(2):
            if step <= reach[j][0]:
                frames[j][-step] = send_up(frames[j][1 - step])
            if step <= reach[j][1]:
                frames[j][step] = send_down(frames[j][step - 1])
    group = -(-(ring - 1) * size // 16) * 16
    weights = lax.all_gather(others(place, chunks, group), "queue", axis=0, tiled=False)

    offsets = [[0, 1, 2, 3, -4, -3, -2, -1], [0, 1, 2, 3, 4, -3, -2, -1]]
    own = (turned_qkv.reshape(3, side, width), w_out_temporal, w_out_spatial)
    mixed, *staged = spatial(
        offsets,
        place,
        jnp.swapaxes(w_qkv_spatial, 1, 2).reshape(3 * side, width),
        mod_table,
        [frames[j][o] for j in range(2) for o in offsets[j]],
    )
    mixed = lax.all_to_all(mixed, "tok", 0, 0, tiled=True)

    per = rows // line
    sent = bundle(line, size, group, place, mixed, side_rows)
    got = lax.all_to_all(sent.reshape(line, 2 * per, sent.shape[1]), "queue", 0, 0, tiled=True)
    moved = temporal(size, per, got.reshape(sent.shape), staged, own, weights)
    got = lax.all_to_all(moved.reshape(line, 2 * per, width), "queue", 0, 0, tiled=True)
    return last(tail, line, got.reshape(2 * rows, width), fresh_frame)


def solution(mesh):
    return jax.shard_map(
        per_device,
        mesh=mesh,
        in_specs=(
            P("queue", "tok", None),
            P("tok", None),
            P("queue"),
            P(),
            P(None, None, "tok"),
            P("tok", None),
            P(None, None, "tok"),
            P("tok", None),
        ),
        out_specs=P("queue", "tok", None),
        check_vma=False,
    )
```

```python
import jax
import jax.numpy as jnp
from jax import lax
from jax.experimental import pallas as pl
from jax.experimental.pallas import tpu as pltpu
from jax.sharding import PartitionSpec as P

HEADS = 16
HDIM = 72
EPS = 1e-06
FACTOR = HDIM ** (-0.5) * 1.4426950408889634
BF16 = jnp.bfloat16
F32 = jnp.float32
VMEM = pltpu.VMEM


def params(mib):
    return pltpu.CompilerParams(vmem_limit_bytes=mib * 1024 * 1024)


def vspec():
    return pl.BlockSpec(memory_space=VMEM)


def in_hbm(values):
    return pltpu.with_memory_space_constraint(values, pltpu.HBM)


def normalize(values):
    mean = jnp.mean(values, axis=-1, keepdims=True)
    centered = values - mean
    variance = jnp.mean(centered * centered, axis=-1, keepdims=True)
    return centered * lax.rsqrt(variance + EPS)


def turned(values, matrix):
    return lax.dot_general(values, matrix, (((1,), (1,)), ((), ())), preferred_element_type=F32)


def first_kernel(line, levels_hbm, table_hbm, tokens_hbm, h0_ref, h1_ref, side_ref, table_ref, held, levels_ref, sems):
    _, rows, width = held.shape
    copies = [
        pltpu.make_async_copy(levels_hbm, levels_ref, sems.at[0]),
        pltpu.make_async_copy(tokens_hbm, held, sems.at[1]),
        pltpu.make_async_copy(table_hbm.at[:, pl.ds(0, 2 * width)], table_ref, sems.at[2]),
    ]
    for copy in copies:
        copy.start()
    for copy in copies:
        copy.wait()
    for j, out in enumerate((h0_ref, h1_ref)):
        row = table_ref[pl.ds(levels_ref[j], 1), :]
        values = normalize(held[j].astype(F32))
        out[...] = (values * (1.0 + row[:, width:]) + row[:, :width]).astype(BF16)
    moved, frame = order_matrix(line, 2 * rows)
    tokens = held[...].reshape(2 * rows, width)
    side_ref[:, :width] = jnp.dot(moved, tokens, preferred_element_type=F32).astype(BF16)
    one, two = levels_ref[0].astype(F32), levels_ref[1].astype(F32)
    side_ref[:, width:] = jnp.broadcast_to(jnp.where(frame == 0, one, two), (2 * rows, 2 * rows)).astype(BF16)


def order_matrix(line, rows):
    per = rows // (2 * line)
    spot = lax.broadcasted_iota(jnp.int32, (rows, 1), 0)
    frame = spot // per % 2
    source = frame * (rows // 2) + spot // (2 * per) * per + spot % per
    moved = (lax.broadcasted_iota(jnp.int32, (rows, rows), 1) == source).astype(BF16)
    return moved, frame


def first(line, levels, table, tokens):
    _, rows, width = tokens.shape
    block = jax.ShapeDtypeStruct((rows, width), BF16)
    return pl.pallas_call(
        lambda *refs: first_kernel(line, *refs),
        out_shape=(block, block, jax.ShapeDtypeStruct((2 * rows, width + 2 * rows), BF16)),
        in_specs=[pl.BlockSpec(memory_space=pl.ANY)] * 3,
        out_specs=(vspec(), vspec(), vspec()),
        scratch_shapes=[
            VMEM((table.shape[0], 2 * width), F32),
            VMEM(tokens.shape, BF16),
            pltpu.SMEM(levels.shape, jnp.int32),
            pltpu.SemaphoreType.DMA((3,)),
        ],
        compiler_params=params(12),
        cost_estimate=pl.CostEstimate(flops=40000000, bytes_accessed=1500000, transcendentals=0),
        name="first",
    )(in_hbm(levels), in_hbm(table), in_hbm(tokens))


def others_kernel(place_ref, chunks_ref, out_ref):
    ring, size, width = chunks_ref.shape
    pieces = [chunks_ref[lax.rem(place_ref[0] + offset, ring)].astype(F32) for offset in range(1, ring)]
    spare = out_ref.shape[0] - (ring - 1) * size
    out_ref[...] = jnp.concatenate(pieces + [jnp.zeros((spare, width), F32)], axis=0).astype(BF16)


def others(place, chunks, rows):
    return pl.pallas_call(
        others_kernel,
        out_shape=jax.ShapeDtypeStruct((rows, chunks.shape[2]), BF16),
        in_specs=[pl.BlockSpec(memory_space=pltpu.SMEM), vspec()],
        out_specs=vspec(),
        compiler_params=params(8),
        cost_estimate=pl.CostEstimate(flops=0, bytes_accessed=900000, transcendentals=0),
        name="others",
    )(place, chunks)


def spatial_kernel(offsets, place_ref, w_hbm, table_hbm, *refs):
    *refs, out_ref, large_ref, small_ref, w_ref, table_ref, sems = refs
    copy = pltpu.make_async_copy(w_hbm, w_ref, sems.at[0])
    copy.start()
    count = table_ref.shape[1]
    table_copy = pltpu.make_async_copy(
        table_hbm.at[:, pl.ds(table_hbm.shape[1] - count, count)], table_ref, sems.at[1]
    )
    table_copy.start()
    rows = refs[0].shape[0]
    ring = len(offsets[0])
    for j in range(2):
        hidden = jnp.concatenate([ref[...] for ref in refs[j * ring : (j + 1) * ring]], axis=0)
        if j == 0:
            copy.wait()
        projected = turned(w_ref[...], hidden)
        side = projected.shape[0] // 3
        projected = jnp.concatenate([FACTOR * projected[:side], projected[side:]], axis=0).astype(BF16)
        heads = []
        for h in range(side // HDIM):
            query, keyed, valued = [
                projected[m * side + h * HDIM : m * side + (h + 1) * HDIM] for m in range(3)
            ]
            scores = lax.dot_general(
                keyed, query, (((0,), (0,)), ((), ())), preferred_element_type=F32
            )
            weights = jnp.exp2(scores - jnp.max(scores, axis=0, keepdims=True))
            total = jnp.sum(weights, axis=0, keepdims=True)
            mixed = jnp.dot(valued, weights.astype(BF16), preferred_element_type=F32)
            heads.append((mixed / total).astype(BF16))
        attended = jnp.concatenate(heads, axis=0)
        for n, offset in enumerate(offsets[j]):
            owner = lax.rem(place_ref[0] + offset + ring, ring)
            out_ref[owner, :, j * rows : (j + 1) * rows] = attended[:, n * rows : (n + 1) * rows]
    table_copy.wait()
    values = table_ref[...]
    large = values.astype(BF16)
    large_ref[...] = large
    small_ref[...] = (values - large.astype(F32)).astype(BF16)


def spatial(offsets, place, w_qkv, table, blocks):
    rows, width = blocks[0].shape
    ring = len(offsets[0])
    whole = rows * ring
    return pl.pallas_call(
        lambda *refs: spatial_kernel(offsets, *refs),
        out_shape=(
            jax.ShapeDtypeStruct((ring, w_qkv.shape[0] // 3, 2 * rows), BF16),
            jax.ShapeDtypeStruct((table.shape[0], 4 * width), BF16),
            jax.ShapeDtypeStruct((table.shape[0], 4 * width), BF16),
        ),
        in_specs=[pl.BlockSpec(memory_space=pltpu.SMEM)]
        + [pl.BlockSpec(memory_space=pl.ANY)] * 2
        + [vspec()] * len(blocks),
        out_specs=(vspec(), vspec(), vspec()),
        scratch_shapes=[
            VMEM(w_qkv.shape, BF16),
            VMEM((table.shape[0], 4 * width), F32),
            pltpu.SemaphoreType.DMA((2,)),
        ],
        compiler_params=params(20),
        cost_estimate=pl.CostEstimate(
            flops=4 * whole * width * 144 * 3 + 8 * whole * whole * 256,
            bytes_accessed=8000000,
            transcendentals=4 * whole * whole,
        ),
        name="spatial",
    )(place, in_hbm(w_qkv), in_hbm(table), *blocks)


def bundle_kernel(line, size, group, place_ref, mixed_ref, side_ref, out_ref):
    ring, side, rows = mixed_ref.shape
    width = ring * side
    parts = [mixed_ref[lax.rem(place_ref[0] + offset, ring)].astype(F32) for offset in range(ring)]
    pieces = []
    for s in range(2):
        for k in range(3 * s, 3 * s + 3):
            pieces += [parts[offset][k * size : (k + 1) * size] for offset in range(1, ring)]
            pieces.append(jnp.zeros((group - (ring - 1) * size, rows), F32))
        if s == 0:
            pieces.append(parts[0])
    mixed = jnp.concatenate(pieces, axis=0).astype(BF16)
    moved, _ = order_matrix(line, rows)
    end = width + mixed.shape[0]
    out_ref[:, :width] = side_ref[:, :width]
    out_ref[:, width:end] = turned(moved, mixed).astype(BF16)
    out_ref[:, end:] = side_ref[:, width : width + out_ref.shape[1] - end]


def bundle(line, size, group, place, mixed, tokens):
    ring, side, rows = mixed.shape
    whole = ring * side + 6 * group + side
    lanes = -(-(whole + 64) // 128) * 128
    return pl.pallas_call(
        lambda *refs: bundle_kernel(line, size, group, *refs),
        out_shape=jax.ShapeDtypeStruct((rows, lanes), BF16),
        in_specs=[pl.BlockSpec(memory_space=pltpu.SMEM), vspec(), vspec()],
        out_specs=vspec(),
        compiler_params=params(12),
        cost_estimate=pl.CostEstimate(flops=40000000, bytes_accessed=1500000, transcendentals=0),
        name="bundle",
    )(place, mixed, tokens)


def temporal_kernel(
    size, per, got_ref, large_ref, small_ref, own_qkv, own_temporal, own_spatial, weights_hbm, out_ref, one_ref, two_ref, sems
):
    group, width = weights_hbm.shape[1:]
    side = own_temporal.shape[0]
    ring = width // side
    held = (one_ref, two_ref)
    gathered = 3 * group

    def start(m, s):
        for k in range(3):
            pltpu.make_async_copy(
                weights_hbm.at[6 * m + 3 * s + k], held[s].at[m, pl.ds(k * group, group)], sems.at[2 * m + s]
            ).start()
        if s == 0:
            own = own_qkv.at[m] if m < 3 else (own_temporal, own_spatial)[m - 3]
            pltpu.make_async_copy(own, one_ref.at[m, pl.ds(gathered, side)], sems.at[2 * m]).start()

    for m, s in ((4, 0), (4, 1), (0, 0), (1, 0), (2, 0), (3, 0), (0, 1), (1, 1), (2, 1), (3, 1)):
        start(m, s)
    rows = got_ref.shape[0]

    def matrix(m, s):
        pltpu.make_async_copy(held[s].at[m], held[s].at[m], sems.at[2 * m + s]).wait()
        return held[s][m]

    split = width + gathered + side
    end = split + gathered
    level = got_ref[:, end : end + large_ref.shape[0]].astype(F32)
    column = lax.broadcasted_iota(jnp.int32, level.shape, 1).astype(F32)
    onehot = (level == column).astype(BF16)

    def mods(n):
        part = slice(n * width, (n + 1) * width)
        return jnp.dot(onehot, large_ref[:, part], preferred_element_type=F32) + jnp.dot(
            onehot, small_ref[:, part], preferred_element_type=F32
        )

    gate1, shift2, scale2, gate2 = [mods(n) for n in range(4)]
    branch = jnp.dot(got_ref[:, width:split], matrix(4, 0), preferred_element_type=F32)
    branch += jnp.dot(got_ref[:, split:end], matrix(4, 1), preferred_element_type=F32)
    x1 = got_ref[:, :width].astype(F32) + gate1 * branch
    hidden = (normalize(x1) * (1.0 + scale2) + shift2).astype(BF16)

    branch = jnp.zeros((rows, width), F32)
    for s in range(2):
        heads = ring + 1 if s == 0 else ring - 1
        query = FACTOR * turned(matrix(0, s), hidden)
        keyed = turned(hidden, matrix(1, s)).astype(BF16)
        valued = turned(matrix(2, s), hidden).astype(BF16)
        row = lax.broadcasted_iota(jnp.int32, (query.shape[0], 1), 0)
        inside = row % group
        owner = jnp.where(inside < (ring - 1) * size, inside // size, -1)
        owner = jnp.where(row >= gathered, ring - 1 + (row - gathered) // HDIM, owner)
        along = lax.broadcasted_iota(jnp.int32, (rows, 1), 0) % per
        across = lax.broadcasted_iota(jnp.int32, (1, heads * rows), 1) % per
        spread = jnp.concatenate(
            [jnp.where(owner == h, query, 0.0).astype(BF16) for h in range(heads)], axis=1
        )
        scores = jnp.dot(keyed, spread, preferred_element_type=F32)
        scores = jnp.where(along == across, scores, -jnp.inf)
        weights = jnp.exp2(scores - jnp.max(scores, axis=0, keepdims=True))
        inverse = 1.0 / jnp.sum(weights, axis=0, keepdims=True)
        mixed = jnp.dot(valued, weights.astype(BF16), preferred_element_type=F32)

        def piece(first_row, count, h):
            columns = slice(h * rows, (h + 1) * rows)
            return mixed[first_row : first_row + count, columns] * inverse[:, columns]

        pieces = []
        for k in range(3):
            pieces += [piece(k * group + h * size, size, h) for h in range(ring - 1)]
            pieces.append(jnp.zeros((group - (ring - 1) * size, rows), F32))
        pieces += [piece(gathered + (h - ring + 1) * HDIM, HDIM, h) for h in range(ring - 1, heads)]
        attended = jnp.concatenate(pieces, axis=0).astype(BF16)
        branch += lax.dot_general(
            attended, matrix(3, s), (((0,), (0,)), ((), ())), preferred_element_type=F32
        )
    y = x1 + gate2 * branch
    y = jnp.concatenate([y[per:], y[:per]], axis=0)
    out_ref[...] = y.astype(BF16)


def temporal(size, per, got, staged, own, weights):
    group, width = weights.shape[1:]
    side = own[1].shape[0]
    rows = got.shape[0]
    return pl.pallas_call(
        lambda *refs: temporal_kernel(size, per, *refs),
        out_shape=jax.ShapeDtypeStruct((rows, width), BF16),
        in_specs=[vspec()] * 3 + [pl.BlockSpec(memory_space=pl.ANY)] * 4,
        out_specs=vspec(),
        scratch_shapes=[
            VMEM((5, 3 * group + side, width), BF16),
            VMEM((5, 3 * group, width), BF16),
            pltpu.SemaphoreType.DMA((10,)),
        ],
        compiler_params=params(40),
        cost_estimate=pl.CostEstimate(
            flops=2 * rows * width * width * 5, bytes_accessed=15000000, transcendentals=16 * rows * rows
        ),
        name="temporal",
    )(got, *staged, *[in_hbm(v) for v in own], in_hbm(weights))


def last_kernel(line, tail_ref, got_ref, fresh_ref, out_ref):
    rows = fresh_ref.shape[0]
    per = rows // line
    spot = lax.broadcasted_iota(jnp.int32, (1, 2 * rows), 1)
    source = spot // per % 2 * rows + spot // (2 * per) * per + spot % per
    back = (lax.broadcasted_iota(jnp.int32, (2 * rows, 2 * rows), 0) == source).astype(BF16)
    values = jnp.dot(back, got_ref[...], preferred_element_type=F32).astype(BF16)
    out_ref[0] = values[:rows]

    @pl.when(tail_ref[0] == 0)
    def _():
        out_ref[1] = values[rows:]

    @pl.when(tail_ref[0] != 0)
    def _():
        out_ref[1] = fresh_ref[...]


def last(tail, line, got, fresh):
    rows, width = fresh.shape
    return pl.pallas_call(
        lambda *refs: last_kernel(line, *refs),
        out_shape=jax.ShapeDtypeStruct((2, rows, width), BF16),
        in_specs=[pl.BlockSpec(memory_space=pltpu.SMEM), vspec(), vspec()],
        out_specs=vspec(),
        compiler_params=params(8),
        cost_estimate=pl.CostEstimate(flops=40000000, bytes_accessed=1000000, transcendentals=0),
        name="last",
    )(tail, got, fresh)


def per_device(
    queue_tokens,
    fresh_frame,
    levels,
    mod_table,
    w_qkv_spatial,
    w_out_spatial,
    w_qkv_temporal,
    w_out_temporal,
):
    _, rows, width = queue_tokens.shape
    ring = lax.axis_size("tok")
    line = lax.axis_size("queue")
    spot = lax.axis_index("queue")
    up = [(i, (i + 1) % ring) for i in range(ring)]
    down = [(i, (i - 1) % ring) for i in range(ring)]

    def send_up(v):
        return lax.ppermute(v, "tok", up)

    def send_down(v):
        return lax.ppermute(v, "tok", down)

    side = w_out_temporal.shape[0]
    size = side // 6
    start = spot * size
    turned_qkv = jnp.swapaxes(w_qkv_temporal, 1, 2).reshape(3 * side, width)

    def rows_from(matrix, first_row):
        at = jnp.clip(start - first_row, 0, matrix.shape[0] - size)
        return lax.dynamic_slice(matrix, (at, 0), (size, width))

    chunk = jnp.where(
        start < 3 * side,
        rows_from(turned_qkv, 0),
        jnp.where(start < 4 * side, rows_from(w_out_temporal, 3 * side), rows_from(w_out_spatial, 4 * side)),
    )
    place = lax.axis_index("tok").astype(jnp.int32)[None]
    tail = (spot == line - 1).astype(jnp.int32)[None]
    chunk, place, tail = lax.optimization_barrier((chunk, place, tail))
    chunks = lax.all_to_all(
        jnp.broadcast_to(chunk[None], (ring, size, width)), "tok", 0, 0, tiled=True
    )

    *hidden, side_rows = first(line, levels, mod_table, queue_tokens)
    frames = [{0: h} for h in hidden]
    reach = ((4, 3), (3, 4))
    for step in range(1, 5):
        for j in range(2):
            if step <= reach[j][0]:
                frames[j][-step] = send_up(frames[j][1 - step])
            if step <= reach[j][1]:
                frames[j][step] = send_down(frames[j][step - 1])
    group = -(-(ring - 1) * size // 16) * 16
    weights = lax.all_gather(others(place, chunks, group), "queue", axis=0, tiled=False)

    offsets = [[0, 1, 2, 3, -4, -3, -2, -1], [0, 1, 2, 3, 4, -3, -2, -1]]
    own = (turned_qkv.reshape(3, side, width), w_out_temporal, w_out_spatial)
    mixed, *staged = spatial(
        offsets,
        place,
        jnp.swapaxes(w_qkv_spatial, 1, 2).reshape(3 * side, width),
        mod_table,
        [frames[j][o] for j in range(2) for o in offsets[j]],
    )
    mixed = lax.all_to_all(mixed, "tok", 0, 0, tiled=True)

    per = rows // line
    sent = bundle(line, size, group, place, mixed, side_rows)
    got = lax.all_to_all(sent.reshape(line, 2 * per, sent.shape[1]), "queue", 0, 0, tiled=True)
    moved = temporal(size, per, got.reshape(sent.shape), staged, own, weights)
    got = lax.all_to_all(moved.reshape(line, 2 * per, width), "queue", 0, 0, tiled=True)
    return last(tail, line, got.reshape(2 * rows, width), fresh_frame)


def solution(mesh):
    return jax.shard_map(
        per_device,
        mesh=mesh,
        in_specs=(
            P("queue", "tok", None),
            P("tok", None),
            P("queue"),
            P(),
            P(None, None, "tok"),
            P("tok", None),
            P(None, None, "tok"),
            P("tok", None),
        ),
        out_specs=P("queue", "tok", None),
        check_vma=False,
    )
```

```python
import jax
import jax.numpy as jnp
from jax import lax
from jax.experimental import pallas as pl
from jax.experimental.pallas import tpu as pltpu
from jax.sharding import PartitionSpec as P

HEADS = 16
HDIM = 72
EPS = 1e-06
FACTOR = HDIM ** (-0.5) * 1.4426950408889634
BF16 = jnp.bfloat16
F32 = jnp.float32
VMEM = pltpu.VMEM


def params(mib):
    return pltpu.CompilerParams(vmem_limit_bytes=mib * 1024 * 1024)


def vspec():
    return pl.BlockSpec(memory_space=VMEM)


def in_hbm(values):
    return pltpu.with_memory_space_constraint(values, pltpu.HBM)


def normalize(values):
    mean = jnp.mean(values, axis=-1, keepdims=True)
    centered = values - mean
    variance = jnp.mean(centered * centered, axis=-1, keepdims=True)
    return centered * lax.rsqrt(variance + EPS)


def turned(values, matrix):
    return lax.dot_general(values, matrix, (((1,), (1,)), ((), ())), preferred_element_type=F32)


def first_kernel(line, levels_hbm, table_hbm, tokens_hbm, h0_ref, h1_ref, side_ref, table_ref, held, levels_ref, sems):
    _, rows, width = held.shape
    copies = [
        pltpu.make_async_copy(levels_hbm, levels_ref, sems.at[0]),
        pltpu.make_async_copy(tokens_hbm, held, sems.at[1]),
        pltpu.make_async_copy(table_hbm.at[:, pl.ds(0, 2 * width)], table_ref, sems.at[2]),
    ]
    for copy in copies:
        copy.start()
    for copy in copies:
        copy.wait()
    for j, out in enumerate((h0_ref, h1_ref)):
        row = table_ref[pl.ds(levels_ref[j], 1), :]
        values = normalize(held[j].astype(F32))
        out[...] = (values * (1.0 + row[:, width:]) + row[:, :width]).astype(BF16)
    moved, frame = order_matrix(line, 2 * rows)
    tokens = held[...].reshape(2 * rows, width)
    side_ref[:, :width] = jnp.dot(moved, tokens, preferred_element_type=F32).astype(BF16)
    one, two = levels_ref[0].astype(F32), levels_ref[1].astype(F32)
    side_ref[:, width:] = jnp.where(frame == 0, one, two).astype(BF16)


def order_matrix(line, rows):
    per = rows // (2 * line)
    spot = lax.broadcasted_iota(jnp.int32, (rows, rows), 0)
    frame = spot // per % 2
    source = frame * (rows // 2) + spot // (2 * per) * per + spot % per
    moved = (lax.broadcasted_iota(jnp.int32, (rows, rows), 1) == source).astype(BF16)
    return moved, frame


def first(line, levels, table, tokens):
    _, rows, width = tokens.shape
    block = jax.ShapeDtypeStruct((rows, width), BF16)
    return pl.pallas_call(
        lambda *refs: first_kernel(line, *refs),
        out_shape=(block, block, jax.ShapeDtypeStruct((2 * rows, width + 2 * rows), BF16)),
        in_specs=[pl.BlockSpec(memory_space=pl.ANY)] * 3,
        out_specs=(vspec(), vspec(), vspec()),
        scratch_shapes=[
            VMEM((table.shape[0], 2 * width), F32),
            VMEM(tokens.shape, BF16),
            pltpu.SMEM(levels.shape, jnp.int32),
            pltpu.SemaphoreType.DMA((3,)),
        ],
        compiler_params=params(12),
        cost_estimate=pl.CostEstimate(flops=40000000, bytes_accessed=1500000, transcendentals=0),
        name="first",
    )(in_hbm(levels), in_hbm(table), in_hbm(tokens))


def others_kernel(place_ref, chunks_ref, out_ref):
    ring, size, width = chunks_ref.shape
    pieces = [chunks_ref[lax.rem(place_ref[0] + offset, ring)].astype(F32) for offset in range(1, ring)]
    spare = out_ref.shape[0] - (ring - 1) * size
    out_ref[...] = jnp.concatenate(pieces + [jnp.zeros((spare, width), F32)], axis=0).astype(BF16)


def others(place, chunks, rows):
    return pl.pallas_call(
        others_kernel,
        out_shape=jax.ShapeDtypeStruct((rows, chunks.shape[2]), BF16),
        in_specs=[pl.BlockSpec(memory_space=pltpu.SMEM), vspec()],
        out_specs=vspec(),
        compiler_params=params(8),
        cost_estimate=pl.CostEstimate(flops=0, bytes_accessed=900000, transcendentals=0),
        name="others",
    )(place, chunks)


def spatial_kernel(offsets, place_ref, w_hbm, table_hbm, *refs):
    *refs, out_ref, large_ref, small_ref, w_ref, table_ref, sems = refs
    copy = pltpu.make_async_copy(w_hbm, w_ref, sems.at[0])
    copy.start()
    count = table_ref.shape[1]
    table_copy = pltpu.make_async_copy(
        table_hbm.at[:, pl.ds(table_hbm.shape[1] - count, count)], table_ref, sems.at[1]
    )
    table_copy.start()
    rows = refs[0].shape[0]
    ring = len(offsets[0])
    for j in range(2):
        hidden = jnp.concatenate([ref[...] for ref in refs[j * ring : (j + 1) * ring]], axis=0)
        if j == 0:
            copy.wait()
        projected = turned(w_ref[...], hidden)
        side = projected.shape[0] // 3
        projected = jnp.concatenate([FACTOR * projected[:side], projected[side:]], axis=0).astype(BF16)
        heads = []
        for h in range(side // HDIM):
            query, keyed, valued = [
                projected[m * side + h * HDIM : m * side + (h + 1) * HDIM] for m in range(3)
            ]
            scores = lax.dot_general(
                keyed, query, (((0,), (0,)), ((), ())), preferred_element_type=F32
            )
            weights = jnp.exp2(scores - jnp.max(scores, axis=0, keepdims=True))
            total = jnp.sum(weights, axis=0, keepdims=True)
            mixed = jnp.dot(valued, weights.astype(BF16), preferred_element_type=F32)
            heads.append((mixed * (1.0 / total)).astype(BF16))
        attended = jnp.concatenate(heads, axis=0)
        for n, offset in enumerate(offsets[j]):
            owner = lax.rem(place_ref[0] + offset + ring, ring)
            out_ref[owner, :, j * rows : (j + 1) * rows] = attended[:, n * rows : (n + 1) * rows]
    table_copy.wait()
    values = table_ref[...]
    large = values.astype(BF16)
    large_ref[...] = large
    small_ref[...] = (values - large.astype(F32)).astype(BF16)


def spatial(offsets, place, w_qkv, table, blocks):
    rows, width = blocks[0].shape
    ring = len(offsets[0])
    whole = rows * ring
    return pl.pallas_call(
        lambda *refs: spatial_kernel(offsets, *refs),
        out_shape=(
            jax.ShapeDtypeStruct((ring, w_qkv.shape[0] // 3, 2 * rows), BF16),
            jax.ShapeDtypeStruct((table.shape[0], 4 * width), BF16),
            jax.ShapeDtypeStruct((table.shape[0], 4 * width), BF16),
        ),
        in_specs=[pl.BlockSpec(memory_space=pltpu.SMEM)]
        + [pl.BlockSpec(memory_space=pl.ANY)] * 2
        + [vspec()] * len(blocks),
        out_specs=(vspec(), vspec(), vspec()),
        scratch_shapes=[
            VMEM(w_qkv.shape, BF16),
            VMEM((table.shape[0], 4 * width), F32),
            pltpu.SemaphoreType.DMA((2,)),
        ],
        compiler_params=params(20),
        cost_estimate=pl.CostEstimate(
            flops=4 * whole * width * 144 * 3 + 8 * whole * whole * 256,
            bytes_accessed=8000000,
            transcendentals=4 * whole * whole,
        ),
        name="spatial",
    )(place, in_hbm(w_qkv), in_hbm(table), *blocks)


def bundle_kernel(line, size, group, place_ref, mixed_ref, side_ref, out_ref):
    ring, side, rows = mixed_ref.shape
    width = ring * side
    parts = [mixed_ref[lax.rem(place_ref[0] + offset, ring)].astype(F32) for offset in range(ring)]
    pieces = []
    for s in range(2):
        for k in range(3 * s, 3 * s + 3):
            pieces += [parts[offset][k * size : (k + 1) * size] for offset in range(1, ring)]
            pieces.append(jnp.zeros((group - (ring - 1) * size, rows), F32))
        if s == 0:
            pieces.append(parts[0])
    mixed = jnp.concatenate(pieces, axis=0).astype(BF16)
    moved, _ = order_matrix(line, rows)
    end = width + mixed.shape[0]
    out_ref[:, :width] = side_ref[:, :width]
    out_ref[:, width:end] = turned(moved, mixed).astype(BF16)
    out_ref[:, end:] = side_ref[:, width : width + out_ref.shape[1] - end]


def bundle(line, size, group, place, mixed, tokens):
    ring, side, rows = mixed.shape
    whole = ring * side + 6 * group + side
    lanes = -(-(whole + 64) // 128) * 128
    return pl.pallas_call(
        lambda *refs: bundle_kernel(line, size, group, *refs),
        out_shape=jax.ShapeDtypeStruct((rows, lanes), BF16),
        in_specs=[pl.BlockSpec(memory_space=pltpu.SMEM), vspec(), vspec()],
        out_specs=vspec(),
        compiler_params=params(12),
        cost_estimate=pl.CostEstimate(flops=40000000, bytes_accessed=1500000, transcendentals=0),
        name="bundle",
    )(place, mixed, tokens)


def temporal_kernel(
    size, per, got_ref, large_ref, small_ref, own_qkv, own_temporal, own_spatial, weights_hbm, out_ref, one_ref, two_ref, sems
):
    group, width = weights_hbm.shape[1:]
    side = own_temporal.shape[0]
    ring = width // side
    held = (one_ref, two_ref)
    gathered = 3 * group

    def start(m, s):
        for k in range(3):
            pltpu.make_async_copy(
                weights_hbm.at[6 * m + 3 * s + k], held[s].at[m, pl.ds(k * group, group)], sems.at[2 * m + s]
            ).start()
        if s == 0:
            own = own_qkv.at[m] if m < 3 else (own_temporal, own_spatial)[m - 3]
            pltpu.make_async_copy(own, one_ref.at[m, pl.ds(gathered, side)], sems.at[2 * m]).start()

    for m, s in ((4, 0), (4, 1), (0, 0), (1, 0), (2, 0), (3, 0), (0, 1), (1, 1), (2, 1), (3, 1)):
        start(m, s)
    rows = got_ref.shape[0]

    def matrix(m, s):
        pltpu.make_async_copy(held[s].at[m], held[s].at[m], sems.at[2 * m + s]).wait()
        return held[s][m]

    split = width + gathered + side
    end = split + gathered
    level = got_ref[:, end : end + large_ref.shape[0]].astype(F32)
    column = lax.broadcasted_iota(jnp.int32, level.shape, 1).astype(F32)
    onehot = (level == column).astype(BF16)

    def mods(n):
        part = slice(n * width, (n + 1) * width)
        return jnp.dot(onehot, large_ref[:, part], preferred_element_type=F32) + jnp.dot(
            onehot, small_ref[:, part], preferred_element_type=F32
        )

    gate1, shift2, scale2, gate2 = [mods(n) for n in range(4)]
    branch = jnp.dot(got_ref[:, width:split], matrix(4, 0), preferred_element_type=F32)
    branch += jnp.dot(got_ref[:, split:end], matrix(4, 1), preferred_element_type=F32)
    x1 = got_ref[:, :width].astype(F32) + gate1 * branch
    hidden = (normalize(x1) * (1.0 + scale2) + shift2).astype(BF16)

    branch = jnp.zeros((rows, width), F32)
    for s in range(2):
        heads = ring + 1 if s == 0 else ring - 1
        query = FACTOR * turned(matrix(0, s), hidden)
        keyed = turned(hidden, matrix(1, s)).astype(BF16)
        valued = turned(matrix(2, s), hidden).astype(BF16)
        row = lax.broadcasted_iota(jnp.int32, (query.shape[0], 1), 0)
        inside = row % group
        owner = jnp.where(inside < (ring - 1) * size, inside // size, -1)
        owner = jnp.where(row >= gathered, ring - 1 + (row - gathered) // HDIM, owner)
        along = lax.broadcasted_iota(jnp.int32, (rows, 1), 0) % per
        across = lax.broadcasted_iota(jnp.int32, (1, heads * rows), 1) % per
        spread = jnp.concatenate(
            [jnp.where(owner == h, query, 0.0).astype(BF16) for h in range(heads)], axis=1
        )
        scores = jnp.dot(keyed, spread, preferred_element_type=F32)
        scores = jnp.where(along == across, scores, -jnp.inf)
        weights = jnp.exp2(scores - jnp.max(scores, axis=0, keepdims=True))
        inverse = 1.0 / jnp.sum(weights, axis=0, keepdims=True)
        mixed = jnp.dot(valued, weights.astype(BF16), preferred_element_type=F32)

        def piece(first_row, count, h):
            columns = slice(h * rows, (h + 1) * rows)
            return mixed[first_row : first_row + count, columns] * inverse[:, columns]

        pieces = []
        for k in range(3):
            pieces += [piece(k * group + h * size, size, h) for h in range(ring - 1)]
            pieces.append(jnp.zeros((group - (ring - 1) * size, rows), F32))
        pieces += [piece(gathered + (h - ring + 1) * HDIM, HDIM, h) for h in range(ring - 1, heads)]
        attended = jnp.concatenate(pieces, axis=0).astype(BF16)
        branch += lax.dot_general(
            attended, matrix(3, s), (((0,), (0,)), ((), ())), preferred_element_type=F32
        )
    y = x1 + gate2 * branch
    y = jnp.concatenate([y[per:], y[:per]], axis=0)
    out_ref[...] = y.astype(BF16)


def temporal(size, per, got, staged, own, weights):
    group, width = weights.shape[1:]
    side = own[1].shape[0]
    rows = got.shape[0]
    return pl.pallas_call(
        lambda *refs: temporal_kernel(size, per, *refs),
        out_shape=jax.ShapeDtypeStruct((rows, width), BF16),
        in_specs=[vspec()] * 3 + [pl.BlockSpec(memory_space=pl.ANY)] * 4,
        out_specs=vspec(),
        scratch_shapes=[
            VMEM((5, 3 * group + side, width), BF16),
            VMEM((5, 3 * group, width), BF16),
            pltpu.SemaphoreType.DMA((10,)),
        ],
        compiler_params=params(40),
        cost_estimate=pl.CostEstimate(
            flops=2 * rows * width * width * 5, bytes_accessed=15000000, transcendentals=16 * rows * rows
        ),
        name="temporal",
    )(got, *staged, *[in_hbm(v) for v in own], in_hbm(weights))


def last_kernel(line, tail_ref, got_ref, fresh_ref, out_ref):
    rows = fresh_ref.shape[0]
    per = rows // line
    spot = lax.broadcasted_iota(jnp.int32, (2 * rows, 2 * rows), 1)
    source = spot // per % 2 * rows + spot // (2 * per) * per + spot % per
    back = (lax.broadcasted_iota(jnp.int32, (2 * rows, 2 * rows), 0) == source).astype(BF16)
    values = jnp.dot(back, got_ref[...], preferred_element_type=F32).astype(BF16)
    out_ref[0] = values[:rows]

    @pl.when(tail_ref[0] == 0)
    def _():
        out_ref[1] = values[rows:]

    @pl.when(tail_ref[0] != 0)
    def _():
        out_ref[1] = fresh_ref[...]


def last(tail, line, got, fresh):
    rows, width = fresh.shape
    return pl.pallas_call(
        lambda *refs: last_kernel(line, *refs),
        out_shape=jax.ShapeDtypeStruct((2, rows, width), BF16),
        in_specs=[pl.BlockSpec(memory_space=pltpu.SMEM), vspec(), vspec()],
        out_specs=vspec(),
        compiler_params=params(8),
        cost_estimate=pl.CostEstimate(flops=40000000, bytes_accessed=1000000, transcendentals=0),
        name="last",
    )(tail, got, fresh)


def per_device(
    queue_tokens,
    fresh_frame,
    levels,
    mod_table,
    w_qkv_spatial,
    w_out_spatial,
    w_qkv_temporal,
    w_out_temporal,
):
    _, rows, width = queue_tokens.shape
    ring = lax.axis_size("tok")
    line = lax.axis_size("queue")
    spot = lax.axis_index("queue")
    up = [(i, (i + 1) % ring) for i in range(ring)]
    down = [(i, (i - 1) % ring) for i in range(ring)]

    def send_up(v):
        return lax.ppermute(v, "tok", up)

    def send_down(v):
        return lax.ppermute(v, "tok", down)

    side = w_out_temporal.shape[0]
    size = side // 6
    start = spot * size
    turned_qkv = jnp.swapaxes(w_qkv_temporal, 1, 2).reshape(3 * side, width)

    def rows_from(matrix, first_row):
        at = jnp.clip(start - first_row, 0, matrix.shape[0] - size)
        return lax.dynamic_slice(matrix, (at, 0), (size, width))

    chunk = jnp.where(
        start < 3 * side,
        rows_from(turned_qkv, 0),
        jnp.where(start < 4 * side, rows_from(w_out_temporal, 3 * side), rows_from(w_out_spatial, 4 * side)),
    )
    place = lax.axis_index("tok").astype(jnp.int32)[None]
    tail = (spot == line - 1).astype(jnp.int32)[None]
    chunk, place, tail = lax.optimization_barrier((chunk, place, tail))
    chunks = lax.all_to_all(
        jnp.broadcast_to(chunk[None], (ring, size, width)), "tok", 0, 0, tiled=True
    )

    *hidden, side_rows = first(line, levels, mod_table, queue_tokens)
    frames = [{0: h} for h in hidden]
    reach = ((4, 3), (3, 4))
    for step in range(1, 5):
        for j in range(2):
            if step <= reach[j][0]:
                frames[j][-step] = send_up(frames[j][1 - step])
            if step <= reach[j][1]:
                frames[j][step] = send_down(frames[j][step - 1])
    group = -(-(ring - 1) * size // 16) * 16
    weights = lax.all_gather(others(place, chunks, group), "queue", axis=0, tiled=False)

    offsets = [[0, 1, 2, 3, -4, -3, -2, -1], [0, 1, 2, 3, 4, -3, -2, -1]]
    own = (turned_qkv.reshape(3, side, width), w_out_temporal, w_out_spatial)
    mixed, *staged = spatial(
        offsets,
        place,
        jnp.swapaxes(w_qkv_spatial, 1, 2).reshape(3 * side, width),
        mod_table,
        [frames[j][o] for j in range(2) for o in offsets[j]],
    )
    mixed = lax.all_to_all(mixed, "tok", 0, 0, tiled=True)

    per = rows // line
    sent = bundle(line, size, group, place, mixed, side_rows)
    got = lax.all_to_all(sent.reshape(line, 2 * per, sent.shape[1]), "queue", 0, 0, tiled=True)
    moved = temporal(size, per, got.reshape(sent.shape), staged, own, weights)
    got = lax.all_to_all(moved.reshape(line, 2 * per, width), "queue", 0, 0, tiled=True)
    return last(tail, line, got.reshape(2 * rows, width), fresh_frame)


def solution(mesh):
    return jax.shard_map(
        per_device,
        mesh=mesh,
        in_specs=(
            P("queue", "tok", None),
            P("tok", None),
            P("queue"),
            P(),
            P(None, None, "tok"),
            P("tok", None),
            P(None, None, "tok"),
            P("tok", None),
        ),
        out_specs=P("queue", "tok", None),
        check_vma=False,
    )
```
